32 devices in a mesh: rep: 2 (over y), pool: 8 (over z, x), tp: 2 (over core).
Axes of the slice: x: 2, y: 2, z: 4, core: 2. Of those that a mesh axis runs over, the one named last changes fastest.
Arguments:
- hidden: bfloat16 [2048, 8192], P(('rep', 'pool'), 'tp'), parts along dimension 0, may hold values from -6 to 6
- adapter_ids: int32 [2048, 1], P(('rep', 'pool')), parts along dimension 0, may hold values from 0 to 7, as said below
- owner_map: int32 [8], replicated, may hold values from 0 to 7, each once
- shrink_factors: bfloat16 [8, 8192, 64], P('pool', 'tp'), may hold values from -0.0625 to 0.0625
- expand_factors: bfloat16 [8, 64, 4096], P('pool', None, 'tp'), may hold values from -0.75 to 0.75
- query_base: bfloat16 [2048, 4096], P(('rep', 'pool'), 'tp'), parts along dimension 0, may hold values from -3 to 3
- new_key: bfloat16 [2048, 512], P(('rep', 'pool'), 'tp'), parts along dimension 0, may hold values from -6 to 6
- new_value: bfloat16 [2048, 512], P(('rep', 'pool'), 'tp'), parts along dimension 0, may hold values from -6 to 6
- cache_keys: bfloat16 [2048, 16, 512], P(('rep', 'pool'), None, 'tp'), parts along dimension 0, may hold values from -12 to 12
- cache_values: bfloat16 [2048, 16, 512], P(('rep', 'pool'), None, 'tp'), parts along dimension 0, may hold values from -6 to 6
- lengths: int32 [2048], P(('rep', 'pool')), parts along dimension 0, may hold values from 1 to 16, as said below
Outputs:
- attended: bfloat16 [2048, 4096], P(('rep', 'pool'), 'tp'), parts along dimension 0
The draws below stay inside these ranges and needn't reach their ends.
There are 2 independent parts, one for each index of `rep`. The reference program is written for one: setup_inputs(seed, part) draws one part's arguments, and reference() takes and returns one part's arrays. A program takes and returns all parts, laid end to end along the dimension named above; an argument that names none is the same for every part. Nothing has to cross between parts.
Inputs may be any that keep to these rules, and one draw needn't show every extreme that they name: `adapter_ids`: among the 128 requests of one pool index no adapter is named more than 32 times, and one adapter is named exactly 32 times by the requests of every pool index. `owner_map`: each storage index appears once. `lengths`: some request has all 16 slots live.
All inputs are finite; a program needn't handle non-finite values.
Results may differ from the reference program's by a relative error of at most 0.006.
Values may be sent and summed in bfloat16 or wider, within the bound.
No kernel may reach another device: no remote copies, remote signals or barrier semaphores. Data moves between devices by JAX's collectives and lax.ppermute only.
A program may use at most 64 MiB of HBM per device.

```python
import math
import jax
import jax.numpy as jnp
from jax import lax

D = 8192
HEAD = 128
QHEADS = 32
KVHEADS = 4
RANK = 64
REQ_DEV = 128
CACHE = 16
TOKENS = 1024
ADAPTERS = 8
CAP = 32


def draw_query_base(key, part):
    key = jax.random.fold_in(key, 11)
    drawn = jnp.clip(jax.random.normal(key, (TOKENS, QHEADS * HEAD)), -3.0, 3.0)
    return drawn.astype(jnp.bfloat16)


def draw_cache_keys(key, part):
    key = jax.random.fold_in(key, 12)
    drawn = jnp.clip(jax.random.normal(key, (TOKENS, CACHE, KVHEADS * HEAD)), -3.0, 3.0)
    return drawn.astype(jnp.bfloat16)


def draw_lengths(key, part):
    key = jax.random.fold_in(key, 13)
    count_key, row_key = jax.random.split(key)
    live_counts = jax.random.randint(count_key, (TOKENS,), 1, CACHE + 1)
    longest_row = jax.random.randint(row_key, (), 0, TOKENS)
    return jnp.where(jnp.arange(TOKENS) == longest_row, CACHE, live_counts).astype(jnp.int32)


def draw_adapter_ids(key, part):
    key = jax.random.fold_in(key, 14)
    hot_key, block_key = jax.random.split(key)
    hot_adapter = jax.random.randint(hot_key, (), 0, ADAPTERS)
    others = jnp.arange(ADAPTERS - 1, dtype=jnp.int32)
    others = others + (others >= hot_adapter).astype(jnp.int32)
    repeated = jnp.repeat(others, CAP)
    block_count = TOKENS // REQ_DEV

    def one_block(single_key):
        shuffle_key, order_key = jax.random.split(single_key)
        shuffled = jax.random.permutation(shuffle_key, repeated)
        picked = jnp.concatenate([jnp.full((CAP,), hot_adapter, dtype=jnp.int32), shuffled[:REQ_DEV - CAP]])
        return jax.random.permutation(order_key, picked)
    blocks = jax.vmap(one_block)(jax.random.split(block_key, block_count))
    return blocks.reshape(TOKENS, 1).astype(jnp.int32)


def block_scale(stream_key, shape, cuts, smallest, high):
    level = 1.0
    for axis_at, parts in cuts:
        draws = jax.random.uniform(jax.random.fold_in(jax.random.fold_in(stream_key, 6), axis_at), (parts,), jnp.float32, smallest / len(cuts), high / len(cuts))
        level = level * jnp.repeat(jnp.exp(draws), shape[axis_at] // parts).reshape((-1,) + (1,) * (len(shape) - 1 - axis_at))
    return level


def centred(own_key, dims, spread, reach, cuts=(), held_as=jnp.bfloat16):
    values = jax.random.normal(own_key, dims, jnp.float32) * spread
    if len(cuts) > 0:
        values = block_scale(own_key, dims, cuts, -0.22, 0.18) * values
    return jnp.clip(values, min=-reach, max=reach).astype(held_as)


def setup_inputs(seed: int = 0, part: int = 0) -> dict:
    arg_keys = jax.random.split(jax.random.key(seed), 12)
    own_keys = jax.random.split(jax.random.fold_in(arg_keys[11], part), 12)
    hidden = centred(own_keys[0], (TOKENS, D), 1.0, 6.0, ((0, 8), (1, 2)))
    adapter_ids = draw_adapter_ids(jax.random.fold_in(jax.random.fold_in(arg_keys[11], part), 71), part)
    owner_map = jax.random.permutation(arg_keys[2], ADAPTERS).astype(jnp.int32)
    shrink_factors = centred(arg_keys[3], (ADAPTERS, D, RANK), D ** -0.5, 0.0625, ((0, 8), (1, 2)))
    expand_factors = centred(arg_keys[4], (ADAPTERS, RANK, QHEADS * HEAD), RANK ** -0.5, 0.75, ((0, 8), (2, 2)))
    query_base = draw_query_base(jax.random.fold_in(jax.random.fold_in(arg_keys[11], part), 71), part)
    new_key = centred(own_keys[6], (TOKENS, KVHEADS * HEAD), 1.0, 6.0, ((0, 8), (1, 2)))
    new_value = centred(own_keys[7], (TOKENS, KVHEADS * HEAD), 1.0, 6.0, ((0, 8), (1, 2)))
    cache_keys = draw_cache_keys(jax.random.fold_in(jax.random.fold_in(arg_keys[11], part), 71), part)
    cache_values = centred(own_keys[9], (TOKENS, CACHE, KVHEADS * HEAD), 1.0, 6.0, ((0, 8), (2, 2)))
    lengths = draw_lengths(jax.random.fold_in(jax.random.fold_in(arg_keys[11], part), 71), part)
    return dict(hidden=hidden, adapter_ids=adapter_ids, owner_map=owner_map, shrink_factors=shrink_factors, expand_factors=expand_factors, query_base=query_base, new_key=new_key, new_value=new_value, cache_keys=cache_keys, cache_values=cache_values, lengths=lengths)


def reference(hidden, adapter_ids, owner_map, shrink_factors, expand_factors, query_base, new_key, new_value, cache_keys, cache_values, lengths):
    block_count = TOKENS // REQ_DEV
    group_size = QHEADS // KVHEADS
    owner = owner_map[adapter_ids[:, 0]]

    def one_block(block_index):
        row_start = block_index * REQ_DEV

        def rows_of(array):
            return lax.dynamic_slice_in_dim(array, row_start, REQ_DEV, 0)
        owners = rows_of(owner)
        hidden_rows = rows_of(hidden).astype(jnp.float32)
        shrink_rows = jnp.take(shrink_factors, owners, axis=0).astype(jnp.float32)
        shrunk = jnp.einsum('rd,rdk->rk', hidden_rows, shrink_rows)
        low_rank = shrunk.astype(jnp.bfloat16)
        expand_rows = jnp.take(expand_factors, owners, axis=0).astype(jnp.float32)
        query_delta = jnp.einsum('rk,rkc->rc', low_rank.astype(jnp.float32), expand_rows).astype(jnp.bfloat16)
        queries = (rows_of(query_base).astype(jnp.float32) + query_delta.astype(jnp.float32)).astype(jnp.bfloat16)
        all_keys = jnp.concatenate([rows_of(cache_keys), rows_of(new_key)[:, None, :]], axis=1)
        all_values = jnp.concatenate([rows_of(cache_values), rows_of(new_value)[:, None, :]], axis=1)
        grouped = queries.reshape(REQ_DEV, KVHEADS, group_size, HEAD).astype(jnp.float32)
        key_blocks = all_keys.reshape(REQ_DEV, CACHE + 1, KVHEADS, HEAD).astype(jnp.float32)
        value_blocks = all_values.reshape(REQ_DEV, CACHE + 1, KVHEADS, HEAD).astype(jnp.float32)
        scores = jnp.einsum('rgqd,rjgd->rgqj', grouped, key_blocks) / math.sqrt(HEAD)
        slot_index = jnp.arange(CACHE + 1, dtype=jnp.int32)
        live_mask = (slot_index[None, :] < rows_of(lengths)[:, None]) | (slot_index[None, :] == CACHE)
        scores = jnp.where(live_mask[:, None, None, :], scores, -jnp.inf)
        row_top = lax.optimization_barrier(jnp.max(scores, axis=-1, keepdims=True))
        exps = jnp.exp(scores - row_top)
        probs = (exps / lax.optimization_barrier(jnp.sum(exps, axis=-1, keepdims=True))).astype(jnp.bfloat16)
        mixed_values = jnp.einsum('rgqj,rjgd->rgqd', probs.astype(jnp.float32), value_blocks)
        return mixed_values.reshape(REQ_DEV, QHEADS * HEAD).astype(jnp.bfloat16)
    stacked = lax.map(one_block, jnp.arange(block_count, dtype=jnp.int32))
    return stacked.reshape(TOKENS, QHEADS * HEAD)
```

```python
import functools
import math

import jax
import jax.numpy as jnp
from jax import lax
from jax.experimental import pallas as pl
from jax.experimental.pallas import tpu as pltpu
from jax.sharding import PartitionSpec as P

HEAD = 128
ROWS = 16
DEAD = -1e30


def attend_kernel(parts, me_ref, base_ref, nk_ref, nv_ref, ck_ref, cv_ref, len_ref, *rest):
    delta_refs, out_ref = rest[:parts], rest[parts]
    me = me_ref[0]
    width = delta_refs[0].shape[1]
    groups = nk_ref.shape[1] // HEAD
    slots = ck_ref.shape[1]
    heads = width // HEAD
    span = parts // groups
    rows = span * heads * ROWS
    row_req = lax.broadcasted_iota(jnp.int32, (rows, ROWS * slots), 0) % ROWS
    col = lax.broadcasted_iota(jnp.int32, (rows, ROWS * slots), 1)
    lens = jnp.concatenate([len_ref[...]] * (span * heads), axis=0)
    live = (row_req == col // slots) & (col % slots < lens)
    own_live = lax.broadcasted_iota(jnp.int32, (rows, ROWS), 0) % ROWS == lax.broadcasted_iota(
        jnp.int32, (rows, ROWS), 1
    )
    scale = 1.0 / math.sqrt(HEAD)
    for first in range(0, parts, span):
        group = (me ^ first) // span
        lanes = pl.ds(pl.multiple_of(group * HEAD, HEAD), HEAD)
        pieces = []
        for s in range(first, first + span):
            at = pl.ds(pl.multiple_of((me ^ s) * width, width), width)
            q = base_ref[:, at].astype(jnp.float32) + delta_refs[s][...].astype(jnp.float32)
            q = q.astype(jnp.bfloat16)
            pieces += [q[:, h * HEAD : (h + 1) * HEAD] for h in range(heads)]
        q = jnp.concatenate(pieces, axis=0)
        keys = ck_ref[:, :, lanes].reshape(ROWS * slots, HEAD)
        values = cv_ref[:, :, lanes].reshape(ROWS * slots, HEAD)
        dims = (((1,), (1,)), ((), ()))
        scores = lax.dot_general(q, keys, dims, preferred_element_type=jnp.float32) * scale
        own = lax.dot_general(q, nk_ref[:, lanes], dims, preferred_element_type=jnp.float32) * scale
        own = jnp.sum(jnp.where(own_live, own, 0.0), axis=1, keepdims=True)
        scores = jnp.where(live, scores, DEAD)
        top = jnp.maximum(jnp.max(scores, axis=1, keepdims=True), own)
        exps = jnp.exp(scores - top)
        own_exp = jnp.exp(own - top)
        total = jnp.sum(exps, axis=1, keepdims=True) + own_exp
        probs = (exps / total).astype(jnp.bfloat16)
        own_prob = (own_exp / total).astype(jnp.bfloat16).astype(jnp.float32)
        mixed = jnp.dot(probs, values, preferred_element_type=jnp.float32)
        own_value = jnp.concatenate([nv_ref[:, lanes].astype(jnp.float32)] * (span * heads), axis=0)
        mixed = (mixed + own_prob * own_value).astype(jnp.bfloat16)
        for i, s in enumerate(range(first, first + span)):
            at = pl.ds(pl.multiple_of((me ^ s) * width, width), width)
            out_ref[:, at] = jnp.concatenate(
                [mixed[(i * heads + h) * ROWS : (i * heads + h + 1) * ROWS] for h in range(heads)],
                axis=1,
            )


def attend(me, base, new_key, new_value, cache_keys, cache_values, lengths, deltas):
    requests, columns = base.shape
    kv = new_key.shape[1]
    slots = cache_keys.shape[1]
    row2 = lambda w: pl.BlockSpec((ROWS, w), lambda i, me: (i, 0))
    row3 = pl.BlockSpec((ROWS, slots, kv), lambda i, me: (i, 0, 0))
    parts = len(deltas)
    return pl.pallas_call(
        functools.partial(attend_kernel, parts),
        out_shape=jax.ShapeDtypeStruct((requests, columns), jnp.bfloat16),
        grid_spec=pltpu.PrefetchScalarGridSpec(
            num_scalar_prefetch=1,
            grid=(requests // ROWS,),
            in_specs=[row2(columns), row2(kv), row2(kv), row3, row3, row2(1)]
            + [row2(columns // parts)] * parts,
            out_specs=row2(columns),
        ),
        compiler_params=pltpu.CompilerParams(vmem_limit_bytes=24 * 1024 * 1024),
        cost_estimate=pl.CostEstimate(
            flops=4 * requests * ROWS * slots * columns,
            bytes_accessed=4 * requests * (columns + slots * kv),
            transcendentals=requests * slots * columns // 8,
        ),
    )(me, base, new_key, new_value, cache_keys, cache_values, lengths, *deltas)


def per_device(
    hidden,
    adapter_ids,
    owner_map,
    shrink_factors,
    expand_factors,
    query_base,
    new_key,
    new_value,
    cache_keys,
    cache_values,
    lengths,
):
    reps, pool, tp = (lax.axis_size(a) for a in ("rep", "pool", "tp"))
    requests = hidden.shape[0]
    rank = shrink_factors.shape[2]
    square = 2 * reps
    column = pool // 2
    features = hidden.shape[1] // square
    outputs = query_base.shape[1] // square
    place = lax.axis_index("pool")
    side, level = place % 2, place // 2
    me = lax.axis_index("rep") * 2 + side
    core = me * tp + lax.axis_index("tp")

    def swap(a, s):
        pairs = [
            (r * pool + p, (r ^ (s // 2)) * pool + (p ^ (s % 2)))
            for r in range(reps)
            for p in range(pool)
        ]
        return lax.ppermute(a, ("rep", "pool"), pairs)

    def swap_core(a, s):
        chip, c = s // tp, s % tp
        pairs = [
            (
                (r * pool + p) * tp + t,
                ((r ^ (chip // 2)) * pool + (p ^ (chip % 2))) * tp + (t ^ c),
            )
            for r in range(reps)
            for p in range(pool)
            for t in range(tp)
        ]
        return lax.ppermute(a, ("rep", "pool", "tp"), pairs)

    def along(a, moves):
        return lax.ppermute(a, "pool", [(i * 2 + s, j * 2 + s) for i, j in moves for s in range(2)])

    def gather_column(a):
        if column == 1:
            return [a]
        near = along(a, [(i, i ^ 1) for i in range(column)])
        if column == 2:
            return [a, near]
        far = along(a, [(i, i ^ 2) for i in range(4)])
        inner = along(a, [(1, 2), (2, 1)])
        outer = along(far, [(2, 3), (1, 0)])
        last = jnp.where((level == 1) | (level == 2), inner, outer)
        return [a, near, far, last]

    ids = adapter_ids[:, 0]
    adapters = jnp.arange(owner_map.shape[0], dtype=jnp.int32)
    owners = jnp.sum(jnp.where(ids[None, :] == adapters[:, None], owner_map[:, None], 0), axis=0)
    owners = owners[None, :]
    all_owners = jnp.concatenate([owners] + [swap(owners, s) for s in range(1, square)], axis=1)

    shrink = shrink_factors[0].T
    expand = expand_factors[0]

    def cut(a, width, at):
        return lax.dynamic_slice_in_dim(a, at * width, width, 1)

    rows = [cut(hidden, features, me)]
    shrink_next = swap(cut(shrink, features, me ^ 1), 1)
    expand_next = swap(cut(expand, outputs, me ^ 1), 1)
    rows += [swap(cut(hidden, features, me ^ s), s) for s in range(1, square)]
    shrink_own = cut(shrink, features, me)
    expand_own = cut(expand, outputs, me)
    all_rows = jnp.concatenate(rows, axis=0)

    def shrink_by(weight, owner):
        sums = lax.dot_general(
            weight, all_rows, (((1,), (1,)), ((), ())), preferred_element_type=jnp.float32
        )
        return jnp.where(all_owners == owner, sums, 0.0)

    small = column in (1, 2, 4)
    if small:
        own_blocks = gather_column(shrink_own)
        next_blocks = gather_column(shrink_next)
        expand_blocks = gather_column(jnp.concatenate([expand_own, expand_next], axis=0))
        partial = 0.0
        for k in range(column):
            partial = partial + shrink_by(own_blocks[k], (level ^ k) * 2 + side)
            partial = partial + shrink_by(next_blocks[k], (level ^ k) * 2 + 1 - side)
    else:
        ring = [(i, (i + 1) % column) for i in range(column)]

        def shrink_step(k, carry):
            total, own, other = carry
            at = (level - k) % column
            total = total + shrink_by(own, at * 2 + side) + shrink_by(other, at * 2 + 1 - side)
            return total, along(own, ring), along(other, ring)

        start = jnp.zeros((rank, square * requests), jnp.float32)
        partial = lax.fori_loop(0, column, shrink_step, (start, shrink_own, shrink_next))[0]

    devices = square * tp
    share = rank // devices
    pieces = partial.reshape(devices, share, square * requests)

    def reorder(a, chip):
        blocks = [a[:, (s ^ chip) * requests : ((s ^ chip) + 1) * requests] for s in range(square)]
        return jnp.concatenate(blocks, axis=1)

    def piece(at):
        return lax.dynamic_index_in_dim(pieces, at, 0, keepdims=False)

    total = piece(core)
    for s in range(1, devices):
        total = total + reorder(swap_core(piece(core ^ s), s), s // tp)
    low = total.astype(jnp.bfloat16)
    lows = [low] + [reorder(swap_core(low, s), s // tp) for s in range(1, devices)]
    low_rank = jnp.stack(lows)[core ^ jnp.arange(devices)]
    low_rank = low_rank.reshape(rank, square * requests)

    def masked(owner):
        return jnp.where(all_owners == owner, low_rank, jnp.zeros_like(low_rank))

    dims = (((0,), (0,)), ((), ()))
    if small:
        picked = []
        for k in range(column):
            picked += [masked((level ^ k) * 2 + side), masked((level ^ k) * 2 + 1 - side)]
        delta = lax.dot_general(
            jnp.concatenate(picked, axis=0),
            jnp.concatenate(expand_blocks, axis=0),
            dims,
            preferred_element_type=jnp.float32,
        ).astype(jnp.bfloat16)
    else:

        def expand_step(k, carry):
            total, block = carry
            at = (level - k) % column
            picked = jnp.concatenate([masked(at * 2 + side), masked(at * 2 + 1 - side)], axis=0)
            total = total + lax.dot_general(
                picked, block, dims, preferred_element_type=jnp.float32
            )
            return total, along(block, ring)

        start = jnp.zeros((square * requests, outputs), jnp.float32)
        block = jnp.concatenate([expand_own, expand_next], axis=0)
        delta = lax.fori_loop(0, column, expand_step, (start, block))[0].astype(jnp.bfloat16)

    deltas = [delta[:requests]]
    deltas += [swap(delta[s * requests : (s + 1) * requests], s) for s in range(1, square)]
    return attend(
        me[None],
        query_base,
        new_key,
        new_value,
        cache_keys,
        cache_values,
        lengths[:, None],
        deltas,
    )


def solution(mesh):
    in_specs = (
        P(("rep", "pool"), "tp"),
        P(("rep", "pool"), None),
        P(),
        P("pool", "tp", None),
        P("pool", None, "tp"),
        P(("rep", "pool"), "tp"),
        P(("rep", "pool"), "tp"),
        P(("rep", "pool"), "tp"),
        P(("rep", "pool"), None, "tp"),
        P(("rep", "pool"), None, "tp"),
        P(("rep", "pool")),
    )
    out_specs = P(("rep", "pool"), "tp")
    return jax.shard_map(
        per_device, mesh=mesh, in_specs=in_specs, out_specs=out_specs, check_vma=False
    )
```

```python
import functools
import math

import jax
import jax.numpy as jnp
from jax import lax
from jax.experimental import pallas as pl
from jax.experimental.pallas import tpu as pltpu
from jax.sharding import Mesh
from jax.sharding import PartitionSpec as P

HEAD = 128
LANES = 128
STEP = 16
HALF = 8
DEAD = -1e30
VMEM = pl.BlockSpec(memory_space=pltpu.VMEM)
PARAMS = pltpu.CompilerParams(vmem_limit_bytes=32 * 1024 * 1024)


def chunk_of(pool):
    return math.gcd(pool, 8)


def owner_mask(owners, start, count, rank):
    lane = lax.broadcasted_iota(jnp.int32, (owners.shape[0], count * rank), 1) // rank + start
    wide = jnp.concatenate([owners] * (count * rank // LANES), axis=1)
    return wide == lane


def shrink_kernel(features, rows_ref, weight_ref, out_ref):
    squares, requests, _ = rows_ref.shape
    count, rank, _ = weight_ref.shape
    step = pl.program_id(0)

    @pl.when(step == 0)
    def _():
        out_ref[...] = jnp.zeros_like(out_ref)

    weight = weight_ref[...].reshape(count * rank, features)
    low = lax.broadcasted_iota(jnp.int32, (requests, LANES), 1) < rank
    folded = []
    for s in range(squares):
        owners = rows_ref[s, :, features:].astype(jnp.float32).astype(jnp.int32)
        sums = lax.dot_general(
            rows_ref[s, :, :features],
            weight,
            (((1,), (1,)), ((), ())),
            preferred_element_type=jnp.float32,
        )
        sums = jnp.where(owner_mask(owners, step * count, count, rank), sums, 0.0)
        total = sums[:, :LANES]
        for k in range(1, count * rank // LANES):
            total = total + sums[:, k * LANES : (k + 1) * LANES]
        folded.append(total + pltpu.roll(total, rank, 1))
    half = squares // 2
    for s in range(half):
        rows = pl.ds(s * requests, requests)
        out_ref[rows, :] += jnp.where(low, folded[s], folded[s + half])


def expand_kernel(features, rows_ref, low_ref, weight_ref, out_ref, total_ref):
    squares, requests, _ = rows_ref.shape
    count, rank, outputs = weight_ref.shape
    step = pl.program_id(0)
    half = squares // 2
    weight = weight_ref[...].reshape(count * rank, outputs)
    low = lax.broadcasted_iota(jnp.int32, (requests, LANES), 1) < rank
    for s in range(squares):
        owners = rows_ref[s, :, features:].astype(jnp.float32).astype(jnp.int32)
        held = low_ref[pl.ds((s % half) * requests, requests), :]
        turned = pltpu.roll(held, rank, 1)
        both = jnp.where(low, held, turned) if s < half else jnp.where(low, turned, held)
        wide = jnp.concatenate([both] * (count * rank // LANES), axis=1)
        wide = jnp.where(owner_mask(owners, step * count, count, rank), wide, 0.0)
        part = jnp.dot(wide.astype(jnp.bfloat16), weight, preferred_element_type=jnp.float32)

        @pl.when(step == 0)
        def _():
            total_ref[s] = part

        @pl.when(step > 0)
        def _():
            total_ref[s] += part

    @pl.when(step == pl.num_programs(0) - 1)
    def _():
        out_ref[...] = total_ref[...].astype(jnp.bfloat16)


def attend_kernel(len_ref, base_ref, nk_ref, nv_ref, ck_ref, cv_ref, delta_ref, out_ref):
    requests, columns = base_ref.shape
    groups = nk_ref.shape[1] // HEAD
    slots = ck_ref.shape[1]
    parts, _, width = delta_ref.shape
    heads = columns // groups // HEAD
    scale = 1.0 / math.sqrt(HEAD)
    keys_in = HALF * slots
    rows = heads * HALF
    col = lax.broadcasted_iota(jnp.int32, (HALF, keys_in), 1)
    row = lax.broadcasted_iota(jnp.int32, (HALF, keys_in), 0)
    same = row == col // slots
    slot = col % slots
    own_col = lax.broadcasted_iota(jnp.int32, (HALF, LANES), 1)
    own_row = lax.broadcasted_iota(jnp.int32, (HALF, LANES), 0)
    own_bias = jnp.where(own_col == own_row, 0.0, DEAD)
    ones = jnp.ones((keys_in + LANES, HEAD), jnp.bfloat16)
    empty = jnp.zeros((LANES - HALF, HEAD), jnp.float32)
    contract = (((1,), (1,)), ((), ()))

    def body(i, _):
        at = pl.ds(pl.multiple_of(i * STEP, STEP), STEP)
        delta = jnp.concatenate([delta_ref[s, at, :] for s in range(parts)], axis=1)
        query = base_ref[at, :].astype(jnp.float32) + delta.astype(jnp.float32)
        fresh_key = nk_ref[at, :].astype(jnp.float32)
        fresh_value = nv_ref[at, :].astype(jnp.float32)
        outs = []
        for h in range(STEP // HALF):
            mine = slice(h * HALF, (h + 1) * HALF)
            lens = len_ref[pl.ds(pl.multiple_of(i * STEP + h * HALF, HALF), HALF), :]
            bias = jnp.where(same & (slot < lens), 0.0, DEAD)
            bias = jnp.concatenate([bias, own_bias], axis=1)
            bias = jnp.concatenate([bias] * heads, axis=0)
            slab = pl.ds(pl.multiple_of(i * STEP + h * HALF, HALF), HALF)
            for g in range(groups):
                lanes = slice(g * HEAD, (g + 1) * HEAD)
                q = jnp.concatenate(
                    [
                        query[mine, (g * heads + k) * HEAD : (g * heads + k + 1) * HEAD]
                        for k in range(heads)
                    ],
                    axis=0,
                ).astype(jnp.bfloat16)
                own_key = jnp.concatenate([fresh_key[mine, lanes], empty], axis=0)
                own_value = jnp.concatenate([fresh_value[mine, lanes], empty], axis=0)
                keys = jnp.concatenate(
                    [ck_ref[slab, :, lanes].reshape(keys_in, HEAD), own_key.astype(jnp.bfloat16)],
                    axis=0,
                )
                values = jnp.concatenate(
                    [cv_ref[slab, :, lanes].reshape(keys_in, HEAD), own_value.astype(jnp.bfloat16)],
                    axis=0,
                )
                scores = lax.dot_general(q, keys, contract, preferred_element_type=jnp.float32)
                scores = scores + bias
                top = jnp.max(scores, axis=1, keepdims=True)
                exps = jnp.exp((scores - top) * scale).astype(jnp.bfloat16)
                mixed = jnp.dot(
                    exps,
                    jnp.concatenate([values, ones], axis=1),
                    preferred_element_type=jnp.float32,
                )
                mixed = mixed[:, :HEAD] / mixed[:, HEAD:]
                outs.append([mixed[k * HALF : (k + 1) * HALF] for k in range(heads)])
        for g in range(groups):
            for k in range(heads):
                both = [outs[h * groups + g][k] for h in range(STEP // HALF)]
                c = (g * heads + k) * HEAD
                out_ref[at, c : c + HEAD] = jnp.concatenate(both, axis=0).astype(jnp.bfloat16)
        return 0

    lax.fori_loop(0, requests // STEP, body, 0)


def attend(base, new_key, new_value, cache_keys, cache_values, lengths, delta):
    requests, columns = base.shape
    kv = new_key.shape[1]
    slots = cache_keys.shape[1]
    return pl.pallas_call(
        attend_kernel,
        out_shape=jax.ShapeDtypeStruct((requests, columns), jnp.bfloat16),
        in_specs=[VMEM] * 7,
        out_specs=VMEM,
        compiler_params=PARAMS,
        cost_estimate=pl.CostEstimate(
            flops=4 * requests * HALF * slots * columns,
            bytes_accessed=4 * requests * (columns + slots * kv),
            transcendentals=requests * slots * columns // 8,
        ),
    )(lengths, base, new_key, new_value, cache_keys, cache_values, delta)


def per_device(
    hidden,
    adapter_ids,
    owner_map,
    shrink_factors,
    expand_factors,
    query_base,
    new_key,
    new_value,
    cache_keys,
    cache_values,
    lengths,
):
    reps, levels, sides, tp = (lax.axis_size(a) for a in ("rep", "level", "side", "tp"))
    pool = levels * sides
    requests, wide = hidden.shape
    rank = shrink_factors.shape[2]
    square = reps * sides
    features = wide // square
    outputs = query_base.shape[1] // square
    chips = ("rep", "side")
    me = lax.axis_index("rep") * sides + lax.axis_index("side")

    shrink = shrink_factors[0].T
    expand = expand_factors[0]
    row_of = lax.axis_index("rep") * sides

    def quarters(a, width):
        mine = lax.dynamic_slice_in_dim(a, row_of * width, sides * width, 1)
        mine = mine.reshape(rank, sides, width).transpose(1, 0, 2)
        return lax.all_to_all(mine, "side", split_axis=0, concat_axis=0, tiled=True)

    shrink = quarters(shrink, features)
    expand = quarters(expand, outputs)
    shrink = lax.all_gather(shrink, "level", axis=0, tiled=True)
    expand = lax.all_gather(expand, "level", axis=0, tiled=True)

    ids = adapter_ids[:, 0]
    adapters = jnp.arange(owner_map.shape[0], dtype=jnp.int32)
    owners = jnp.sum(jnp.where(ids[:, None] == adapters[None, :], owner_map[None, :], 0), axis=1)
    owners = jnp.broadcast_to(owners.astype(jnp.bfloat16)[None, :, None], (square, requests, LANES))
    rows = hidden.reshape(requests, square, features).transpose(1, 0, 2)
    rows = jnp.concatenate([rows, owners], axis=2)
    rows = lax.all_to_all(rows, chips, split_axis=0, concat_axis=0, tiled=True)

    chunk = chunk_of(pool)
    partial = pl.pallas_call(
        functools.partial(shrink_kernel, features),
        out_shape=jax.ShapeDtypeStruct((square // 2 * requests, LANES), jnp.float32),
        grid=(pool // chunk,),
        in_specs=[
            pl.BlockSpec(rows.shape, lambda i: (0, 0, 0)),
            pl.BlockSpec((chunk, rank, features), lambda i: (i, 0, 0)),
        ],
        out_specs=pl.BlockSpec((square // 2 * requests, LANES), lambda i: (0, 0)),
        compiler_params=PARAMS,
    )(rows, shrink)
    low_rank = lax.psum(partial, ("rep", "side", "tp"))
    delta = pl.pallas_call(
        functools.partial(expand_kernel, features),
        out_shape=jax.ShapeDtypeStruct((square, requests, outputs), jnp.bfloat16),
        grid=(pool // chunk,),
        in_specs=[
            pl.BlockSpec(rows.shape, lambda i: (0, 0, 0)),
            pl.BlockSpec(partial.shape, lambda i: (0, 0)),
            pl.BlockSpec((chunk, rank, outputs), lambda i: (i, 0, 0)),
        ],
        out_specs=pl.BlockSpec((square, requests, outputs), lambda i: (0, 0, 0)),
        scratch_shapes=[pltpu.VMEM((square, requests, outputs), jnp.float32)],
        compiler_params=PARAMS,
    )(rows, low_rank, expand)
    delta = lax.all_to_all(delta, chips, split_axis=0, concat_axis=0, tiled=True)
    return attend(
        query_base, new_key, new_value, cache_keys, cache_values, lengths[:, None], delta
    )


def solution(mesh):
    reps, pool, tp = (mesh.shape[a] for a in ("rep", "pool", "tp"))
    finer = Mesh(mesh.devices.reshape(reps, pool // 2, 2, tp), ("rep", "level", "side", "tp"))
    pooled = ("level", "side")
    requests = ("rep", "level", "side")
    in_specs = (
        P(requests, "tp"),
        P(requests, None),
        P(),
        P(pooled, "tp", None),
        P(pooled, None, "tp"),
        P(requests, "tp"),
        P(requests, "tp"),
        P(requests, "tp"),
        P(requests, None, "tp"),
        P(requests, None, "tp"),
        P(requests),
    )
    return jax.shard_map(
        per_device, mesh=finer, in_specs=in_specs, out_specs=P(requests, "tp"), check_vma=False
    )
```

```python
import functools
import math

import jax
import jax.numpy as jnp
from jax import lax
from jax.experimental import pallas as pl
from jax.experimental.pallas import tpu as pltpu
from jax.sharding import Mesh
from jax.sharding import PartitionSpec as P

HEAD = 128
LANES = 128
STEP = 16
HALF = 8
BATCH = 4
DEAD = -1e30
VMEM = pl.BlockSpec(memory_space=pltpu.VMEM)
SMEM = pl.BlockSpec(memory_space=pltpu.SMEM)
PARAMS = pltpu.CompilerParams(vmem_limit_bytes=32 * 1024 * 1024)
NT = (((1,), (1,)), ((), ()))
TN = (((0,), (0,)), ((), ()))


def pack_kernel(parts, me_ref, map_ref, ids_ref, hidden_ref, *out_refs):
    requests, wide = hidden_ref.shape
    features = wide // parts
    me = me_ref[0]
    ids = ids_ref[...]

    def look(k, found):
        return jnp.where(ids == k, map_ref[k], found)

    owners = lax.fori_loop(0, map_ref.shape[0], look, jnp.zeros_like(ids))
    owners = jnp.broadcast_to(owners.astype(jnp.float32), (requests, LANES)).astype(jnp.bfloat16)
    for s in range(parts):
        at = pl.ds(pl.multiple_of((me ^ s) * features, features), features)
        out_refs[s][:, :features] = hidden_ref[:, at]
        out_refs[s][:, features:] = owners


def owner_mask(owners, ids, rank):
    lane = lax.broadcasted_iota(jnp.int32, (1, len(ids) * rank), 1) // rank
    named = jnp.full_like(lane, -1)
    for k, owner in enumerate(ids):
        named = jnp.where(lane == k, owner, named)
    wide = jnp.concatenate([owners] * (len(ids) * rank // LANES), axis=1)
    return wide == named


def row_owners(ref, features):
    return ref[:, features:].astype(jnp.float32).astype(jnp.int32)


def stacked(refs):
    blocks = [r[k] for r in refs for k in range(r.shape[0])]
    return jnp.concatenate(blocks, axis=0)


def shrink_kernel(parts, blocks, gridded, ids_ref, *refs):
    row_refs, weight_refs, base_ref, out_ref = (
        refs[:parts],
        refs[parts : parts + blocks],
        refs[parts + blocks],
        refs[-1],
    )
    rank, features = weight_refs[0].shape[1:]
    requests = row_refs[0].shape[0]
    count = sum(r.shape[0] for r in weight_refs)
    step = pl.program_id(0) if gridded else 0
    ids = [ids_ref[step * count + k] for k in range(count)]
    weight = stacked(weight_refs)
    low = lax.broadcasted_iota(jnp.int32, (requests, LANES), 1) < rank
    folded = []
    for ref in row_refs:
        sums = lax.dot_general(
            ref[:, :features], weight, NT, preferred_element_type=jnp.float32
        )
        sums = jnp.where(owner_mask(row_owners(ref, features), ids, rank), sums, 0.0)
        total = sums[:, :LANES]
        for k in range(1, count * rank // LANES):
            total = total + sums[:, k * LANES : (k + 1) * LANES]
        folded.append(total + pltpu.roll(total, rank, 1))
    if gridded:

        @pl.when(step == 0)
        def _():
            out_ref[...] = base_ref[...]

    else:
        out_ref[...] = base_ref[...]
    half = parts // 2
    for s in range(half):
        rows = pl.ds(s * requests, requests)
        out_ref[rows, :] += jnp.where(low, folded[s], folded[s + half])


def expand_kernel(parts, blocks, cores, gridded, ids_ref, me_ref, *refs):
    row_refs, low_ref, weight_refs, out_refs, total_ref = (
        refs[:parts],
        refs[parts],
        refs[parts + 1 : parts + 1 + blocks],
        refs[-parts - 1 : -1],
        refs[-1],
    )
    rank, outputs = weight_refs[0].shape[1:]
    features = row_refs[0].shape[1] - LANES
    requests = row_refs[0].shape[0]
    count = sum(r.shape[0] for r in weight_refs)
    step = pl.program_id(0) if gridded else 0
    last = pl.num_programs(0) - 1 if gridded else 0
    ids = [ids_ref[step * count + k] for k in range(count)]
    weight = stacked(weight_refs)
    half = parts // 2
    low = lax.broadcasted_iota(jnp.int32, (requests, LANES), 1) < rank
    me = me_ref[0]
    held = [[0.0] * half for _ in range(2)]
    for t in range(parts):
        for core in range(cores):
            sums = low_ref[(me ^ t) * cores + core].astype(jnp.float32)
            for s in range(half):
                at = (s ^ t) % half
                piece = sums[at * requests : (at + 1) * requests]
                held[t // half][s] = held[t // half][s] + piece
    for s in range(half):
        straight = held[0][s] + pltpu.roll(held[1][s], rank, 1)
        turned = pltpu.roll(straight, rank, 1)
        for part in (s, s + half):
            first = straight if part < half else turned
            other = turned if part < half else straight
            both = jnp.where(low, first, other)
            wide = jnp.concatenate([both] * (count * rank // LANES), axis=1)
            mask = owner_mask(row_owners(row_refs[part], features), ids, rank)
            wide = jnp.where(mask, wide, 0.0).astype(jnp.bfloat16)
            product = jnp.dot(wide, weight, preferred_element_type=jnp.float32)
            if not gridded:
                out_refs[part][...] = product.astype(jnp.bfloat16)
            else:

                @pl.when(step == 0)
                def _():
                    total_ref[part] = product

                @pl.when(step > 0)
                def _():
                    total_ref[part] += product

                @pl.when(step == last)
                def _():
                    out_refs[part][...] = total_ref[part].astype(jnp.bfloat16)


def attend_kernel(
    parts, me_ref, len_ref, base_ref, nk_ref, nv_ref, ck_ref, cv_ref, *refs
):
    delta_refs, out_ref = refs[:parts], refs[parts]
    me = me_ref[0]
    requests, columns = base_ref.shape
    width = columns // parts
    groups = nk_ref.shape[1] // HEAD
    slots = ck_ref.shape[1]
    heads = columns // HEAD
    per_part = width // HEAD
    span = heads * HALF
    part_span = per_part * HALF
    keys_in = HALF * slots + STEP
    row = lax.broadcasted_iota(jnp.int32, (keys_in, span), 0)
    lane_req = lax.broadcasted_iota(jnp.int32, (keys_in, span), 1) % HALF
    own = row - HALF * slots
    slot_of = []
    for h in range(STEP // HALF):
        cached = jnp.where(row // slots == lane_req, row % slots, slots)
        fresh = jnp.where(own == lane_req + h * HALF, -1, slots)
        slot_of.append(jnp.where(own >= 0, fresh, cached))
    part_at = [me ^ s for s in range(parts)]
    group_at = [p // (parts // groups) for p in part_at]
    lane_part = lax.broadcasted_iota(jnp.int32, (1, span), 1) // part_span
    lane_group = jnp.zeros_like(lane_part)
    for s in range(parts):
        lane_group = jnp.where(lane_part == s, group_at[s], lane_group)
    scale = 1.0 / math.sqrt(HEAD)
    ones = jnp.ones((keys_in, HEAD), jnp.bfloat16)

    def body(step, _):
        units = []
        for j in range(BATCH):
            start = pl.multiple_of((step * BATCH + j) * STEP, STEP)
            at = pl.ds(start, STEP)
            pieces = []
            for s in range(parts):
                lanes = pl.ds(pl.multiple_of(part_at[s] * width, width), width)
                q = base_ref[at, lanes].astype(jnp.float32)
                q = q + delta_refs[s][at, :].astype(jnp.float32)
                pieces += [q[:, k * HEAD : (k + 1) * HEAD] for k in range(per_part)]
            for h in range(STEP // HALF):
                slab = pl.ds(pl.multiple_of(start + h * HALF, HALF), HALF)
                q = jnp.concatenate([p[h * HALF : (h + 1) * HALF] for p in pieces], axis=0)
                units.append((step * BATCH + j, at, h, slab, q.astype(jnp.bfloat16)))
        scores = []
        for _, at, h, slab, q in units:
            both = []
            for g in range(groups):
                lanes = slice(g * HEAD, (g + 1) * HEAD)
                keys = ck_ref[slab, :, lanes].reshape(HALF * slots, HEAD)
                keys = jnp.concatenate([keys, nk_ref[at, lanes]], axis=0)
                both.append(lax.dot_general(keys, q, NT, preferred_element_type=jnp.float32))
            score = both[0]
            for g in range(1, groups):
                score = jnp.where(lane_group == g, both[g], score)
            scores.append(score)
        probs = []
        for (i, at, h, slab, q), score in zip(units, scores):
            lens = len_ref[pl.ds(i * (STEP // HALF) + h, 1), :]
            score = jnp.where(slot_of[h] < lens, score, DEAD)
            top = jnp.max(score, axis=0, keepdims=True)
            exps = jnp.exp((score - top) * scale)
            total = jnp.sum(exps, axis=0, keepdims=True)
            probs.append((exps * (1.0 / total)).astype(jnp.bfloat16))
        mixed = []
        for (i, at, h, slab, q), prob in zip(units, probs):
            whole = []
            for g in range(groups):
                lanes = slice(g * HEAD, (g + 1) * HEAD)
                values = cv_ref[slab, :, lanes].reshape(HALF * slots, HEAD)
                values = jnp.concatenate([values, nv_ref[at, lanes]], axis=0)
                whole.append(
                    lax.dot_general(prob, values, TN, preferred_element_type=jnp.float32)
                )
            mixed.append(whole)
        for j in range(BATCH):
            at = units[2 * j][1]
            for s in range(parts):
                rows = slice(s * part_span, (s + 1) * part_span)
                halves = []
                for h in range(STEP // HALF):
                    whole = mixed[2 * j + h]
                    part = whole[0][rows]
                    for g in range(1, groups):
                        part = jnp.where(group_at[s] == g, whole[g][rows], part)
                    halves.append(part)
                out = [
                    jnp.concatenate([p[k * HALF : (k + 1) * HALF] for p in halves], axis=0)
                    for k in range(per_part)
                ]
                lanes = pl.ds(pl.multiple_of(part_at[s] * width, width), width)
                out_ref[at, lanes] = jnp.concatenate(out, axis=1).astype(jnp.bfloat16)
        return 0

    lax.fori_loop(0, requests // (STEP * BATCH), body, 0)


def attend(me, base, new_key, new_value, cache_keys, cache_values, lengths, deltas):
    requests, columns = base.shape
    kv = new_key.shape[1]
    slots = cache_keys.shape[1]
    lengths = jnp.tile(lengths.reshape(requests // HALF, HALF), (1, columns // HEAD))
    return pl.pallas_call(
        functools.partial(attend_kernel, len(deltas)),
        out_shape=jax.ShapeDtypeStruct((requests, columns), jnp.bfloat16),
        in_specs=[SMEM] + [VMEM] * (6 + len(deltas)),
        out_specs=VMEM,
        compiler_params=PARAMS,
        cost_estimate=pl.CostEstimate(
            flops=4 * requests * HALF * slots * columns,
            bytes_accessed=4 * requests * (columns + slots * kv),
            transcendentals=requests * slots * columns // 16,
        ),
    )(me, lengths, base, new_key, new_value, cache_keys, cache_values, *deltas)


def shrink_rows(ids, rows, weights, base, chunk):
    parts = len(rows)
    gridded = chunk is not None
    rank, features = weights[0].shape[1:]
    specs = [SMEM] + [VMEM] * (parts + len(weights) + 1)
    grid = ()
    if gridded:
        grid = (weights[0].shape[0] // chunk,)
        specs[1 + parts] = pl.BlockSpec((chunk, rank, features), lambda i: (i, 0, 0))
    return pl.pallas_call(
        functools.partial(shrink_kernel, parts, len(weights), gridded),
        out_shape=jax.ShapeDtypeStruct(base.shape, jnp.float32),
        grid=grid,
        in_specs=specs,
        out_specs=VMEM,
        compiler_params=PARAMS,
        cost_estimate=pl.CostEstimate(
            flops=2 * parts * rows[0].shape[0] * features * rank * sum(w.shape[0] for w in weights),
            bytes_accessed=4 * parts * rows[0].size,
            transcendentals=0,
        ),
    )(ids, *rows, *weights, base)


def expand_rows(ids, me, rows, low, weights, chunk, cores):
    parts = len(rows)
    gridded = chunk is not None
    rank, outputs = weights[0].shape[1:]
    requests = rows[0].shape[0]
    specs = [SMEM, SMEM] + [VMEM] * (parts + 1 + len(weights))
    grid = ()
    if gridded:
        grid = (weights[0].shape[0] // chunk,)
        specs[3 + parts] = pl.BlockSpec((chunk, rank, outputs), lambda i: (i, 0, 0))
    held = (parts, requests, outputs) if gridded else (1, 8, LANES)
    return pl.pallas_call(
        functools.partial(expand_kernel, parts, len(weights), cores, gridded),
        out_shape=[jax.ShapeDtypeStruct((requests, outputs), jnp.bfloat16)] * parts,
        grid=grid,
        in_specs=specs,
        out_specs=[VMEM] * parts,
        scratch_shapes=[pltpu.VMEM(held, jnp.float32)],
        compiler_params=PARAMS,
    )(ids, me, *rows, low, *weights)


def per_device(
    hidden,
    adapter_ids,
    owner_map,
    shrink_factors,
    expand_factors,
    query_base,
    new_key,
    new_value,
    cache_keys,
    cache_values,
    lengths,
):
    reps, levels, sides, tp = (lax.axis_size(a) for a in ("rep", "level", "side", "tp"))
    requests, wide = hidden.shape
    rank = shrink_factors.shape[2]
    square = reps * sides
    features = wide // square
    outputs = query_base.shape[1] // square
    level, side = lax.axis_index("level"), lax.axis_index("side")
    me = lax.axis_index("rep") * sides + side

    def swap(a, s):
        pairs = [(c, c ^ s) for c in range(square)]
        return lax.ppermute(a, ("rep", "side"), pairs)

    def tied(a, *others):
        return lax.optimization_barrier((a, *others))[0]

    def cut(a, width, at):
        return lax.dynamic_slice_in_dim(a, at * width, width, 2)

    shrink = shrink_factors.swapaxes(1, 2)
    shrink_own = cut(shrink, features, me)
    shrink_next = swap(cut(shrink, features, me ^ 1), 1)
    rows = pl.pallas_call(
        functools.partial(pack_kernel, square),
        out_shape=[jax.ShapeDtypeStruct((requests, features + LANES), jnp.bfloat16)] * square,
        in_specs=[SMEM, SMEM, VMEM, VMEM],
        out_specs=[VMEM] * square,
        compiler_params=PARAMS,
    )(me[None], owner_map, adapter_ids, hidden)
    rows = [rows[0]] + [swap(rows[s], s) for s in range(1, square)]

    empty = jnp.zeros((square // 2 * requests, LANES), jnp.float32)
    order = jnp.arange(levels, dtype=jnp.int32)
    if levels == 4:
        near_pairs = [(i, i ^ 1) for i in range(levels)]
        far_pairs = [(i, i ^ 2) for i in range(levels)]

        def gather(a):
            far = lax.ppermute(a, "level", far_pairs)
            near = lax.ppermute(a, "level", near_pairs)
            inner = lax.ppermute(a, "level", [(1, 2), (2, 1)])
            outer = lax.ppermute(far, "level", [(2, 3), (1, 0)])
            return [a, near, far, jnp.where((level == 1) | (level == 2), inner, outer)]

        own_ids = (level ^ order) * sides + side
        next_ids = (level ^ order) * sides + (side ^ 1)
        own_blocks = gather(shrink_own)
        next_blocks = gather(shrink_next)
        partial = shrink_rows(own_ids, rows, own_blocks, empty, None)
        partial = shrink_rows(next_ids, rows, next_blocks, partial, None)
        expand = tied(expand_factors, own_blocks[1], own_blocks[2])
        expand_own = cut(expand, outputs, me)
        expand_next = swap(cut(expand, outputs, me ^ 1), 1)
        expand = gather(jnp.concatenate([expand_own, expand_next], axis=0))
        expand_ids = jnp.stack([own_ids, next_ids], axis=1).reshape(-1)
        chunk = None
    else:
        expand_own = cut(expand_factors, outputs, me)
        expand_next = swap(cut(expand_factors, outputs, me ^ 1), 1)
        pair = jnp.stack([side, side ^ 1])
        expand_ids = (order[:, None] * sides + pair[None, :]).reshape(-1)
        chunk = 4

        def gather(own, other):
            both = jnp.concatenate([own, other], axis=0)
            return lax.all_gather(both, "level", axis=0, tiled=True)

        expand = [gather(expand_own, expand_next)]
        weights = [gather(shrink_own, shrink_next)]
        partial = shrink_rows(expand_ids, rows, weights, empty, chunk)

    partial = partial.astype(jnp.bfloat16)
    partial = jnp.broadcast_to(partial[None], (square * tp,) + partial.shape)
    sums = lax.all_to_all(partial, ("rep", "side", "tp"), split_axis=0, concat_axis=0, tiled=True)
    deltas = expand_rows(expand_ids, me[None], rows, sums, expand, chunk, tp)
    deltas = [deltas[0]] + [swap(deltas[s], s) for s in range(1, square)]
    return attend(
        me[None],
        query_base,
        new_key,
        new_value,
        cache_keys,
        cache_values,
        lengths,
        deltas,
    )


def solution(mesh):
    reps, pool, tp = (mesh.shape[a] for a in ("rep", "pool", "tp"))
    finer = Mesh(mesh.devices.reshape(reps, pool // 2, 2, tp), ("rep", "level", "side", "tp"))
    pooled = ("level", "side")
    requests = ("rep", "level", "side")
    in_specs = (
        P(requests, "tp"),
        P(requests, None),
        P(),
        P(pooled, "tp", None),
        P(pooled, None, "tp"),
        P(requests, "tp"),
        P(requests, "tp"),
        P(requests, "tp"),
        P(requests, None, "tp"),
        P(requests, None, "tp"),
        P(requests),
    )
    return jax.shard_map(
        per_device, mesh=finer, in_specs=in_specs, out_specs=P(requests, "tp"), check_vma=False
    )
```

```python
import functools
import math

import jax
import jax.numpy as jnp
from jax import lax
from jax.experimental import pallas as pl
from jax.experimental.pallas import tpu as pltpu
from jax.sharding import Mesh
from jax.sharding import PartitionSpec as P

HEAD = 128
LANES = 128
STEP = 16
HALF = 8
BATCH = 4
DEAD = -1e30
VMEM = pl.BlockSpec(memory_space=pltpu.VMEM)
SMEM = pl.BlockSpec(memory_space=pltpu.SMEM)
HBM = pl.BlockSpec(memory_space=pltpu.HBM)
PARAMS = pltpu.CompilerParams(vmem_limit_bytes=12 * 1024 * 1024)
NT = (((1,), (1,)), ((), ()))
TN = (((0,), (0,)), ((), ()))


def pack_kernel(parts, me_ref, map_ref, ids_ref, hidden_ref, shrink_ref, expand_ref, *refs):
    rows_ref, own_ref, next_ref, expand_own_ref, sems = refs
    requests, wide = hidden_ref.shape
    features, outputs = wide // parts, expand_ref.shape[2] // parts
    me = me_ref[0]

    def columns(at, width):
        return pl.ds(pl.multiple_of(at * width, width), width)

    moves = [
        (shrink_ref.at[:, :, columns(me, features)], own_ref),
        (shrink_ref.at[:, :, columns(me ^ 1, features)], next_ref.at[:, :, :features]),
        (expand_ref.at[:, :, columns(me ^ 1, outputs)], next_ref.at[:, :, features:]),
        (expand_ref.at[:, :, columns(me, outputs)], expand_own_ref),
    ]
    for s in range(parts):
        at = slice(s * features, (s + 1) * features)
        moves.append((hidden_ref.at[:, at], rows_ref.at[s, :, :features]))
    copies = [pltpu.make_async_copy(src, dst, sems.at[k]) for k, (src, dst) in enumerate(moves)]
    for copy in copies:
        copy.start()
    ids = ids_ref[...]

    def look(k, found):
        return jnp.where(ids == k, map_ref[k], found)

    owners = lax.fori_loop(0, map_ref.shape[0], look, jnp.zeros_like(ids))
    owners = jnp.broadcast_to(owners.astype(jnp.float32), (LANES, requests)).T
    for s in range(parts):
        rows_ref[s, :, features:] = owners.astype(jnp.bfloat16)
    for copy in copies:
        copy.wait()


def owner_mask(owners, ids, rank):
    lane = lax.broadcasted_iota(jnp.int32, (1, len(ids) * rank), 1) // rank
    named = jnp.full_like(lane, -1)
    for k, owner in enumerate(ids):
        named = jnp.where(lane == k, owner, named)
    wide = jnp.concatenate([owners] * (len(ids) * rank // LANES), axis=1)
    return wide == named


def row_owners(ref, features):
    return ref[:, features:].astype(jnp.float32).astype(jnp.int32)


def stacked(refs):
    blocks = [r[k] for r in refs for k in range(r.shape[0])]
    return jnp.concatenate(blocks, axis=0)


def shrink_kernel(parts, blocks, gridded, ids_ref, *refs):
    rows_ref, weight_refs, base_ref, out_ref = refs[0], refs[1 : 1 + blocks], refs[1 + blocks], refs[-1]
    row_refs = [rows_ref.at[s] for s in range(parts)]
    rank, features = weight_refs[0].shape[1:]
    requests = row_refs[0].shape[0]
    count = sum(r.shape[0] for r in weight_refs)
    step = pl.program_id(0) if gridded else 0
    ids = [ids_ref[step * count + k] for k in range(count)]
    weight = stacked(weight_refs)
    low = lax.broadcasted_iota(jnp.int32, (requests, LANES), 1) < rank
    folded = []
    for ref in row_refs:
        sums = lax.dot_general(
            ref[:, :features], weight, NT, preferred_element_type=jnp.float32
        )
        sums = jnp.where(owner_mask(row_owners(ref, features), ids, rank), sums, 0.0)
        total = sums[:, :LANES]
        for k in range(1, count * rank // LANES):
            total = total + sums[:, k * LANES : (k + 1) * LANES]
        folded.append(total + pltpu.roll(total, rank, 1))
    if gridded:

        @pl.when(step == 0)
        def _():
            out_ref[...] = base_ref[...]

    else:
        out_ref[...] = base_ref[...]
    half = parts // 2
    for s in range(half):
        rows = pl.ds(s * requests, requests)
        out_ref[rows, :] += jnp.where(low, folded[s], folded[s + half])


def expand_kernel(parts, blocks, gridded, ids_ref, me_ref, rows_ref, *refs):
    low_refs, weight_refs, out_refs, (held_ref, total_ref) = (
        refs[:parts],
        refs[parts : parts + blocks],
        refs[parts + blocks : 2 * parts + blocks],
        refs[-2:],
    )
    me = me_ref[0]
    rank, outputs = weight_refs[0].shape[1:]
    requests, features = rows_ref.shape[1], rows_ref.shape[2] - LANES
    count = sum(r.shape[0] for r in weight_refs)
    step = pl.program_id(0) if gridded else 0
    last = pl.num_programs(0) - 1 if gridded else 0
    ids = [ids_ref[step * count + k] for k in range(count)]
    weight = stacked(weight_refs)
    half = parts // 2
    low = lax.broadcasted_iota(jnp.int32, (requests, LANES), 1) < rank
    low_sum = low_refs[0][...].astype(jnp.float32)
    for ref in low_refs[1:]:
        low_sum = low_sum + ref[...].astype(jnp.float32)
    for s in range(half):
        straight = low_sum[s * requests : (s + 1) * requests]
        turned = pltpu.roll(straight, rank, 1)
        held_ref[s] = jnp.where(low, straight, turned)
        held_ref[s + half] = jnp.where(low, turned, straight)
    for s in range(parts):
        both = held_ref[me ^ s]
        wide = jnp.concatenate([both] * (count * rank // LANES), axis=1)
        mask = owner_mask(row_owners(rows_ref.at[me ^ s], features), ids, rank)
        wide = jnp.where(mask, wide, 0.0).astype(jnp.bfloat16)
        product = jnp.dot(wide, weight, preferred_element_type=jnp.float32)
        if not gridded:
            out_refs[s][...] = product.astype(jnp.bfloat16)
        else:

            @pl.when(step == 0)
            def _():
                total_ref[s] = product

            @pl.when(step > 0)
            def _():
                total_ref[s] += product

            @pl.when(step == last)
            def _():
                out_refs[s][...] = total_ref[s].astype(jnp.bfloat16)


def attend_kernel(
    parts, me_ref, len_ref, base_ref, nk_ref, nv_ref, ck_ref, cv_ref, *refs
):
    delta_refs, out_ref = refs[:parts], refs[parts]
    me = me_ref[0]
    requests, columns = base_ref.shape
    width = columns // parts
    groups = nk_ref.shape[1] // HEAD
    slots = ck_ref.shape[1]
    heads = columns // HEAD
    per_part = width // HEAD
    span = heads * HALF
    part_span = per_part * HALF
    keys_in = HALF * slots + STEP
    row = lax.broadcasted_iota(jnp.int32, (keys_in, span), 0)
    lane_req = lax.broadcasted_iota(jnp.int32, (keys_in, span), 1) % HALF
    own = row - HALF * slots
    slot_of = []
    for h in range(STEP // HALF):
        cached = jnp.where(row // slots == lane_req, row % slots, slots)
        fresh = jnp.where(own == lane_req + h * HALF, -1, slots)
        slot_of.append(jnp.where(own >= 0, fresh, cached))
    part_at = [me ^ s for s in range(parts)]
    group_at = [p // (parts // groups) for p in part_at]
    lane_part = lax.broadcasted_iota(jnp.int32, (1, span), 1) // part_span
    lane_group = jnp.zeros_like(lane_part)
    for s in range(parts):
        lane_group = jnp.where(lane_part == s, group_at[s], lane_group)
    scale = 1.0 / math.sqrt(HEAD)
    ones = jnp.ones((keys_in, HEAD), jnp.bfloat16)

    def body(step, _):
        units = []
        for j in range(BATCH):
            start = pl.multiple_of((step * BATCH + j) * STEP, STEP)
            at = pl.ds(start, STEP)
            pieces = []
            for s in range(parts):
                lanes = pl.ds(pl.multiple_of(part_at[s] * width, width), width)
                q = base_ref[at, lanes].astype(jnp.float32)
                q = q + delta_refs[s][at, :].astype(jnp.float32)
                pieces += [q[:, k * HEAD : (k + 1) * HEAD] for k in range(per_part)]
            for h in range(STEP // HALF):
                slab = pl.ds(pl.multiple_of(start + h * HALF, HALF), HALF)
                q = jnp.concatenate([p[h * HALF : (h + 1) * HALF] for p in pieces], axis=0)
                units.append((step * BATCH + j, at, h, slab, q.astype(jnp.bfloat16)))
        scores = []
        for _, at, h, slab, q in units:
            both = []
            for g in range(groups):
                lanes = slice(g * HEAD, (g + 1) * HEAD)
                keys = ck_ref[slab, :, lanes].reshape(HALF * slots, HEAD)
                keys = jnp.concatenate([keys, nk_ref[at, lanes]], axis=0)
                both.append(lax.dot_general(keys, q, NT, preferred_element_type=jnp.float32))
            score = both[0]
            for g in range(1, groups):
                score = jnp.where(lane_group == g, both[g], score)
            scores.append(score)
        probs = []
        for (i, at, h, slab, q), score in zip(units, scores):
            lens = len_ref[pl.ds(i * (STEP // HALF) + h, 1), :]
            score = jnp.where(slot_of[h] < lens, score, DEAD)
            top = jnp.max(score, axis=0, keepdims=True)
            exps = jnp.exp((score - top) * scale)
            total = jnp.sum(exps, axis=0, keepdims=True)
            probs.append((exps * (1.0 / total)).astype(jnp.bfloat16))
        mixed = []
        for (i, at, h, slab, q), prob in zip(units, probs):
            whole = []
            for g in range(groups):
                lanes = slice(g * HEAD, (g + 1) * HEAD)
                values = cv_ref[slab, :, lanes].reshape(HALF * slots, HEAD)
                values = jnp.concatenate([values, nv_ref[at, lanes]], axis=0)
                whole.append(
                    lax.dot_general(prob, values, TN, preferred_element_type=jnp.float32)
                )
            mixed.append(whole)
        for j in range(BATCH):
            at = units[2 * j][1]
            for s in range(parts):
                rows = slice(s * part_span, (s + 1) * part_span)
                halves = []
                for h in range(STEP // HALF):
                    whole = mixed[2 * j + h]
                    part = whole[0][rows]
                    for g in range(1, groups):
                        part = jnp.where(group_at[s] == g, whole[g][rows], part)
                    halves.append(part)
                out = [
                    jnp.concatenate([p[k * HALF : (k + 1) * HALF] for p in halves], axis=0)
                    for k in range(per_part)
                ]
                lanes = pl.ds(pl.multiple_of(part_at[s] * width, width), width)
                out_ref[at, lanes] = jnp.concatenate(out, axis=1).astype(jnp.bfloat16)
        return 0

    lax.fori_loop(0, requests // (STEP * BATCH), body, 0)


def attend(me, base, new_key, new_value, cache_keys, cache_values, lengths, deltas):
    requests, columns = base.shape
    kv = new_key.shape[1]
    slots = cache_keys.shape[1]
    lengths = jnp.tile(lengths.reshape(requests // HALF, HALF), (1, columns // HEAD))
    return pl.pallas_call(
        functools.partial(attend_kernel, len(deltas)),
        out_shape=jax.ShapeDtypeStruct((requests, columns), jnp.bfloat16),
        in_specs=[SMEM] + [VMEM] * (6 + len(deltas)),
        out_specs=VMEM,
        compiler_params=PARAMS,
        cost_estimate=pl.CostEstimate(
            flops=4 * requests * HALF * slots * columns,
            bytes_accessed=4 * requests * (columns + slots * kv),
            transcendentals=requests * slots * columns // 16,
        ),
    )(me, lengths, base, new_key, new_value, cache_keys, cache_values, *deltas)


def shrink_rows(ids, rows, weights, base, chunk):
    parts = rows.shape[0]
    gridded = chunk is not None
    rank, features = weights[0].shape[1:]
    specs = [SMEM] + [VMEM] * (len(weights) + 2)
    grid = ()
    if gridded:
        grid = (weights[0].shape[0] // chunk,)
        specs[2] = pl.BlockSpec((chunk, rank, features), lambda i: (i, 0, 0))
    return pl.pallas_call(
        functools.partial(shrink_kernel, parts, len(weights), gridded),
        out_shape=jax.ShapeDtypeStruct(base.shape, jnp.float32),
        grid=grid,
        in_specs=specs,
        out_specs=VMEM,
        compiler_params=PARAMS,
        cost_estimate=pl.CostEstimate(
            flops=2 * parts * rows.shape[1] * features * rank * sum(w.shape[0] for w in weights),
            bytes_accessed=4 * rows.size,
            transcendentals=0,
        ),
    )(ids, rows, *weights, base)


def expand_rows(ids, me, rows, lows, weights, chunk):
    parts, requests, _ = rows.shape
    gridded = chunk is not None
    rank, outputs = weights[0].shape[1:]
    specs = [SMEM, SMEM] + [VMEM] * (1 + parts + len(weights))
    grid = ()
    if gridded:
        grid = (weights[0].shape[0] // chunk,)
        specs[3 + parts] = pl.BlockSpec((chunk, rank, outputs), lambda i: (i, 0, 0))
    held = (parts, requests, outputs) if gridded else (1, 8, LANES)
    return pl.pallas_call(
        functools.partial(expand_kernel, parts, len(weights), gridded),
        out_shape=[jax.ShapeDtypeStruct((requests, outputs), jnp.bfloat16)] * parts,
        grid=grid,
        in_specs=specs,
        out_specs=[VMEM] * parts,
        scratch_shapes=[
            pltpu.VMEM((parts, requests, LANES), jnp.float32),
            pltpu.VMEM(held, jnp.float32),
        ],
        compiler_params=PARAMS,
    )(ids, me, rows, *lows, *weights)


def per_device(
    hidden,
    adapter_ids,
    owner_map,
    shrink_factors,
    expand_factors,
    query_base,
    new_key,
    new_value,
    cache_keys,
    cache_values,
    lengths,
):
    reps, levels, sides, tp = (lax.axis_size(a) for a in ("rep", "level", "side", "tp"))
    requests, wide = hidden.shape
    rank = shrink_factors.shape[2]
    square = reps * sides
    features = wide // square
    outputs = query_base.shape[1] // square
    level, side = lax.axis_index("level"), lax.axis_index("side")
    me = lax.axis_index("rep") * sides + side

    def swap(a, s):
        pairs = [(c, c ^ s) for c in range(square)]
        return lax.ppermute(a, ("rep", "side"), pairs)

    def tied(a, *others):
        return lax.optimization_barrier((a, *others))[0]

    shrink = shrink_factors.swapaxes(1, 2)
    rows, shrink_own, both_next, expand_own = pl.pallas_call(
        functools.partial(pack_kernel, square),
        out_shape=[jax.ShapeDtypeStruct((square, requests, features + LANES), jnp.bfloat16)]
        + [jax.ShapeDtypeStruct((1, rank, w), jnp.bfloat16) for w in (features, features + outputs, outputs)],
        in_specs=[SMEM, SMEM, VMEM, HBM, HBM, HBM],
        out_specs=[VMEM] * 4,
        scratch_shapes=[pltpu.SemaphoreType.DMA((square + 4,))],
        compiler_params=pltpu.CompilerParams(vmem_limit_bytes=48 * 1024 * 1024),
    )(me[None], owner_map, adapter_ids.T, hidden, shrink, expand_factors)
    both_next = swap(both_next, 1)
    rows = lax.all_to_all(rows, ("rep", "side"), split_axis=0, concat_axis=0, tiled=True)
    shrink_next, expand_next = both_next[:, :, :features], both_next[:, :, features:]

    empty = jnp.zeros((square // 2 * requests, LANES), jnp.float32)
    order = jnp.arange(levels, dtype=jnp.int32)
    both_sides = jnp.stack([side, side ^ 1])[None, :]

    def gather_pairs(own, other):
        both = jnp.concatenate([own, other], axis=0)
        return lax.all_gather(both, "level", axis=0, tiled=True)

    if levels == 4:

        def gather(a):
            return [a] + [
                lax.ppermute(a, "level", [(i, i ^ k) for i in range(levels)])
                for k in range(1, levels)
            ]

        own_blocks = gather(shrink_own)
        next_blocks = gather(shrink_next)
        partial = shrink_rows((level ^ order) * sides + side, rows, own_blocks, empty, None)
        partial = shrink_rows((level ^ order) * sides + (side ^ 1), rows, next_blocks, partial, None)
        pair = jnp.concatenate([expand_own, expand_next], axis=0)
        pair = tied(pair, own_blocks[1], own_blocks[2])
        expand = gather(pair)
        level_ids = (level ^ order)[:, None] * sides
        chunk = None
    else:
        chunk = 4
        level_ids = order[:, None] * sides
        weights = [gather_pairs(shrink_own, shrink_next)]
        partial = shrink_rows((level_ids + both_sides).reshape(-1), rows, weights, empty, chunk)
        expand = [gather_pairs(expand_own, expand_next)]

    for c in range(1, tp):
        partial = partial + lax.ppermute(partial, "tp", [(t, t ^ c) for t in range(tp)])
    partial = partial.astype(jnp.bfloat16)
    lows = [partial] + [swap(partial, s) for s in range(1, square)]
    expand_ids = (level_ids + both_sides).reshape(-1)
    deltas = expand_rows(expand_ids, me[None], rows, lows, expand, chunk)
    deltas = [deltas[0]] + [swap(deltas[s], s) for s in range(1, square)]
    return attend(
        me[None],
        query_base,
        new_key,
        new_value,
        cache_keys,
        cache_values,
        lengths,
        deltas,
    )


def solution(mesh):
    reps, pool, tp = (mesh.shape[a] for a in ("rep", "pool", "tp"))
    finer = Mesh(mesh.devices.reshape(reps, pool // 2, 2, tp), ("rep", "level", "side", "tp"))
    pooled = ("level", "side")
    requests = ("rep", "level", "side")
    in_specs = (
        P(requests, "tp"),
        P(requests, None),
        P(),
        P(pooled, "tp", None),
        P(pooled, None, "tp"),
        P(requests, "tp"),
        P(requests, "tp"),
        P(requests, "tp"),
        P(requests, None, "tp"),
        P(requests, None, "tp"),
        P(requests),
    )
    return jax.shard_map(
        per_device, mesh=finer, in_specs=in_specs, out_specs=P(requests, "tp"), check_vma=False
    )
```

```python
import functools
import math

import jax
import jax.numpy as jnp
from jax import lax
from jax.experimental import pallas as pl
from jax.experimental.pallas import tpu as pltpu
from jax.sharding import Mesh
from jax.sharding import PartitionSpec as P

HEAD = 128
LANES = 128
STEP = 16
HALF = 8
BATCH = 2
DEAD = -1e30
VMEM = pl.BlockSpec(memory_space=pltpu.VMEM)
SMEM = pl.BlockSpec(memory_space=pltpu.SMEM)
HBM = pl.BlockSpec(memory_space=pltpu.HBM)
PARAMS = pltpu.CompilerParams(vmem_limit_bytes=12 * 1024 * 1024)
NT = (((1,), (1,)), ((), ()))
TN = (((0,), (0,)), ((), ()))


def columns(at, width):
    return pl.ds(pl.multiple_of(at * width, width), width)


def factor_kernel(parts, me_ref, shrink_ref, expand_ref, own_ref, next_ref, sems):
    features, outputs = shrink_ref.shape[2] // parts, expand_ref.shape[2] // parts
    copies = []
    for k, (at, ref) in enumerate(((me_ref[0] ^ 1, next_ref), (me_ref[0], own_ref))):
        shrink = shrink_ref.at[:, :, columns(at, features)]
        expand = expand_ref.at[:, :, columns(at, outputs)]
        copies += [
            pltpu.make_async_copy(shrink, ref.at[:, :, :features], sems.at[2 * k]),
            pltpu.make_async_copy(expand, ref.at[:, :, features:], sems.at[2 * k + 1]),
        ]
    for copy in copies:
        copy.start()
    for copy in copies:
        copy.wait()


def row_kernel(parts, map_ref, ids_ref, hidden_ref, rows_ref, sems):
    requests, wide = hidden_ref.shape
    features = wide // parts
    copies = []
    for s in range(parts):
        at = slice(s * features, (s + 1) * features)
        dst = rows_ref.at[s, :, :features]
        copies.append(pltpu.make_async_copy(hidden_ref.at[:, at], dst, sems.at[s]))
    for copy in copies:
        copy.start()
    ids = ids_ref[...]

    def look(k, found):
        return jnp.where(ids == k, map_ref[k], found)

    owners = lax.fori_loop(0, map_ref.shape[0], look, jnp.zeros_like(ids))
    owners = jnp.broadcast_to(owners.astype(jnp.float32), (LANES, requests)).T
    for s in range(parts):
        rows_ref[s, :, features:] = owners.astype(jnp.bfloat16)
    for copy in copies:
        copy.wait()


def owner_mask(owners, ids, rank):
    lane = lax.broadcasted_iota(jnp.int32, (1, len(ids) * rank), 1) // rank
    named = jnp.full_like(lane, -1)
    for k, owner in enumerate(ids):
        named = jnp.where(lane == k, owner, named)
    wide = jnp.concatenate([owners] * (len(ids) * rank // LANES), axis=1)
    return wide == named


def row_owners(ref, features):
    return ref[:, features:].astype(jnp.float32).astype(jnp.int32)


def stacked(refs, lanes):
    blocks = [r[k, :, lanes] for r in refs for k in range(r.shape[0])]
    return jnp.concatenate(blocks, axis=0)


def shrink_kernel(parts, blocks, gridded, ids_ref, *refs):
    rows_ref, weight_refs, base_ref, out_ref = refs[0], refs[1 : 1 + blocks], refs[1 + blocks], refs[-1]
    row_refs = [rows_ref.at[s] for s in range(parts)]
    rank = weight_refs[0].shape[1]
    requests, features = rows_ref.shape[1], rows_ref.shape[2] - LANES
    count = sum(r.shape[0] for r in weight_refs)
    step = pl.program_id(0) if gridded else 0
    ids = [ids_ref[step * count + k] for k in range(count)]
    weight = stacked(weight_refs, slice(0, features))
    low = lax.broadcasted_iota(jnp.int32, (requests, LANES), 1) < rank
    folded = []
    for ref in row_refs:
        sums = lax.dot_general(
            ref[:, :features], weight, NT, preferred_element_type=jnp.float32
        )
        sums = jnp.where(owner_mask(row_owners(ref, features), ids, rank), sums, 0.0)
        total = sums[:, :LANES]
        for k in range(1, count * rank // LANES):
            total = total + sums[:, k * LANES : (k + 1) * LANES]
        folded.append(total + pltpu.roll(total, rank, 1))
    if gridded:

        @pl.when(step == 0)
        def _():
            out_ref[...] = base_ref[...]

    else:
        out_ref[...] = base_ref[...]
    half = parts // 2
    for s in range(half):
        rows = pl.ds(s * requests, requests)
        out_ref[rows, :] += jnp.where(low, folded[s], folded[s + half])


def expand_kernel(parts, blocks, gridded, ids_ref, me_ref, rows_ref, *refs):
    low_refs, weight_refs, out_refs, (held_ref, total_ref) = (
        refs[:parts],
        refs[parts : parts + blocks],
        refs[parts + blocks : 2 * parts + blocks],
        refs[-2:],
    )
    me = me_ref[0]
    rank, outputs = weight_refs[0].shape[1], out_refs[0].shape[1]
    requests, features = rows_ref.shape[1], rows_ref.shape[2] - LANES
    count = sum(r.shape[0] for r in weight_refs)
    step = pl.program_id(0) if gridded else 0
    last = pl.num_programs(0) - 1 if gridded else 0
    ids = [ids_ref[step * count + k] for k in range(count)]
    weight = stacked(weight_refs, slice(features, features + outputs))
    half = parts // 2
    low = lax.broadcasted_iota(jnp.int32, (requests, LANES), 1) < rank
    low_sum = low_refs[0][...].astype(jnp.float32)
    for ref in low_refs[1:]:
        low_sum = low_sum + ref[...].astype(jnp.float32)
    for s in range(half):
        straight = low_sum[s * requests : (s + 1) * requests]
        turned = pltpu.roll(straight, rank, 1)
        held_ref[s] = jnp.where(low, straight, turned)
        held_ref[s + half] = jnp.where(low, turned, straight)
    for s in range(parts):
        both = held_ref[me ^ s]
        wide = jnp.concatenate([both] * (count * rank // LANES), axis=1)
        mask = owner_mask(row_owners(rows_ref.at[me ^ s], features), ids, rank)
        wide = jnp.where(mask, wide, 0.0).astype(jnp.bfloat16)
        product = jnp.dot(wide, weight, preferred_element_type=jnp.float32)
        if not gridded:
            out_refs[s][...] = product.astype(jnp.bfloat16)
        else:

            @pl.when(step == 0)
            def _():
                total_ref[s] = product

            @pl.when(step > 0)
            def _():
                total_ref[s] += product

            @pl.when(step == last)
            def _():
                out_refs[s][...] = total_ref[s].astype(jnp.bfloat16)


def attend_kernel(
    parts, me_ref, len_ref, base_ref, nk_ref, nv_ref, ck_ref, cv_ref, *refs
):
    delta_refs, out_ref = refs[:parts], refs[parts]
    me = me_ref[0]
    requests, columns = base_ref.shape
    width = columns // parts
    groups = nk_ref.shape[1] // HEAD
    slots = ck_ref.shape[1]
    heads = columns // HEAD
    per_part = width // HEAD
    span = heads * HALF
    part_span = per_part * HALF
    keys_in = HALF * slots + STEP
    row = lax.broadcasted_iota(jnp.int32, (keys_in, span), 0)
    lane_req = lax.broadcasted_iota(jnp.int32, (keys_in, span), 1) % HALF
    own = row - HALF * slots
    slot_of = []
    for h in range(STEP // HALF):
        cached = jnp.where(row // slots == lane_req, row % slots, slots)
        fresh = jnp.where(own == lane_req + h * HALF, -1, slots)
        slot_of.append(jnp.where(own >= 0, fresh, cached))
    part_at = [me ^ s for s in range(parts)]
    group_at = [p // (parts // groups) for p in part_at]
    lane_part = lax.broadcasted_iota(jnp.int32, (1, span), 1) // part_span
    lane_group = jnp.zeros_like(lane_part)
    for s in range(parts):
        lane_group = jnp.where(lane_part == s, group_at[s], lane_group)
    scale = 1.0 / math.sqrt(HEAD)
    ones = jnp.ones((keys_in, HEAD), jnp.bfloat16)

    if True:
        step = pl.program_id(0)
        units = []
        for j in range(BATCH):
            start = j * STEP
            at = pl.ds(start, STEP)
            pieces = []
            for s in range(parts):
                lanes = pl.ds(pl.multiple_of(part_at[s] * width, width), width)
                q = base_ref[at, lanes].astype(jnp.float32)
                q = q + delta_refs[s][at, :].astype(jnp.float32)
                pieces += [q[:, k * HEAD : (k + 1) * HEAD] for k in range(per_part)]
            for h in range(STEP // HALF):
                slab = pl.ds(start + h * HALF, HALF)
                q = jnp.concatenate([p[h * HALF : (h + 1) * HALF] for p in pieces], axis=0)
                units.append((step * BATCH + j, at, h, slab, q.astype(jnp.bfloat16)))
        scores = []
        for _, at, h, slab, q in units:
            both = []
            for g in range(groups):
                lanes = slice(g * HEAD, (g + 1) * HEAD)
                keys = ck_ref[slab, :, lanes].reshape(HALF * slots, HEAD)
                keys = jnp.concatenate([keys, nk_ref[at, lanes]], axis=0)
                both.append(lax.dot_general(keys, q, NT, preferred_element_type=jnp.float32))
            score = both[0]
            for g in range(1, groups):
                score = jnp.where(lane_group == g, both[g], score)
            scores.append(score)
        probs = []
        for (i, at, h, slab, q), score in zip(units, scores):
            lens = len_ref[pl.ds(i * (STEP // HALF) + h, 1), :]
            score = jnp.where(slot_of[h] < lens, score, DEAD)
            top = jnp.max(score, axis=0, keepdims=True)
            exps = jnp.exp((score - top) * scale)
            total = jnp.sum(exps, axis=0, keepdims=True)
            probs.append((exps * (1.0 / total)).astype(jnp.bfloat16))
        mixed = []
        for (i, at, h, slab, q), prob in zip(units, probs):
            whole = []
            for g in range(groups):
                lanes = slice(g * HEAD, (g + 1) * HEAD)
                values = cv_ref[slab, :, lanes].reshape(HALF * slots, HEAD)
                values = jnp.concatenate([values, nv_ref[at, lanes]], axis=0)
                whole.append(
                    lax.dot_general(prob, values, TN, preferred_element_type=jnp.float32)
                )
            mixed.append(whole)
        for j in range(BATCH):
            at = units[2 * j][1]
            for s in range(parts):
                rows = slice(s * part_span, (s + 1) * part_span)
                halves = []
                for h in range(STEP // HALF):
                    whole = mixed[2 * j + h]
                    part = whole[0][rows]
                    for g in range(1, groups):
                        part = jnp.where(group_at[s] == g, whole[g][rows], part)
                    halves.append(part)
                out = [
                    jnp.concatenate([p[k * HALF : (k + 1) * HALF] for p in halves], axis=0)
                    for k in range(per_part)
                ]
                lanes = pl.ds(pl.multiple_of(part_at[s] * width, width), width)
                out_ref[at, lanes] = jnp.concatenate(out, axis=1).astype(jnp.bfloat16)


def attend(me, base, new_key, new_value, cache_keys, cache_values, lengths, deltas):
    requests, columns = base.shape
    kv = new_key.shape[1]
    slots = cache_keys.shape[1]
    lengths = jnp.tile(lengths.reshape(requests // HALF, HALF), (1, columns // HEAD))
    block = STEP * BATCH
    rows2 = lambda w: pl.BlockSpec((block, w), lambda i: (i, 0))
    rows3 = pl.BlockSpec((block, slots, kv), lambda i: (i, 0, 0))
    return pl.pallas_call(
        functools.partial(attend_kernel, len(deltas)),
        out_shape=jax.ShapeDtypeStruct((requests, columns), jnp.bfloat16),
        grid=(requests // block,),
        in_specs=[SMEM, whole(lengths), rows2(columns), rows2(kv), rows2(kv), rows3, rows3]
        + [rows2(d.shape[1]) for d in deltas],
        out_specs=rows2(columns),
        compiler_params=PARAMS,
        cost_estimate=pl.CostEstimate(
            flops=4 * requests * HALF * slots * columns,
            bytes_accessed=4 * requests * (columns + slots * kv),
            transcendentals=requests * slots * columns // 16,
        ),
    )(me, lengths, base, new_key, new_value, cache_keys, cache_values, *deltas)


def whole(array):
    return pl.BlockSpec(array.shape, lambda *_: (0,) * len(array.shape))


def factor_specs(weights, chunk):
    if chunk is None:
        return (1,), [whole(w) for w in weights]
    (weight,) = weights
    return (weight.shape[0] // chunk,), [
        pl.BlockSpec((chunk,) + weight.shape[1:], lambda i: (i, 0, 0))
    ]


def shrink_rows(ids, rows, weights, base, chunk):
    parts = rows.shape[0]
    grid, specs = factor_specs(weights, chunk)
    return pl.pallas_call(
        functools.partial(shrink_kernel, parts, len(weights), chunk is not None),
        out_shape=jax.ShapeDtypeStruct(base.shape, jnp.float32),
        grid=grid,
        in_specs=[SMEM, whole(rows), *specs, whole(base)],
        out_specs=whole(base),
        compiler_params=PARAMS,
    )(ids, rows, *weights, base)


def expand_rows(ids, me, rows, lows, weights, chunk, outputs):
    parts, requests, _ = rows.shape
    grid, specs = factor_specs(weights, chunk)
    out = jax.ShapeDtypeStruct((requests, outputs), jnp.bfloat16)
    held = (1, 8, LANES) if chunk is None else (parts, requests, outputs)
    return pl.pallas_call(
        functools.partial(expand_kernel, parts, len(weights), chunk is not None),
        out_shape=[out] * parts,
        grid=grid,
        in_specs=[SMEM, SMEM, whole(rows), *map(whole, lows), *specs],
        out_specs=[whole(out)] * parts,
        scratch_shapes=[
            pltpu.VMEM((parts, requests, LANES), jnp.float32),
            pltpu.VMEM(held, jnp.float32),
        ],
        compiler_params=PARAMS,
    )(ids, me, rows, *lows, *weights)


def per_device(
    hidden,
    adapter_ids,
    owner_map,
    shrink_factors,
    expand_factors,
    query_base,
    new_key,
    new_value,
    cache_keys,
    cache_values,
    lengths,
):
    reps, levels, sides, tp = (lax.axis_size(a) for a in ("rep", "level", "side", "tp"))
    requests, wide = hidden.shape
    rank = shrink_factors.shape[2]
    square = reps * sides
    features = wide // square
    outputs = query_base.shape[1] // square
    level, side = lax.axis_index("level"), lax.axis_index("side")
    me = lax.axis_index("rep") * sides + side

    def swap(a, s):
        pairs = [(c, c ^ s) for c in range(square)]
        return lax.ppermute(a, ("rep", "side"), pairs)

    def tied(a, *others):
        return lax.optimization_barrier((a, *others))[0]

    shrink = shrink_factors.swapaxes(1, 2)
    block = jax.ShapeDtypeStruct((1, rank, features + outputs), jnp.bfloat16)
    own, other = pl.pallas_call(
        functools.partial(factor_kernel, square),
        out_shape=[block, block],
        in_specs=[SMEM, HBM, HBM],
        out_specs=[VMEM, VMEM],
        scratch_shapes=[pltpu.SemaphoreType.DMA((4,))],
    )(me[None], shrink, expand_factors)
    other = swap(other, 1)
    rows = pl.pallas_call(
        functools.partial(row_kernel, square),
        out_shape=jax.ShapeDtypeStruct((square, requests, features + LANES), jnp.bfloat16),
        in_specs=[SMEM, VMEM, HBM],
        out_specs=VMEM,
        scratch_shapes=[pltpu.SemaphoreType.DMA((square,))],
    )(owner_map, adapter_ids.T, hidden)
    rows = tied(rows, other)
    rows = lax.all_to_all(rows, ("rep", "side"), split_axis=0, concat_axis=0, tiled=True)

    empty = jnp.zeros((square // 2 * requests, LANES), jnp.float32)
    order = jnp.arange(levels, dtype=jnp.int32)
    if levels == 4:
        near_pairs = [(i, i ^ 1) for i in range(levels)]
        far_pairs = [(i, i ^ 2) for i in range(levels)]

        def gather(a):
            far = lax.ppermute(a, "level", far_pairs)
            near = lax.ppermute(a, "level", near_pairs)
            inner = lax.ppermute(a, "level", [(1, 2), (2, 1)])
            outer = lax.ppermute(far, "level", [(2, 3), (1, 0)])
            return [a, near, far, jnp.where((level == 1) | (level == 2), inner, outer)]

        own_ids = (level ^ order) * sides + side
        next_ids = (level ^ order) * sides + (side ^ 1)
        own, other = gather(own), gather(other)
        partial = shrink_rows(own_ids, rows, own, empty, None)
        partial = shrink_rows(next_ids, rows, other, partial, None)
        factors, ids, chunk = own + other, jnp.concatenate([own_ids, next_ids]), None
    else:
        both = jnp.concatenate([own, other], axis=0)
        factors = [lax.all_gather(both, "level", axis=0, tiled=True)]
        ids = (order[:, None] * sides + jnp.stack([side, side ^ 1])[None, :]).reshape(-1)
        chunk = 4
        partial = shrink_rows(ids, rows, factors, empty, chunk)

    for c in range(1, tp):
        partial = partial + lax.ppermute(partial, "tp", [(t, t ^ c) for t in range(tp)])
    partial = partial.astype(jnp.bfloat16)
    lows = [partial] + [swap(partial, s) for s in range(1, square)]
    deltas = expand_rows(ids, me[None], rows, lows, factors, chunk, outputs)
    deltas = [deltas[0]] + [swap(deltas[s], s) for s in range(1, square)]
    return attend(
        me[None],
        query_base,
        new_key,
        new_value,
        cache_keys,
        cache_values,
        lengths,
        deltas,
    )


def solution(mesh):
    reps, pool, tp = (mesh.shape[a] for a in ("rep", "pool", "tp"))
    finer = Mesh(mesh.devices.reshape(reps, pool // 2, 2, tp), ("rep", "level", "side", "tp"))
    pooled = ("level", "side")
    requests = ("rep", "level", "side")
    in_specs = (
        P(requests, "tp"),
        P(requests, None),
        P(),
        P(pooled, "tp", None),
        P(pooled, None, "tp"),
        P(requests, "tp"),
        P(requests, "tp"),
        P(requests, "tp"),
        P(requests, None, "tp"),
        P(requests, None, "tp"),
        P(requests),
    )
    return jax.shard_map(
        per_device, mesh=finer, in_specs=in_specs, out_specs=P(requests, "tp"), check_vma=False
    )
```

```python
import functools
import math

import jax
import jax.numpy as jnp
from jax import lax
from jax.experimental import pallas as pl
from jax.experimental.pallas import tpu as pltpu
from jax.sharding import Mesh
from jax.sharding import PartitionSpec as P

HEAD = 128
LANES = 128
STEP = 16
HALF = 8
BATCH = 2
DEAD = -1e30
VMEM = pl.BlockSpec(memory_space=pltpu.VMEM)
SMEM = pl.BlockSpec(memory_space=pltpu.SMEM)
HBM = pl.BlockSpec(memory_space=pltpu.HBM)
PARAMS = pltpu.CompilerParams(vmem_limit_bytes=12 * 1024 * 1024)
NT = (((1,), (1,)), ((), ()))
TN = (((0,), (0,)), ((), ()))


def columns(at, width):
    return pl.ds(pl.multiple_of(at * width, width), width)


def factor_kernel(parts, me_ref, shrink_ref, expand_ref, own_ref, expand_own_ref, next_ref, sems):
    features, outputs = shrink_ref.shape[2] // parts, expand_ref.shape[2] // parts
    me = me_ref[0]
    moves = [
        (shrink_ref.at[:, :, columns(me ^ 1, features)], next_ref.at[:, :, :features]),
        (expand_ref.at[:, :, columns(me ^ 1, outputs)], next_ref.at[:, :, features:]),
        (shrink_ref.at[:, :, columns(me, features)], own_ref),
        (expand_ref.at[:, :, columns(me, outputs)], expand_own_ref),
    ]
    copies = [pltpu.make_async_copy(src, dst, sems.at[k]) for k, (src, dst) in enumerate(moves)]
    for copy in copies:
        copy.start()
    for copy in copies:
        copy.wait()


def row_kernel(parts, map_ref, ids_ref, hidden_ref, rows_ref, sems):
    requests, wide = hidden_ref.shape
    features = wide // parts
    copies = []
    for s in range(parts):
        at = slice(s * features, (s + 1) * features)
        dst = rows_ref.at[s, :, :features]
        copies.append(pltpu.make_async_copy(hidden_ref.at[:, at], dst, sems.at[s]))
    for copy in copies:
        copy.start()
    ids = ids_ref[...]

    def look(k, found):
        return jnp.where(ids == k, map_ref[k], found)

    owners = lax.fori_loop(0, map_ref.shape[0], look, jnp.zeros_like(ids))
    owners = jnp.broadcast_to(owners.astype(jnp.float32), (LANES, requests)).T
    for s in range(parts):
        rows_ref[s, :, features:] = owners.astype(jnp.bfloat16)
    for copy in copies:
        copy.wait()


def owner_mask(owners, ids, rank):
    lane = lax.broadcasted_iota(jnp.int32, (1, len(ids) * rank), 1) // rank
    named = jnp.full_like(lane, -1)
    for k, owner in enumerate(ids):
        named = jnp.where(lane == k, owner, named)
    wide = jnp.concatenate([owners] * (len(ids) * rank // LANES), axis=1)
    return wide == named


def row_owners(ref, features):
    return ref[:, features:].astype(jnp.float32).astype(jnp.int32)


def stacked(refs):
    blocks = [r[k] for r in refs for k in range(r.shape[0])]
    return jnp.concatenate(blocks, axis=0)


def shrink_kernel(parts, blocks, gridded, ids_ref, *refs):
    rows_ref, weight_refs, base_ref, out_ref = refs[0], refs[1 : 1 + blocks], refs[1 + blocks], refs[-1]
    row_refs = [rows_ref.at[s] for s in range(parts)]
    rank = weight_refs[0].shape[1]
    requests, features = rows_ref.shape[1], rows_ref.shape[2] - LANES
    count = sum(r.shape[0] for r in weight_refs)
    step = pl.program_id(0) if gridded else 0
    ids = [ids_ref[step * count + k] for k in range(count)]
    weight = stacked(weight_refs)
    low = lax.broadcasted_iota(jnp.int32, (requests, LANES), 1) < rank
    folded = []
    for ref in row_refs:
        sums = lax.dot_general(
            ref[:, :features], weight, NT, preferred_element_type=jnp.float32
        )
        sums = jnp.where(owner_mask(row_owners(ref, features), ids, rank), sums, 0.0)
        total = sums[:, :LANES]
        for k in range(1, count * rank // LANES):
            total = total + sums[:, k * LANES : (k + 1) * LANES]
        folded.append(total + pltpu.roll(total, rank, 1))
    if gridded:

        @pl.when(step == 0)
        def _():
            out_ref[...] = base_ref[...]

    else:
        out_ref[...] = base_ref[...]
    half = parts // 2
    for s in range(half):
        rows = pl.ds(s * requests, requests)
        out_ref[rows, :] += jnp.where(low, folded[s], folded[s + half])


def expand_kernel(parts, blocks, gridded, ids_ref, me_ref, rows_ref, *refs):
    low_refs, weight_refs, out_refs, (held_ref, total_ref) = (
        refs[:parts],
        refs[parts : parts + blocks],
        refs[parts + blocks : 2 * parts + blocks],
        refs[-2:],
    )
    me = me_ref[0]
    rank, outputs = weight_refs[0].shape[1], out_refs[0].shape[1]
    requests, features = rows_ref.shape[1], rows_ref.shape[2] - LANES
    count = sum(r.shape[0] for r in weight_refs)
    step = pl.program_id(0) if gridded else 0
    last = pl.num_programs(0) - 1 if gridded else 0
    ids = [ids_ref[step * count + k] for k in range(count)]
    weight = stacked(weight_refs)
    half = parts // 2
    low = lax.broadcasted_iota(jnp.int32, (requests, LANES), 1) < rank
    low_sum = low_refs[0][...].astype(jnp.float32)
    for ref in low_refs[1:]:
        low_sum = low_sum + ref[...].astype(jnp.float32)
    for s in range(half):
        straight = low_sum[s * requests : (s + 1) * requests]
        turned = pltpu.roll(straight, rank, 1)
        held_ref[s] = jnp.where(low, straight, turned)
        held_ref[s + half] = jnp.where(low, turned, straight)
    for s in range(parts):
        both = held_ref[me ^ s]
        wide = jnp.concatenate([both] * (count * rank // LANES), axis=1)
        mask = owner_mask(row_owners(rows_ref.at[me ^ s], features), ids, rank)
        wide = jnp.where(mask, wide, 0.0).astype(jnp.bfloat16)
        product = jnp.dot(wide, weight, preferred_element_type=jnp.float32)
        if not gridded:
            out_refs[s][...] = product.astype(jnp.bfloat16)
        else:

            @pl.when(step == 0)
            def _():
                total_ref[s] = product

            @pl.when(step > 0)
            def _():
                total_ref[s] += product

            @pl.when(step == last)
            def _():
                out_refs[s][...] = total_ref[s].astype(jnp.bfloat16)


def attend_kernel(
    parts, me_ref, len_ref, base_ref, nk_ref, nv_ref, ck_ref, cv_ref, *refs
):
    delta_refs, out_ref = refs[:parts], refs[parts]
    me = me_ref[0]
    requests, columns = base_ref.shape
    width = columns // parts
    groups = nk_ref.shape[1] // HEAD
    slots = ck_ref.shape[1]
    heads = columns // HEAD
    per_part = width // HEAD
    span = heads * HALF
    part_span = per_part * HALF
    keys_in = HALF * slots + STEP
    row = lax.broadcasted_iota(jnp.int32, (keys_in, span), 0)
    lane_req = lax.broadcasted_iota(jnp.int32, (keys_in, span), 1) % HALF
    own = row - HALF * slots
    slot_of = []
    for h in range(STEP // HALF):
        cached = jnp.where(row // slots == lane_req, row % slots, slots)
        fresh = jnp.where(own == lane_req + h * HALF, -1, slots)
        slot_of.append(jnp.where(own >= 0, fresh, cached))
    part_at = [me ^ s for s in range(parts)]
    group_at = [p // (parts // groups) for p in part_at]
    lane_part = lax.broadcasted_iota(jnp.int32, (1, span), 1) // part_span
    lane_group = jnp.zeros_like(lane_part)
    for s in range(parts):
        lane_group = jnp.where(lane_part == s, group_at[s], lane_group)
    scale = 1.0 / math.sqrt(HEAD)
    ones = jnp.ones((keys_in, HEAD), jnp.bfloat16)

    if True:
        step = pl.program_id(0)
        units = []
        for j in range(BATCH):
            start = j * STEP
            at = pl.ds(start, STEP)
            pieces = []
            for s in range(parts):
                lanes = pl.ds(pl.multiple_of(part_at[s] * width, width), width)
                q = base_ref[at, lanes].astype(jnp.float32)
                q = q + delta_refs[s][at, :].astype(jnp.float32)
                pieces += [q[:, k * HEAD : (k + 1) * HEAD] for k in range(per_part)]
            for h in range(STEP // HALF):
                slab = pl.ds(start + h * HALF, HALF)
                q = jnp.concatenate([p[h * HALF : (h + 1) * HALF] for p in pieces], axis=0)
                units.append((step * BATCH + j, at, h, slab, q.astype(jnp.bfloat16)))
        scores = []
        for _, at, h, slab, q in units:
            both = []
            for g in range(groups):
                lanes = slice(g * HEAD, (g + 1) * HEAD)
                keys = ck_ref[slab, :, lanes].reshape(HALF * slots, HEAD)
                keys = jnp.concatenate([keys, nk_ref[at, lanes]], axis=0)
                both.append(lax.dot_general(keys, q, NT, preferred_element_type=jnp.float32))
            score = both[0]
            for g in range(1, groups):
                score = jnp.where(lane_group == g, both[g], score)
            scores.append(score)
        probs = []
        for (i, at, h, slab, q), score in zip(units, scores):
            lens = len_ref[pl.ds(i * (STEP // HALF) + h, 1), :]
            score = jnp.where(slot_of[h] < lens, score, DEAD)
            top = jnp.max(score, axis=0, keepdims=True)
            exps = jnp.exp((score - top) * scale)
            total = jnp.sum(exps, axis=0, keepdims=True)
            probs.append((exps * (1.0 / total)).astype(jnp.bfloat16))
        mixed = []
        for (i, at, h, slab, q), prob in zip(units, probs):
            whole = []
            for g in range(groups):
                lanes = slice(g * HEAD, (g + 1) * HEAD)
                values = cv_ref[slab, :, lanes].reshape(HALF * slots, HEAD)
                values = jnp.concatenate([values, nv_ref[at, lanes]], axis=0)
                whole.append(
                    lax.dot_general(prob, values, TN, preferred_element_type=jnp.float32)
                )
            mixed.append(whole)
        for j in range(BATCH):
            at = units[2 * j][1]
            for s in range(parts):
                rows = slice(s * part_span, (s + 1) * part_span)
                halves = []
                for h in range(STEP // HALF):
                    whole = mixed[2 * j + h]
                    part = whole[0][rows]
                    for g in range(1, groups):
                        part = jnp.where(group_at[s] == g, whole[g][rows], part)
                    halves.append(part)
                out = [
                    jnp.concatenate([p[k * HALF : (k + 1) * HALF] for p in halves], axis=0)
                    for k in range(per_part)
                ]
                lanes = pl.ds(pl.multiple_of(part_at[s] * width, width), width)
                out_ref[at, lanes] = jnp.concatenate(out, axis=1).astype(jnp.bfloat16)


def attend(me, base, new_key, new_value, cache_keys, cache_values, lengths, deltas):
    requests, columns = base.shape
    kv = new_key.shape[1]
    slots = cache_keys.shape[1]
    lengths = jnp.tile(lengths.reshape(requests // HALF, HALF), (1, columns // HEAD))
    block = STEP * BATCH
    rows2 = lambda w: pl.BlockSpec((block, w), lambda i: (i, 0))
    rows3 = pl.BlockSpec((block, slots, kv), lambda i: (i, 0, 0))
    return pl.pallas_call(
        functools.partial(attend_kernel, len(deltas)),
        out_shape=jax.ShapeDtypeStruct((requests, columns), jnp.bfloat16),
        grid=(requests // block,),
        in_specs=[SMEM, whole(lengths), rows2(columns), rows2(kv), rows2(kv), rows3, rows3]
        + [rows2(d.shape[1]) for d in deltas],
        out_specs=rows2(columns),
        cost_estimate=pl.CostEstimate(
            flops=4 * requests * HALF * slots * columns,
            bytes_accessed=4 * requests * (columns + slots * kv),
            transcendentals=requests * slots * columns // 16,
        ),
    )(me, lengths, base, new_key, new_value, cache_keys, cache_values, *deltas)


def whole(array):
    return pl.BlockSpec(array.shape, lambda *_: (0,) * len(array.shape))


def factor_specs(weights, chunk):
    if chunk is None:
        return (1,), [whole(w) for w in weights]
    (weight,) = weights
    return (weight.shape[0] // chunk,), [
        pl.BlockSpec((chunk,) + weight.shape[1:], lambda i: (i, 0, 0))
    ]


def shrink_rows(ids, rows, weights, base, chunk):
    parts = rows.shape[0]
    grid, specs = factor_specs(weights, chunk)
    return pl.pallas_call(
        functools.partial(shrink_kernel, parts, len(weights), chunk is not None),
        out_shape=jax.ShapeDtypeStruct(base.shape, jnp.float32),
        grid=grid,
        in_specs=[SMEM, whole(rows), *specs, whole(base)],
        out_specs=whole(base),
        compiler_params=PARAMS,
    )(ids, rows, *weights, base)


def expand_rows(ids, me, rows, lows, weights, chunk, outputs):
    parts, requests, _ = rows.shape
    grid, specs = factor_specs(weights, chunk)
    out = jax.ShapeDtypeStruct((requests, outputs), jnp.bfloat16)
    held = (1, 8, LANES) if chunk is None else (parts, requests, outputs)
    return pl.pallas_call(
        functools.partial(expand_kernel, parts, len(weights), chunk is not None),
        out_shape=[out] * parts,
        grid=grid,
        in_specs=[SMEM, SMEM, whole(rows), *map(whole, lows), *specs],
        out_specs=[whole(out)] * parts,
        scratch_shapes=[
            pltpu.VMEM((parts, requests, LANES), jnp.float32),
            pltpu.VMEM(held, jnp.float32),
        ],
        compiler_params=PARAMS,
    )(ids, me, rows, *lows, *weights)


def per_device(
    hidden,
    adapter_ids,
    owner_map,
    shrink_factors,
    expand_factors,
    query_base,
    new_key,
    new_value,
    cache_keys,
    cache_values,
    lengths,
):
    reps, levels, sides, tp = (lax.axis_size(a) for a in ("rep", "level", "side", "tp"))
    requests, wide = hidden.shape
    rank = shrink_factors.shape[2]
    square = reps * sides
    features = wide // square
    outputs = query_base.shape[1] // square
    level, side = lax.axis_index("level"), lax.axis_index("side")
    me = lax.axis_index("rep") * sides + side

    def swap(a, s):
        pairs = [(c, c ^ s) for c in range(square)]
        return lax.ppermute(a, ("rep", "side"), pairs)

    def tied(a, *others):
        return lax.optimization_barrier((a, *others))[0]

    shrink = shrink_factors.swapaxes(1, 2)
    own, expand_own, other = pl.pallas_call(
        functools.partial(factor_kernel, square),
        out_shape=[
            jax.ShapeDtypeStruct((1, rank, w), jnp.bfloat16)
            for w in (features, outputs, features + outputs)
        ],
        in_specs=[SMEM, HBM, HBM],
        out_specs=[VMEM] * 3,
        scratch_shapes=[pltpu.SemaphoreType.DMA((4,))],
    )(me[None], shrink, expand_factors)
    other = swap(other, 1)
    rows = pl.pallas_call(
        functools.partial(row_kernel, square),
        out_shape=jax.ShapeDtypeStruct((square, requests, features + LANES), jnp.bfloat16),
        in_specs=[SMEM, VMEM, HBM],
        out_specs=VMEM,
        scratch_shapes=[pltpu.SemaphoreType.DMA((square,))],
    )(owner_map, adapter_ids.T, hidden)
    rows = tied(rows, other)
    rows = lax.all_to_all(rows, ("rep", "side"), split_axis=0, concat_axis=0, tiled=True)

    empty = jnp.zeros((square // 2 * requests, LANES), jnp.float32)
    order = jnp.arange(levels, dtype=jnp.int32)
    ids = (order[:, None] * sides + jnp.stack([side, side ^ 1])[None, :]).reshape(-1)
    other, expand_next = other[:, :, :features], other[:, :, features:]

    def gather_pairs(own, other):
        both = jnp.concatenate([own, other], axis=0)
        return lax.all_gather(both, "level", axis=0, tiled=True)

    expand = gather_pairs(expand_own, expand_next)
    if levels == 4:

        def gather(a):
            return [a] + [
                lax.ppermute(a, "level", [(i, i ^ k) for i in range(levels)])
                for k in range(1, levels)
            ]

        own_ids = (level ^ order) * sides + side
        next_ids = (level ^ order) * sides + (side ^ 1)
        own, other = gather(own), gather(other)
        partial = shrink_rows(own_ids, rows, own, empty, None)
        partial, expand = lax.optimization_barrier((partial, expand))
        partial = shrink_rows(next_ids, rows, other, partial, None)
        chunk = None
    else:
        chunk = 4
        partial = shrink_rows(ids, rows, [gather_pairs(own, other)], empty, chunk)

    for c in range(1, tp):
        partial = partial + lax.ppermute(partial, "tp", [(t, t ^ c) for t in range(tp)])
    partial = partial.astype(jnp.bfloat16)
    lows = [partial] + [swap(partial, s) for s in range(1, square)]
    deltas = expand_rows(ids, me[None], rows, lows, [expand], chunk, outputs)
    deltas = [deltas[0]] + [swap(deltas[s], s) for s in range(1, square)]
    return attend(
        me[None],
        query_base,
        new_key,
        new_value,
        cache_keys,
        cache_values,
        lengths,
        deltas,
    )


def solution(mesh):
    reps, pool, tp = (mesh.shape[a] for a in ("rep", "pool", "tp"))
    finer = Mesh(mesh.devices.reshape(reps, pool // 2, 2, tp), ("rep", "level", "side", "tp"))
    pooled = ("level", "side")
    requests = ("rep", "level", "side")
    in_specs = (
        P(requests, "tp"),
        P(requests, None),
        P(),
        P(pooled, "tp", None),
        P(pooled, None, "tp"),
        P(requests, "tp"),
        P(requests, "tp"),
        P(requests, "tp"),
        P(requests, None, "tp"),
        P(requests, None, "tp"),
        P(requests),
    )
    return jax.shard_map(
        per_device, mesh=finer, in_specs=in_specs, out_specs=P(requests, "tp"), check_vma=False
    )
```

```python
import functools
import math

import jax
import jax.numpy as jnp
from jax import lax
from jax.experimental import pallas as pl
from jax.experimental.pallas import tpu as pltpu
from jax.sharding import Mesh
from jax.sharding import PartitionSpec as P

HEAD = 128
LANES = 128
STEP = 16
HALF = 8
BATCH = 2
DEAD = -1e30
VMEM = pl.BlockSpec(memory_space=pltpu.VMEM)
SMEM = pl.BlockSpec(memory_space=pltpu.SMEM)
ANY = pl.BlockSpec(memory_space=pl.ANY)
HBM = pl.BlockSpec(memory_space=pltpu.HBM)
PARAMS = pltpu.CompilerParams(vmem_limit_bytes=12 * 1024 * 1024)
NT = (((1,), (1,)), ((), ()))
TN = (((0,), (0,)), ((), ()))


def columns(at, width):
    return pl.ds(pl.multiple_of(at * width, width), width)


def cut_kernel(parts, me_ref, map_ref, ids_ref, hidden_ref, shrink_ref, expand_ref, *refs):
    own_ref, next_ref, rows_ref, sems = refs
    requests, wide = hidden_ref.shape
    features, outputs = wide // parts, expand_ref.shape[2] // parts
    me = me_ref[0]
    moves = []
    for at, ref in ((me ^ 1, next_ref), (me, own_ref)):
        moves.append((shrink_ref.at[:, :, columns(at, features)], ref.at[:, :, :features]))
        moves.append((expand_ref.at[:, :, columns(at, outputs)], ref.at[:, :, features:]))
    for s in range(parts):
        at = slice(s * features, (s + 1) * features)
        moves.append((hidden_ref.at[:, at], rows_ref.at[s, :, :features]))
    copies = [pltpu.make_async_copy(src, dst, sems.at[k]) for k, (src, dst) in enumerate(moves)]
    for copy in copies:
        copy.start()
    ids = ids_ref[...]

    def look(k, found):
        return jnp.where(ids == k, map_ref[k], found)

    owners = lax.fori_loop(0, map_ref.shape[0], look, jnp.zeros_like(ids))
    owners = jnp.broadcast_to(owners.astype(jnp.float32), (LANES, requests)).T
    for s in range(parts):
        rows_ref[s, :, features:] = owners.astype(jnp.bfloat16)
    for copy in copies:
        copy.wait()


def owner_mask(owners, ids, rank):
    lane = lax.broadcasted_iota(jnp.int32, (1, len(ids) * rank), 1) // rank
    named = jnp.full_like(lane, -1)
    for k, owner in enumerate(ids):
        named = jnp.where(lane == k, owner, named)
    wide = jnp.concatenate([owners] * (len(ids) * rank // LANES), axis=1)
    return wide == named


def row_owners(ref, features):
    return ref[:, features:].astype(jnp.float32).astype(jnp.int32)


def stacked(refs, lanes):
    blocks = [r[k, :, lanes] for r in refs for k in range(r.shape[0])]
    return jnp.concatenate(blocks, axis=0)


def shrink_kernel(parts, blocks, gridded, ids_ref, *refs):
    rows_ref, weight_refs, base_ref, out_ref = refs[0], refs[1 : 1 + blocks], refs[1 + blocks], refs[-1]
    row_refs = [rows_ref.at[s] for s in range(parts)]
    rank = weight_refs[0].shape[1]
    requests, features = rows_ref.shape[1], rows_ref.shape[2] - LANES
    count = sum(r.shape[0] for r in weight_refs)
    step = pl.program_id(0) if gridded else 0
    ids = [ids_ref[step * count + k] for k in range(count)]
    weight = stacked(weight_refs, slice(0, features))
    low = lax.broadcasted_iota(jnp.int32, (requests, LANES), 1) < rank
    folded = []
    for ref in row_refs:
        sums = lax.dot_general(
            ref[:, :features], weight, NT, preferred_element_type=jnp.float32
        )
        sums = jnp.where(owner_mask(row_owners(ref, features), ids, rank), sums, 0.0)
        total = sums[:, :LANES]
        for k in range(1, count * rank // LANES):
            total = total + sums[:, k * LANES : (k + 1) * LANES]
        folded.append(total + pltpu.roll(total, rank, 1))
    if gridded:

        @pl.when(step == 0)
        def _():
            out_ref[...] = base_ref[...]

    else:
        out_ref[...] = base_ref[...]
    half = parts // 2
    for s in range(half):
        rows = pl.ds(s * requests, requests)
        out_ref[rows, :] += jnp.where(low, folded[s], folded[s + half])


def expand_kernel(parts, blocks, gridded, ids_ref, me_ref, rows_ref, *refs):
    low_refs, weight_refs, out_refs, (held_ref, total_ref) = (
        refs[:parts],
        refs[parts : parts + blocks],
        refs[parts + blocks : 2 * parts + blocks],
        refs[-2:],
    )
    me = me_ref[0]
    rank, outputs = weight_refs[0].shape[1], out_refs[0].shape[1]
    requests, features = rows_ref.shape[1], rows_ref.shape[2] - LANES
    count = sum(r.shape[0] for r in weight_refs)
    step = pl.program_id(0) if gridded else 0
    last = pl.num_programs(0) - 1 if gridded else 0
    ids = [ids_ref[step * count + k] for k in range(count)]
    weight = stacked(weight_refs, slice(features, features + outputs))
    half = parts // 2
    low = lax.broadcasted_iota(jnp.int32, (requests, LANES), 1) < rank
    low_sum = low_refs[0][...].astype(jnp.float32)
    for ref in low_refs[1:]:
        low_sum = low_sum + ref[...].astype(jnp.float32)
    for s in range(half):
        straight = low_sum[s * requests : (s + 1) * requests]
        turned = pltpu.roll(straight, rank, 1)
        held_ref[s] = jnp.where(low, straight, turned)
        held_ref[s + half] = jnp.where(low, turned, straight)
    for s in range(parts):
        both = held_ref[me ^ s]
        wide = jnp.concatenate([both] * (count * rank // LANES), axis=1)
        mask = owner_mask(row_owners(rows_ref.at[me ^ s], features), ids, rank)
        wide = jnp.where(mask, wide, 0.0).astype(jnp.bfloat16)
        product = jnp.dot(wide, weight, preferred_element_type=jnp.float32)
        if not gridded:
            out_refs[s][...] = product.astype(jnp.bfloat16)
        else:

            @pl.when(step == 0)
            def _():
                total_ref[s] = product

            @pl.when(step > 0)
            def _():
                total_ref[s] += product

            @pl.when(step == last)
            def _():
                out_refs[s][...] = total_ref[s].astype(jnp.bfloat16)


def attend_kernel(parts, me_ref, len_ref, *refs):
    inputs = 5 + parts
    sources, out_hbm = refs[:inputs], refs[inputs]
    held, (out_ref, sems, out_sems) = refs[inputs + 1 : 2 * inputs + 1], refs[2 * inputs + 1 :]
    base_ref, nk_ref, nv_ref, ck_ref, cv_ref, *delta_refs = held
    me = me_ref[0]
    block = STEP * BATCH
    steps = base_ref.shape[0] // block
    arrivals = []
    for step in range(steps):
        at = pl.ds(step * block, block)
        arrivals.append(
            [
                pltpu.make_async_copy(src.at[at], dst.at[at], sems.at[step, k])
                for k, (src, dst) in enumerate(zip(sources, held))
            ]
        )
        for copy in arrivals[-1]:
            copy.start()
    requests, columns = base_ref.shape
    width = columns // parts
    groups = nk_ref.shape[1] // HEAD
    slots = ck_ref.shape[1]
    heads = columns // HEAD
    per_part = width // HEAD
    span = heads * HALF
    part_span = per_part * HALF
    keys_in = HALF * slots + STEP
    row = lax.broadcasted_iota(jnp.int32, (keys_in, span), 0)
    lane_req = lax.broadcasted_iota(jnp.int32, (keys_in, span), 1) % HALF
    own = row - HALF * slots
    slot_of = []
    for h in range(STEP // HALF):
        cached = jnp.where(row // slots == lane_req, row % slots, slots)
        fresh = jnp.where(own == lane_req + h * HALF, -1, slots)
        slot_of.append(jnp.where(own >= 0, fresh, cached))
    part_at = [me ^ s for s in range(parts)]
    group_at = [p // (parts // groups) for p in part_at]
    lane_part = lax.broadcasted_iota(jnp.int32, (1, span), 1) // part_span
    lane_group = jnp.zeros_like(lane_part)
    for s in range(parts):
        lane_group = jnp.where(lane_part == s, group_at[s], lane_group)
    scale = 1.0 / math.sqrt(HEAD)
    ones = jnp.ones((keys_in, HEAD), jnp.bfloat16)

    departures = []
    for step in range(steps):
        for copy in arrivals[step]:
            copy.wait()
        units = []
        for j in range(BATCH):
            start = step * block + j * STEP
            at = pl.ds(start, STEP)
            pieces = []
            for s in range(parts):
                lanes = pl.ds(pl.multiple_of(part_at[s] * width, width), width)
                q = base_ref[at, lanes].astype(jnp.float32)
                q = q + delta_refs[s][at, :].astype(jnp.float32)
                pieces += [q[:, k * HEAD : (k + 1) * HEAD] for k in range(per_part)]
            for h in range(STEP // HALF):
                slab = pl.ds(start + h * HALF, HALF)
                q = jnp.concatenate([p[h * HALF : (h + 1) * HALF] for p in pieces], axis=0)
                units.append((step * BATCH + j, at, h, slab, q.astype(jnp.bfloat16)))
        scores = []
        for _, at, h, slab, q in units:
            both = []
            for g in range(groups):
                lanes = slice(g * HEAD, (g + 1) * HEAD)
                keys = ck_ref[slab, :, lanes].reshape(HALF * slots, HEAD)
                keys = jnp.concatenate([keys, nk_ref[at, lanes]], axis=0)
                both.append(lax.dot_general(keys, q, NT, preferred_element_type=jnp.float32))
            score = both[0]
            for g in range(1, groups):
                score = jnp.where(lane_group == g, both[g], score)
            scores.append(score)
        probs = []
        for (i, at, h, slab, q), score in zip(units, scores):
            lens = len_ref[pl.ds(i * (STEP // HALF) + h, 1), :]
            score = jnp.where(slot_of[h] < lens, score, DEAD)
            top = jnp.max(score, axis=0, keepdims=True)
            exps = jnp.exp((score - top) * scale)
            total = jnp.sum(exps, axis=0, keepdims=True)
            probs.append((exps * (1.0 / total)).astype(jnp.bfloat16))
        mixed = []
        for (i, at, h, slab, q), prob in zip(units, probs):
            whole = []
            for g in range(groups):
                lanes = slice(g * HEAD, (g + 1) * HEAD)
                values = cv_ref[slab, :, lanes].reshape(HALF * slots, HEAD)
                values = jnp.concatenate([values, nv_ref[at, lanes]], axis=0)
                whole.append(
                    lax.dot_general(prob, values, TN, preferred_element_type=jnp.float32)
                )
            mixed.append(whole)
        for j in range(BATCH):
            at = units[2 * j][1]
            for s in range(parts):
                rows = slice(s * part_span, (s + 1) * part_span)
                halves = []
                for h in range(STEP // HALF):
                    whole = mixed[2 * j + h]
                    part = whole[0][rows]
                    for g in range(1, groups):
                        part = jnp.where(group_at[s] == g, whole[g][rows], part)
                    halves.append(part)
                out = [
                    jnp.concatenate([p[k * HALF : (k + 1) * HALF] for p in halves], axis=0)
                    for k in range(per_part)
                ]
                lanes = pl.ds(pl.multiple_of(part_at[s] * width, width), width)
                out_ref[at, lanes] = jnp.concatenate(out, axis=1).astype(jnp.bfloat16)
        at = pl.ds(step * block, block)
        copy = pltpu.make_async_copy(out_ref.at[at], out_hbm.at[at], out_sems.at[step])
        copy.start()
        departures.append(copy)
    for copy in departures:
        copy.wait()


def attend(me, base, new_key, new_value, cache_keys, cache_values, lengths, deltas):
    requests, columns = base.shape
    kv = new_key.shape[1]
    slots = cache_keys.shape[1]
    lengths = jnp.tile(lengths.reshape(requests // HALF, HALF), (1, columns // HEAD))
    steps = requests // (STEP * BATCH)
    arrays = [base, new_key, new_value, cache_keys, cache_values, *deltas]
    return pl.pallas_call(
        functools.partial(attend_kernel, len(deltas)),
        out_shape=jax.ShapeDtypeStruct((requests, columns), jnp.bfloat16),
        in_specs=[SMEM, VMEM] + [ANY] * len(arrays),
        out_specs=ANY,
        scratch_shapes=[pltpu.VMEM(a.shape, jnp.bfloat16) for a in arrays]
        + [
            pltpu.VMEM((requests, columns), jnp.bfloat16),
            pltpu.SemaphoreType.DMA((steps, len(arrays))),
            pltpu.SemaphoreType.DMA((steps,)),
        ],
        cost_estimate=pl.CostEstimate(
            flops=4 * requests * HALF * slots * columns,
            bytes_accessed=4 * requests * (columns + slots * kv),
            transcendentals=requests * slots * columns // 16,
        ),
    )(me, lengths, *arrays)


def whole(array):
    return pl.BlockSpec(array.shape, lambda *_: (0,) * len(array.shape))


def factor_specs(weights, chunk):
    if chunk is None:
        return (1,), [whole(w) for w in weights]
    (weight,) = weights
    return (weight.shape[0] // chunk,), [
        pl.BlockSpec((chunk,) + weight.shape[1:], lambda i: (i, 0, 0))
    ]


def shrink_rows(ids, rows, weights, base, chunk):
    parts = rows.shape[0]
    grid, specs = factor_specs(weights, chunk)
    return pl.pallas_call(
        functools.partial(shrink_kernel, parts, len(weights), chunk is not None),
        out_shape=jax.ShapeDtypeStruct(base.shape, jnp.float32),
        grid=grid,
        in_specs=[SMEM, whole(rows), *specs, whole(base)],
        out_specs=whole(base),
        compiler_params=PARAMS,
    )(ids, rows, *weights, base)


def expand_rows(ids, me, rows, lows, weights, chunk, outputs):
    parts, requests, _ = rows.shape
    grid, specs = factor_specs(weights, chunk)
    out = jax.ShapeDtypeStruct((requests, outputs), jnp.bfloat16)
    held = (1, 8, LANES) if chunk is None else (parts, requests, outputs)
    return pl.pallas_call(
        functools.partial(expand_kernel, parts, len(weights), chunk is not None),
        out_shape=[out] * parts,
        grid=grid,
        in_specs=[SMEM, SMEM, whole(rows), *map(whole, lows), *specs],
        out_specs=[whole(out)] * parts,
        scratch_shapes=[
            pltpu.VMEM((parts, requests, LANES), jnp.float32),
            pltpu.VMEM(held, jnp.float32),
        ],
        compiler_params=PARAMS,
    )(ids, me, rows, *lows, *weights)


def per_device(
    hidden,
    adapter_ids,
    owner_map,
    shrink_factors,
    expand_factors,
    query_base,
    new_key,
    new_value,
    cache_keys,
    cache_values,
    lengths,
):
    reps, levels, sides, tp = (lax.axis_size(a) for a in ("rep", "level", "side", "tp"))
    requests, wide = hidden.shape
    rank = shrink_factors.shape[2]
    square = reps * sides
    features = wide // square
    outputs = query_base.shape[1] // square
    level, side = lax.axis_index("level"), lax.axis_index("side")
    me = lax.axis_index("rep") * sides + side

    def swap(a, s):
        pairs = [(c, c ^ s) for c in range(square)]
        return lax.ppermute(a, ("rep", "side"), pairs)

    def tied(a, *others):
        return lax.optimization_barrier((a, *others))[0]

    shrink = shrink_factors.swapaxes(1, 2)
    block = jax.ShapeDtypeStruct((1, rank, features + outputs), jnp.bfloat16)
    own, other, rows = pl.pallas_call(
        functools.partial(cut_kernel, square),
        out_shape=[
            block,
            block,
            jax.ShapeDtypeStruct((square, requests, features + LANES), jnp.bfloat16),
        ],
        in_specs=[SMEM, SMEM, VMEM, HBM, HBM, HBM],
        out_specs=[VMEM] * 3,
        scratch_shapes=[pltpu.SemaphoreType.DMA((square + 4,))],
    )(me[None], owner_map, adapter_ids.T, hidden, shrink, expand_factors)
    own = lax.all_gather(own, "level", axis=0, tiled=True)
    other = swap(other, 1)
    rows = tied(rows, other)
    rows = lax.all_to_all(rows, ("rep", "side"), split_axis=0, concat_axis=0, tiled=True)

    order = jnp.arange(levels, dtype=jnp.int32)
    own_ids = order * sides + side
    partial = jnp.zeros((square // 2 * requests, LANES), jnp.float32)
    if levels == 4:
        other = [other] + [
            lax.ppermute(other, "level", [(i, i ^ k) for i in range(levels)])
            for k in range(1, levels)
        ]
        other_ids = (level ^ order) * sides + (side ^ 1)
        chunk = None
        partial = shrink_rows(own_ids, rows, [own], partial, chunk)
        partial = shrink_rows(other_ids, rows, other, partial, chunk)
        factors, ids = [own] + other, jnp.concatenate([own_ids, other_ids])
    else:
        other = lax.all_gather(other, "level", axis=0, tiled=True)
        factors = [jnp.concatenate([own, other], axis=0)]
        ids = jnp.concatenate([own_ids, order * sides + (side ^ 1)])
        chunk = 4
        partial = shrink_rows(ids, rows, factors, partial, chunk)

    for c in range(1, tp):
        partial = partial + lax.ppermute(partial, "tp", [(t, t ^ c) for t in range(tp)])
    partial = partial.astype(jnp.bfloat16)
    lows = [partial] + [swap(partial, s) for s in range(1, square)]
    deltas = expand_rows(ids, me[None], rows, lows, factors, chunk, outputs)
    deltas = [deltas[0]] + [swap(deltas[s], s) for s in range(1, square)]
    return attend(
        me[None],
        query_base,
        new_key,
        new_value,
        cache_keys,
        cache_values,
        lengths,
        deltas,
    )


def solution(mesh):
    reps, pool, tp = (mesh.shape[a] for a in ("rep", "pool", "tp"))
    finer = Mesh(mesh.devices.reshape(reps, pool // 2, 2, tp), ("rep", "level", "side", "tp"))
    pooled = ("level", "side")
    requests = ("rep", "level", "side")
    in_specs = (
        P(requests, "tp"),
        P(requests, None),
        P(),
        P(pooled, "tp", None),
        P(pooled, None, "tp"),
        P(requests, "tp"),
        P(requests, "tp"),
        P(requests, "tp"),
        P(requests, None, "tp"),
        P(requests, None, "tp"),
        P(requests),
    )
    return jax.shard_map(
        per_device, mesh=finer, in_specs=in_specs, out_specs=P(requests, "tp"), check_vma=False
    )
```

```python
import functools
import math

import jax
import jax.numpy as jnp
from jax import lax
from jax.experimental import pallas as pl
from jax.experimental.pallas import tpu as pltpu
from jax.sharding import Mesh
from jax.sharding import PartitionSpec as P

HEAD = 128
LANES = 128
STEP = 16
HALF = 8
BATCH = 2
DEAD = -1e30
VMEM = pl.BlockSpec(memory_space=pltpu.VMEM)
SMEM = pl.BlockSpec(memory_space=pltpu.SMEM)
HBM = pl.BlockSpec(memory_space=pltpu.HBM)
PARAMS = pltpu.CompilerParams(vmem_limit_bytes=12 * 1024 * 1024)
NT = (((1,), (1,)), ((), ()))
TN = (((0,), (0,)), ((), ()))


def beside(us):
    return pl.CostEstimate(flops=0, bytes_accessed=us * 3_690_000, transcendentals=0)


def columns(at, width):
    return pl.ds(pl.multiple_of(at * width, width), width)


def factor_kernel(parts, me_ref, shrink_ref, expand_ref, own_ref, next_ref, sems):
    features, outputs = shrink_ref.shape[2] // parts, expand_ref.shape[2] // parts
    me = me_ref[0]
    moves = []
    for at, ref in ((me ^ 1, next_ref), (me, own_ref)):
        moves.append((shrink_ref.at[:, :, columns(at, features)], ref.at[:, :, :features]))
        moves.append((expand_ref.at[:, :, columns(at, outputs)], ref.at[:, :, features:]))
    copies = [pltpu.make_async_copy(src, dst, sems.at[k]) for k, (src, dst) in enumerate(moves)]
    for copy in copies:
        copy.start()
    for copy in copies:
        copy.wait()


def row_kernel(parts, map_ref, ids_ref, hidden_ref, rows_ref, sems):
    requests, wide = hidden_ref.shape
    features = wide // parts
    copies = []
    for s in range(parts):
        at = slice(s * features, (s + 1) * features)
        dst = rows_ref.at[s, :, :features]
        copies.append(pltpu.make_async_copy(hidden_ref.at[:, at], dst, sems.at[s]))
    for copy in copies:
        copy.start()
    ids = ids_ref[...]

    def look(k, found):
        return jnp.where(ids == k, map_ref[k], found)

    owners = lax.fori_loop(0, map_ref.shape[0], look, jnp.zeros_like(ids))
    owners = jnp.broadcast_to(owners.astype(jnp.float32), (LANES, requests)).T
    for s in range(parts):
        rows_ref[s, :, features:] = owners.astype(jnp.bfloat16)
    for copy in copies:
        copy.wait()


def owner_mask(owners, ids, rank):
    lane = lax.broadcasted_iota(jnp.int32, (1, len(ids) * rank), 1) // rank
    named = jnp.full_like(lane, -1)
    for k, owner in enumerate(ids):
        named = jnp.where(lane == k, owner, named)
    wide = jnp.concatenate([owners] * (len(ids) * rank // LANES), axis=1)
    return wide == named


def row_owners(ref, features):
    return ref[:, features:].astype(jnp.float32).astype(jnp.int32)


def stacked(refs, lanes):
    blocks = [r[k, :, lanes] for r in refs for k in range(r.shape[0])]
    return jnp.concatenate(blocks, axis=0)


def shrink_kernel(parts, blocks, gridded, ids_ref, *refs):
    rows_ref, weight_refs, base_ref, out_ref = refs[0], refs[1 : 1 + blocks], refs[1 + blocks], refs[-1]
    row_refs = [rows_ref.at[s] for s in range(parts)]
    rank = weight_refs[0].shape[1]
    requests, features = rows_ref.shape[1], rows_ref.shape[2] - LANES
    count = sum(r.shape[0] for r in weight_refs)
    step = pl.program_id(0) if gridded else 0
    ids = [ids_ref[step * count + k] for k in range(count)]
    weight = stacked(weight_refs, slice(0, features))
    low = lax.broadcasted_iota(jnp.int32, (requests, LANES), 1) < rank
    folded = []
    for ref in row_refs:
        sums = lax.dot_general(
            ref[:, :features], weight, NT, preferred_element_type=jnp.float32
        )
        sums = jnp.where(owner_mask(row_owners(ref, features), ids, rank), sums, 0.0)
        total = sums[:, :LANES]
        for k in range(1, count * rank // LANES):
            total = total + sums[:, k * LANES : (k + 1) * LANES]
        folded.append(total + pltpu.roll(total, rank, 1))
    if gridded:

        @pl.when(step == 0)
        def _():
            out_ref[...] = base_ref[...]

    else:
        out_ref[...] = base_ref[...]
    half = parts // 2
    for s in range(half):
        rows = pl.ds(s * requests, requests)
        out_ref[rows, :] += jnp.where(low, folded[s], folded[s + half])


def expand_kernel(parts, blocks, gridded, ids_ref, me_ref, rows_ref, *refs):
    low_refs, weight_refs, out_refs, (held_ref, total_ref) = (
        refs[:parts],
        refs[parts : parts + blocks],
        refs[parts + blocks : 2 * parts + blocks],
        refs[-2:],
    )
    me = me_ref[0]
    rank, outputs = weight_refs[0].shape[1], out_refs[0].shape[1]
    requests, features = rows_ref.shape[1], rows_ref.shape[2] - LANES
    count = sum(r.shape[0] for r in weight_refs)
    step = pl.program_id(0) if gridded else 0
    last = pl.num_programs(0) - 1 if gridded else 0
    ids = [ids_ref[step * count + k] for k in range(count)]
    weight = stacked(weight_refs, slice(features, features + outputs))
    half = parts // 2
    low = lax.broadcasted_iota(jnp.int32, (requests, LANES), 1) < rank
    low_sum = low_refs[0][...].astype(jnp.float32)
    for ref in low_refs[1:]:
        low_sum = low_sum + ref[...].astype(jnp.float32)
    for s in range(half):
        straight = low_sum[s * requests : (s + 1) * requests]
        turned = pltpu.roll(straight, rank, 1)
        held_ref[s] = jnp.where(low, straight, turned)
        held_ref[s + half] = jnp.where(low, turned, straight)
    for s in range(parts):
        both = held_ref[me ^ s]
        wide = jnp.concatenate([both] * (count * rank // LANES), axis=1)
        mask = owner_mask(row_owners(rows_ref.at[me ^ s], features), ids, rank)
        wide = jnp.where(mask, wide, 0.0).astype(jnp.bfloat16)
        product = jnp.dot(wide, weight, preferred_element_type=jnp.float32)
        if not gridded:
            out_refs[s][...] = product.astype(jnp.bfloat16)
        else:

            @pl.when(step == 0)
            def _():
                total_ref[s] = product

            @pl.when(step > 0)
            def _():
                total_ref[s] += product

            @pl.when(step == last)
            def _():
                out_refs[s][...] = total_ref[s].astype(jnp.bfloat16)


def attend_kernel(parts, me_ref, len_ref, *refs):
    base_ref, nk_ref, nv_ref, ck_ref, cv_ref, *delta_refs, out_ref = refs
    me = me_ref[0]
    block = STEP * BATCH
    steps = base_ref.shape[0] // block
    requests, columns = base_ref.shape
    width = columns // parts
    groups = nk_ref.shape[1] // HEAD
    slots = ck_ref.shape[1]
    heads = columns // HEAD
    per_part = width // HEAD
    span = heads * HALF
    part_span = per_part * HALF
    keys_in = HALF * slots + STEP
    row = lax.broadcasted_iota(jnp.int32, (keys_in, span), 0)
    lane_req = lax.broadcasted_iota(jnp.int32, (keys_in, span), 1) % HALF
    own = row - HALF * slots
    slot_of = []
    for h in range(STEP // HALF):
        cached = jnp.where(row // slots == lane_req, row % slots, slots)
        fresh = jnp.where(own == lane_req + h * HALF, -1, slots)
        slot_of.append(jnp.where(own >= 0, fresh, cached))
    part_at = [me ^ s for s in range(parts)]
    group_at = [p // (parts // groups) for p in part_at]
    lane_part = lax.broadcasted_iota(jnp.int32, (1, span), 1) // part_span
    lane_group = jnp.zeros_like(lane_part)
    for s in range(parts):
        lane_group = jnp.where(lane_part == s, group_at[s], lane_group)
    scale = 1.0 / math.sqrt(HEAD)
    ones = jnp.ones((keys_in, HEAD), jnp.bfloat16)

    for step in range(steps):
        units = []
        for j in range(BATCH):
            start = step * block + j * STEP
            at = pl.ds(start, STEP)
            pieces = []
            for s in range(parts):
                lanes = pl.ds(pl.multiple_of(part_at[s] * width, width), width)
                q = base_ref[at, lanes].astype(jnp.float32)
                q = q + delta_refs[s][at, :].astype(jnp.float32)
                pieces += [q[:, k * HEAD : (k + 1) * HEAD] for k in range(per_part)]
            for h in range(STEP // HALF):
                slab = pl.ds(start + h * HALF, HALF)
                q = jnp.concatenate([p[h * HALF : (h + 1) * HALF] for p in pieces], axis=0)
                units.append((step * BATCH + j, at, h, slab, q.astype(jnp.bfloat16)))
        scores = []
        for _, at, h, slab, q in units:
            both = []
            for g in range(groups):
                lanes = slice(g * HEAD, (g + 1) * HEAD)
                keys = ck_ref[slab, :, lanes].reshape(HALF * slots, HEAD)
                keys = jnp.concatenate([keys, nk_ref[at, lanes]], axis=0)
                both.append(lax.dot_general(keys, q, NT, preferred_element_type=jnp.float32))
            score = both[0]
            for g in range(1, groups):
                score = jnp.where(lane_group == g, both[g], score)
            scores.append(score)
        probs = []
        for (i, at, h, slab, q), score in zip(units, scores):
            lens = len_ref[pl.ds(i * (STEP // HALF) + h, 1), :]
            score = jnp.where(slot_of[h] < lens, score, DEAD)
            top = jnp.max(score, axis=0, keepdims=True)
            exps = jnp.exp((score - top) * scale)
            total = jnp.sum(exps, axis=0, keepdims=True)
            probs.append((exps * (1.0 / total)).astype(jnp.bfloat16))
        mixed = []
        for (i, at, h, slab, q), prob in zip(units, probs):
            whole = []
            for g in range(groups):
                lanes = slice(g * HEAD, (g + 1) * HEAD)
                values = cv_ref[slab, :, lanes].reshape(HALF * slots, HEAD)
                values = jnp.concatenate([values, nv_ref[at, lanes]], axis=0)
                whole.append(
                    lax.dot_general(prob, values, TN, preferred_element_type=jnp.float32)
                )
            mixed.append(whole)
        for j in range(BATCH):
            at = units[2 * j][1]
            for s in range(parts):
                rows = slice(s * part_span, (s + 1) * part_span)
                halves = []
                for h in range(STEP // HALF):
                    whole = mixed[2 * j + h]
                    part = whole[0][rows]
                    for g in range(1, groups):
                        part = jnp.where(group_at[s] == g, whole[g][rows], part)
                    halves.append(part)
                out = [
                    jnp.concatenate([p[k * HALF : (k + 1) * HALF] for p in halves], axis=0)
                    for k in range(per_part)
                ]
                lanes = pl.ds(pl.multiple_of(part_at[s] * width, width), width)
                out_ref[at, lanes] = jnp.concatenate(out, axis=1).astype(jnp.bfloat16)


def attend(me, base, new_key, new_value, cache_keys, cache_values, lengths, deltas):
    requests, columns = base.shape
    kv = new_key.shape[1]
    slots = cache_keys.shape[1]
    lengths = jnp.tile(lengths.reshape(requests // HALF, HALF), (1, columns // HEAD))
    arrays = [base, new_key, new_value, cache_keys, cache_values, *deltas]
    return pl.pallas_call(
        functools.partial(attend_kernel, len(deltas)),
        out_shape=jax.ShapeDtypeStruct((requests, columns), jnp.bfloat16),
        in_specs=[SMEM] + [VMEM] * (1 + len(arrays)),
        out_specs=VMEM,
        compiler_params=PARAMS,
        cost_estimate=pl.CostEstimate(
            flops=4 * requests * HALF * slots * columns,
            bytes_accessed=4 * requests * (columns + slots * kv),
            transcendentals=requests * slots * columns // 16,
        ),
    )(me, lengths, *arrays)


def whole(array):
    return pl.BlockSpec(array.shape, lambda *_: (0,) * len(array.shape))


def factor_specs(weights, chunk):
    if chunk is None:
        return (1,), [whole(w) for w in weights]
    (weight,) = weights
    return (weight.shape[0] // chunk,), [
        pl.BlockSpec((chunk,) + weight.shape[1:], lambda i: (i, 0, 0))
    ]


def shrink_rows(ids, rows, weights, base, chunk):
    parts = rows.shape[0]
    grid, specs = factor_specs(weights, chunk)
    return pl.pallas_call(
        functools.partial(shrink_kernel, parts, len(weights), chunk is not None),
        out_shape=jax.ShapeDtypeStruct(base.shape, jnp.float32),
        grid=grid,
        in_specs=[SMEM, whole(rows), *specs, whole(base)],
        out_specs=whole(base),
        compiler_params=PARAMS,
        cost_estimate=beside(10),
    )(ids, rows, *weights, base)


def expand_rows(ids, me, rows, lows, weights, chunk, outputs):
    parts, requests, _ = rows.shape
    grid, specs = factor_specs(weights, chunk)
    out = jax.ShapeDtypeStruct((requests, outputs), jnp.bfloat16)
    held = (1, 8, LANES) if chunk is None else (parts, requests, outputs)
    return pl.pallas_call(
        functools.partial(expand_kernel, parts, len(weights), chunk is not None),
        out_shape=[out] * parts,
        grid=grid,
        in_specs=[SMEM, SMEM, whole(rows), *map(whole, lows), *specs],
        out_specs=[whole(out)] * parts,
        scratch_shapes=[
            pltpu.VMEM((parts, requests, LANES), jnp.float32),
            pltpu.VMEM(held, jnp.float32),
        ],
        compiler_params=PARAMS,
        cost_estimate=beside(20),
    )(ids, me, rows, *lows, *weights)


def per_device(
    hidden,
    adapter_ids,
    owner_map,
    shrink_factors,
    expand_factors,
    query_base,
    new_key,
    new_value,
    cache_keys,
    cache_values,
    lengths,
):
    reps, levels, sides, tp = (lax.axis_size(a) for a in ("rep", "level", "side", "tp"))
    requests, wide = hidden.shape
    rank = shrink_factors.shape[2]
    square = reps * sides
    features = wide // square
    outputs = query_base.shape[1] // square
    level, side = lax.axis_index("level"), lax.axis_index("side")
    me = lax.axis_index("rep") * sides + side

    def swap(a, s):
        pairs = [(c, c ^ s) for c in range(square)]
        return lax.ppermute(a, ("rep", "side"), pairs)

    def tied(a, *others):
        return lax.optimization_barrier((a, *others))[0]

    shrink = shrink_factors.swapaxes(1, 2)
    block = jax.ShapeDtypeStruct((1, rank, features + outputs), jnp.bfloat16)
    own, other = pl.pallas_call(
        functools.partial(factor_kernel, square),
        out_shape=[block, block],
        in_specs=[SMEM, HBM, HBM],
        out_specs=[VMEM] * 2,
        scratch_shapes=[pltpu.SemaphoreType.DMA((4,))],
    )(me[None], shrink, expand_factors)
    own = lax.all_gather(own, "level", axis=0, tiled=True)
    rows = pl.pallas_call(
        functools.partial(row_kernel, square),
        out_shape=jax.ShapeDtypeStruct((square, requests, features + LANES), jnp.bfloat16),
        in_specs=[SMEM, VMEM, HBM],
        out_specs=VMEM,
        scratch_shapes=[pltpu.SemaphoreType.DMA((square,))],
        cost_estimate=beside(100),
    )(owner_map, adapter_ids.T, hidden)
    other = swap(other, 1)
    rows = tied(rows, other)
    rows = lax.all_to_all(rows, ("rep", "side"), split_axis=0, concat_axis=0, tiled=True)

    order = jnp.arange(levels, dtype=jnp.int32)
    own_ids = order * sides + side
    partial = jnp.zeros((square // 2 * requests, LANES), jnp.float32)
    if levels == 4:
        other = [other] + [
            lax.ppermute(other, "level", [(i, i ^ k) for i in range(levels)])
            for k in range(1, levels)
        ]
        other_ids = (level ^ order) * sides + (side ^ 1)
        chunk = None
        partial = shrink_rows(own_ids, rows, [own], partial, chunk)
        partial = shrink_rows(other_ids, rows, other, partial, chunk)
        factors, ids = [own] + other, jnp.concatenate([own_ids, other_ids])
    else:
        other = lax.all_gather(other, "level", axis=0, tiled=True)
        factors = [jnp.concatenate([own, other], axis=0)]
        ids = jnp.concatenate([own_ids, order * sides + (side ^ 1)])
        chunk = 4
        partial = shrink_rows(ids, rows, factors, partial, chunk)

    for c in range(1, tp):
        partial = partial + lax.ppermute(partial, "tp", [(t, t ^ c) for t in range(tp)])
    partial = partial.astype(jnp.bfloat16)
    lows = [partial] + [swap(partial, s) for s in range(1, square)]
    deltas = expand_rows(ids, me[None], rows, lows, factors, chunk, outputs)
    deltas = [deltas[0]] + [swap(deltas[s], s) for s in range(1, square)]
    return attend(
        me[None],
        query_base,
        new_key,
        new_value,
        cache_keys,
        cache_values,
        lengths,
        deltas,
    )


def solution(mesh):
    reps, pool, tp = (mesh.shape[a] for a in ("rep", "pool", "tp"))
    finer = Mesh(mesh.devices.reshape(reps, pool // 2, 2, tp), ("rep", "level", "side", "tp"))
    pooled = ("level", "side")
    requests = ("rep", "level", "side")
    in_specs = (
        P(requests, "tp"),
        P(requests, None),
        P(),
        P(pooled, "tp", None),
        P(pooled, None, "tp"),
        P(requests, "tp"),
        P(requests, "tp"),
        P(requests, "tp"),
        P(requests, None, "tp"),
        P(requests, None, "tp"),
        P(requests),
    )
    return jax.shard_map(
        per_device, mesh=finer, in_specs=in_specs, out_specs=P(requests, "tp"), check_vma=False
    )
```

```python
import functools
import math

import jax
import jax.numpy as jnp
from jax import lax
from jax.experimental import pallas as pl
from jax.experimental.pallas import tpu as pltpu
from jax.sharding import Mesh
from jax.sharding import PartitionSpec as P

HEAD = 128
LANES = 128
STEP = 16
HALF = 8
BATCH = 2
DEAD = -1e30
VMEM = pl.BlockSpec(memory_space=pltpu.VMEM)
SMEM = pl.BlockSpec(memory_space=pltpu.SMEM)
HBM = pl.BlockSpec(memory_space=pltpu.HBM)
PARAMS = pltpu.CompilerParams(vmem_limit_bytes=12 * 1024 * 1024)
NT = (((1,), (1,)), ((), ()))
TN = (((0,), (0,)), ((), ()))


def columns(at, width):
    return pl.ds(pl.multiple_of(at * width, width), width)


def run_copies(moves, sems, meanwhile=None):
    copies = [pltpu.make_async_copy(src, dst, sems.at[k]) for k, (src, dst) in enumerate(moves)]
    for copy in copies:
        copy.start()
    if meanwhile is not None:
        meanwhile()
    for copy in copies:
        copy.wait()


def factor_kernel(sides, levels, rep_ref, factor_ref, send_ref, sems):
    width = send_ref.shape[2]
    moves = []
    for side in range(sides):
        share = factor_ref.at[0, :, columns(rep_ref[0] * sides + side, width)]
        moves += [(share, send_ref.at[level * sides + side]) for level in range(levels)]
    run_copies(moves, sems)


def load_kernel(count, *refs):
    run_copies(list(zip(refs[:count], refs[count : 2 * count])), refs[-1])


def row_kernel(parts, me_ref, map_ref, ids_ref, hidden_ref, *refs):
    out_refs, sems = refs[:parts], refs[parts]
    requests, wide = hidden_ref.shape
    features = wide // parts
    moves = [
        (hidden_ref.at[:, columns(me_ref[0] ^ s, features)], out_refs[s].at[:, :features])
        for s in range(parts)
    ]

    def owners():
        ids = ids_ref[...]

        def look(k, found):
            return jnp.where(ids == k, map_ref[k], found)

        found = lax.fori_loop(0, map_ref.shape[0], look, jnp.zeros_like(ids))
        found = jnp.broadcast_to(found.astype(jnp.float32), (LANES, requests)).T
        for s in range(parts):
            out_refs[s][:, features:] = found.astype(jnp.bfloat16)

    run_copies(moves, sems, owners)


def owner_mask(rows_ref, first, count, rank):
    features = rows_ref.shape[1] - LANES
    owners = rows_ref[:, features:].astype(jnp.float32).astype(jnp.int32)
    wide = jnp.concatenate([owners] * (count * rank // LANES), axis=1)
    return wide == lax.broadcasted_iota(jnp.int32, (1, count * rank), 1) // rank + first


def shrink_kernel(parts, *refs):
    row_refs, weight_ref, out_ref = refs[:parts], refs[parts], refs[parts + 1]
    count, rank, features = weight_ref.shape
    requests = row_refs[0].shape[0]
    step = pl.program_id(0)
    weight = weight_ref[...].reshape(count * rank, features)
    low = lax.broadcasted_iota(jnp.int32, (requests, LANES), 1) < rank
    folded = []
    for ref in row_refs:
        sums = lax.dot_general(
            ref[:, :features], weight, NT, preferred_element_type=jnp.float32
        )
        sums = jnp.where(owner_mask(ref, step * count, count, rank), sums, 0.0)
        total = sums[:, :LANES]
        for k in range(1, count * rank // LANES):
            total = total + sums[:, k * LANES : (k + 1) * LANES]
        folded.append(total + pltpu.roll(total, rank, 1))

    @pl.when(step == 0)
    def _():
        out_ref[...] = jnp.zeros_like(out_ref)

    half = parts // 2
    for s in range(half):
        rows = pl.ds(s * requests, requests)
        out_ref[rows, :] += jnp.where(low, folded[s], folded[s + half])


def expand_kernel(parts, *refs):
    row_refs, low_refs, weight_ref = refs[:parts], refs[parts : 2 * parts], refs[2 * parts]
    out_refs, total_ref = refs[2 * parts + 1 : 3 * parts + 1], refs[3 * parts + 1]
    count, rank, outputs = weight_ref.shape
    requests = row_refs[0].shape[0]
    step, last = pl.program_id(0), pl.num_programs(0) - 1
    weight = weight_ref[...].reshape(count * rank, outputs)
    half = parts // 2
    low = lax.broadcasted_iota(jnp.int32, (requests, LANES), 1) < rank
    held = [[0.0] * half for _ in range(2)]
    for t in range(parts):
        sums = low_refs[t][...].astype(jnp.float32)
        for s in range(half):
            at = (s ^ t) % half
            piece = sums[at * requests : (at + 1) * requests]
            held[t // half][s] = held[t // half][s] + piece
    for s in range(half):
        straight = held[0][s] + pltpu.roll(held[1][s], rank, 1)
        turned = pltpu.roll(straight, rank, 1)
        for part in (s, s + half):
            first, other = (straight, turned) if part < half else (turned, straight)
            wide = jnp.concatenate([jnp.where(low, first, other)] * (count * rank // LANES), axis=1)
            wide = jnp.where(owner_mask(row_refs[part], step * count, count, rank), wide, 0.0)
            product = jnp.dot(
                wide.astype(jnp.bfloat16), weight, preferred_element_type=jnp.float32
            )

            @pl.when(step == 0)
            def _():
                total_ref[part] = product

            @pl.when(step > 0)
            def _():
                total_ref[part] += product

            @pl.when(step == last)
            def _():
                out_refs[part][...] = total_ref[part].astype(jnp.bfloat16)


def attend_kernel(parts, me_ref, len_ref, *refs):
    base_ref, nk_ref, nv_ref, ck_ref, cv_ref, *delta_refs, out_ref = refs
    me = me_ref[0]
    block = STEP * BATCH
    steps = base_ref.shape[0] // block
    requests, columns = base_ref.shape
    width = columns // parts
    groups = nk_ref.shape[1] // HEAD
    slots = ck_ref.shape[1]
    heads = columns // HEAD
    per_part = width // HEAD
    span = heads * HALF
    part_span = per_part * HALF
    keys_in = HALF * slots + STEP
    row = lax.broadcasted_iota(jnp.int32, (keys_in, span), 0)
    lane_req = lax.broadcasted_iota(jnp.int32, (keys_in, span), 1) % HALF
    own = row - HALF * slots
    slot_of = []
    for h in range(STEP // HALF):
        cached = jnp.where(row // slots == lane_req, row % slots, slots)
        fresh = jnp.where(own == lane_req + h * HALF, -1, slots)
        slot_of.append(jnp.where(own >= 0, fresh, cached))
    part_at = [me ^ s for s in range(parts)]
    group_at = [p // (parts // groups) for p in part_at]
    lane_part = lax.broadcasted_iota(jnp.int32, (1, span), 1) // part_span
    lane_group = jnp.zeros_like(lane_part)
    for s in range(parts):
        lane_group = jnp.where(lane_part == s, group_at[s], lane_group)
    scale = 1.0 / math.sqrt(HEAD)
    ones = jnp.ones((keys_in, HEAD), jnp.bfloat16)

    for step in range(steps):
        units = []
        for j in range(BATCH):
            start = step * block + j * STEP
            at = pl.ds(start, STEP)
            pieces = []
            for s in range(parts):
                lanes = pl.ds(pl.multiple_of(part_at[s] * width, width), width)
                q = base_ref[at, lanes].astype(jnp.float32)
                q = q + delta_refs[s][at, :].astype(jnp.float32)
                pieces += [q[:, k * HEAD : (k + 1) * HEAD] for k in range(per_part)]
            for h in range(STEP // HALF):
                slab = pl.ds(start + h * HALF, HALF)
                q = jnp.concatenate([p[h * HALF : (h + 1) * HALF] for p in pieces], axis=0)
                units.append((step * BATCH + j, at, h, slab, q.astype(jnp.bfloat16)))
        scores = []
        for _, at, h, slab, q in units:
            both = []
            for g in range(groups):
                lanes = slice(g * HEAD, (g + 1) * HEAD)
                keys = ck_ref[slab, :, lanes].reshape(HALF * slots, HEAD)
                keys = jnp.concatenate([keys, nk_ref[at, lanes]], axis=0)
                both.append(lax.dot_general(keys, q, NT, preferred_element_type=jnp.float32))
            score = both[0]
            for g in range(1, groups):
                score = jnp.where(lane_group == g, both[g], score)
            scores.append(score)
        probs = []
        for (i, at, h, slab, q), score in zip(units, scores):
            lens = len_ref[pl.ds(i * (STEP // HALF) + h, 1), :]
            score = jnp.where(slot_of[h] < lens, score, DEAD)
            top = jnp.max(score, axis=0, keepdims=True)
            exps = jnp.exp((score - top) * scale)
            total = jnp.sum(exps, axis=0, keepdims=True)
            probs.append((exps * (1.0 / total)).astype(jnp.bfloat16))
        mixed = []
        for (i, at, h, slab, q), prob in zip(units, probs):
            whole = []
            for g in range(groups):
                lanes = slice(g * HEAD, (g + 1) * HEAD)
                values = cv_ref[slab, :, lanes].reshape(HALF * slots, HEAD)
                values = jnp.concatenate([values, nv_ref[at, lanes]], axis=0)
                whole.append(
                    lax.dot_general(prob, values, TN, preferred_element_type=jnp.float32)
                )
            mixed.append(whole)
        for j in range(BATCH):
            at = units[2 * j][1]
            for s in range(parts):
                rows = slice(s * part_span, (s + 1) * part_span)
                halves = []
                for h in range(STEP // HALF):
                    whole = mixed[2 * j + h]
                    part = whole[0][rows]
                    for g in range(1, groups):
                        part = jnp.where(group_at[s] == g, whole[g][rows], part)
                    halves.append(part)
                out = [
                    jnp.concatenate([p[k * HALF : (k + 1) * HALF] for p in halves], axis=0)
                    for k in range(per_part)
                ]
                lanes = pl.ds(pl.multiple_of(part_at[s] * width, width), width)
                out_ref[at, lanes] = jnp.concatenate(out, axis=1).astype(jnp.bfloat16)


def attend(me, base, new_key, new_value, cache_keys, cache_values, lengths, deltas):
    requests, columns = base.shape
    kv = new_key.shape[1]
    slots = cache_keys.shape[1]
    lengths = jnp.tile(lengths.reshape(requests // HALF, HALF), (1, columns // HEAD))
    arrays = [base, new_key, new_value, cache_keys, cache_values, *deltas]
    return pl.pallas_call(
        functools.partial(attend_kernel, len(deltas)),
        out_shape=jax.ShapeDtypeStruct((requests, columns), jnp.bfloat16),
        in_specs=[SMEM] + [VMEM] * (1 + len(arrays)),
        out_specs=VMEM,
        compiler_params=PARAMS,
        cost_estimate=pl.CostEstimate(
            flops=4 * requests * HALF * slots * columns,
            bytes_accessed=4 * requests * (columns + slots * kv),
            transcendentals=requests * slots * columns // 16,
        ),
    )(me, lengths, *arrays)


def whole(array):
    return pl.BlockSpec(array.shape, lambda *_: (0,) * len(array.shape))


def in_chunks(weight):
    chunk = math.gcd(weight.shape[0], 8)
    return weight.shape[0] // chunk, pl.BlockSpec((chunk,) + weight.shape[1:], lambda i: (i, 0, 0))


def shrink_rows(rows, weight):
    parts, requests = len(rows), rows[0].shape[0]
    steps, spec = in_chunks(weight)
    out = jax.ShapeDtypeStruct((parts // 2 * requests, LANES), jnp.float32)
    return pl.pallas_call(
        functools.partial(shrink_kernel, parts),
        out_shape=out,
        grid=(steps,),
        in_specs=[*map(whole, rows), spec],
        out_specs=whole(out),
        compiler_params=PARAMS,
    )(*rows, weight)


def expand_rows(rows, lows, weight):
    parts, requests, outputs = len(rows), rows[0].shape[0], weight.shape[2]
    steps, spec = in_chunks(weight)
    out = jax.ShapeDtypeStruct((requests, outputs), jnp.bfloat16)
    return pl.pallas_call(
        functools.partial(expand_kernel, parts),
        out_shape=[out] * parts,
        grid=(steps,),
        in_specs=[*map(whole, rows), *map(whole, lows), spec],
        out_specs=[whole(out)] * parts,
        scratch_shapes=[pltpu.VMEM((parts, requests, outputs), jnp.float32)],
        compiler_params=PARAMS,
    )(*rows, *lows, weight)


def per_device(
    hidden,
    adapter_ids,
    owner_map,
    shrink_factors,
    expand_factors,
    query_base,
    new_key,
    new_value,
    cache_keys,
    cache_values,
    lengths,
):
    reps, levels, sides, tp = (lax.axis_size(a) for a in ("rep", "level", "side", "tp"))
    pool = levels * sides
    requests, wide = hidden.shape
    rank = shrink_factors.shape[2]
    square = reps * sides
    rep = lax.axis_index("rep")
    me = rep * sides + lax.axis_index("side")

    def swap(a, s):
        pairs = [(c, c ^ s) for c in range(square)]
        return lax.ppermute(a, ("rep", "side"), pairs)

    def to_pool(factor, after=None):
        width = factor.shape[2] // square
        send = pl.pallas_call(
            functools.partial(factor_kernel, sides, levels),
            out_shape=jax.ShapeDtypeStruct((pool, rank, width), jnp.bfloat16),
            in_specs=[SMEM, HBM],
            out_specs=VMEM,
            scratch_shapes=[pltpu.SemaphoreType.DMA((pool,))],
        )(rep[None], factor)
        if after is not None:
            send, after = lax.optimization_barrier((send, after))
        got = lax.all_to_all(send, ("level", "side"), split_axis=0, concat_axis=0, tiled=True)
        return got, after

    shrink, _ = to_pool(shrink_factors.swapaxes(1, 2))
    rows = pl.pallas_call(
        functools.partial(row_kernel, square),
        out_shape=[jax.ShapeDtypeStruct((requests, wide // square + LANES), jnp.bfloat16)] * square,
        in_specs=[SMEM, SMEM, VMEM, HBM],
        out_specs=[VMEM] * square,
        scratch_shapes=[pltpu.SemaphoreType.DMA((square,))],
    )(me[None], owner_map, adapter_ids.T, hidden)
    rows = [rows[0]] + [swap(rows[s], s) for s in range(1, square)]
    arrays = [query_base, new_key, new_value, cache_keys, cache_values]
    arrays = pl.pallas_call(
        functools.partial(load_kernel, len(arrays)),
        out_shape=[jax.ShapeDtypeStruct(a.shape, a.dtype) for a in arrays],
        in_specs=[HBM] * len(arrays),
        out_specs=[VMEM] * len(arrays),
        scratch_shapes=[pltpu.SemaphoreType.DMA((len(arrays),))],
    )(*arrays)
    rows[0], *arrays = lax.optimization_barrier((rows[0], *arrays))

    expand, shrink = to_pool(expand_factors, shrink)
    partial = shrink_rows(rows, shrink)
    for c in range(1, tp):
        partial = partial + lax.ppermute(partial, "tp", [(t, t ^ c) for t in range(tp)])
    partial = partial.astype(jnp.bfloat16)
    lows = [partial] + [swap(partial, s) for s in range(1, square)]
    deltas = expand_rows(rows, lows, expand)
    deltas = [deltas[0]] + [swap(deltas[s], s) for s in range(1, square)]
    return attend(me[None], *arrays, lengths, deltas)


def solution(mesh):
    reps, pool, tp = (mesh.shape[a] for a in ("rep", "pool", "tp"))
    finer = Mesh(mesh.devices.reshape(reps, pool // 2, 2, tp), ("rep", "level", "side", "tp"))
    pooled = ("level", "side")
    requests = ("rep", "level", "side")
    in_specs = (
        P(requests, "tp"),
        P(requests, None),
        P(),
        P(pooled, "tp", None),
        P(pooled, None, "tp"),
        P(requests, "tp"),
        P(requests, "tp"),
        P(requests, "tp"),
        P(requests, None, "tp"),
        P(requests, None, "tp"),
        P(requests),
    )
    return jax.shard_map(
        per_device, mesh=finer, in_specs=in_specs, out_specs=P(requests, "tp"), check_vma=False
    )
```

```python
import functools
import math

import jax
import jax.numpy as jnp
from jax import lax
from jax.experimental import pallas as pl
from jax.experimental.pallas import tpu as pltpu
from jax.sharding import Mesh
from jax.sharding import PartitionSpec as P

HEAD = 128
LANES = 128
STEP = 16
HALF = 8
BATCH = 2
DEAD = -1e30
VMEM = pl.BlockSpec(memory_space=pltpu.VMEM)
SMEM = pl.BlockSpec(memory_space=pltpu.SMEM)
HBM = pl.BlockSpec(memory_space=pltpu.HBM)
PARAMS = pltpu.CompilerParams(vmem_limit_bytes=12 * 1024 * 1024)
NT = (((1,), (1,)), ((), ()))
TN = (((0,), (0,)), ((), ()))


def columns(at, width):
    return pl.ds(pl.multiple_of(at * width, width), width)


def run_copies(moves, sems, meanwhile=None):
    copies = [pltpu.make_async_copy(src, dst, sems.at[k]) for k, (src, dst) in enumerate(moves)]
    for copy in copies:
        copy.start()
    if meanwhile is not None:
        meanwhile()
    for copy in copies:
        copy.wait()


def factor_kernel(sides, levels, rep_ref, factor_ref, send_ref, sems):
    width = send_ref.shape[2]
    moves = []
    for side in range(sides):
        share = factor_ref.at[0, :, columns(rep_ref[0] * sides + side, width)]
        moves += [(share, send_ref.at[level * sides + side]) for level in range(levels)]
    run_copies(moves, sems)


def row_kernel(parts, me_ref, map_ref, ids_ref, hidden_ref, *refs):
    out_refs, sems = refs[:parts], refs[parts]
    requests, wide = hidden_ref.shape
    features = wide // parts
    moves = [
        (hidden_ref.at[:, columns(me_ref[0] ^ s, features)], out_refs[s].at[:, :features])
        for s in range(parts)
    ]

    def owners():
        ids = ids_ref[...]

        def look(k, found):
            return jnp.where(ids == k, map_ref[k], found)

        found = lax.fori_loop(0, map_ref.shape[0], look, jnp.zeros_like(ids))
        found = jnp.broadcast_to(found.astype(jnp.float32), (LANES, requests)).T
        for s in range(parts):
            out_refs[s][:, features:] = found.astype(jnp.bfloat16)

    run_copies(moves, sems, owners)


def owner_mask(owners, first, count, rank):
    owners = owners.astype(jnp.float32).astype(jnp.int32)
    wide = jnp.concatenate([owners] * (count * rank // LANES), axis=1)
    return wide == lax.broadcasted_iota(jnp.int32, (1, count * rank), 1) // rank + first


def shrink_kernel(parts, *refs):
    row_refs, weight_ref, out_ref = refs[:parts], refs[parts], refs[parts + 1]
    count, rank, features = weight_ref.shape
    requests = row_refs[0].shape[0]
    step = pl.program_id(0)
    weight = weight_ref[...].reshape(count * rank, features)
    low = lax.broadcasted_iota(jnp.int32, (requests, LANES), 1) < rank
    folded = []
    for ref in row_refs:
        sums = lax.dot_general(
            ref[:, :features], weight, NT, preferred_element_type=jnp.float32
        )
        sums = jnp.where(owner_mask(ref[:, features:], step * count, count, rank), sums, 0.0)
        total = sums[:, :LANES]
        for k in range(1, count * rank // LANES):
            total = total + sums[:, k * LANES : (k + 1) * LANES]
        folded.append(total + pltpu.roll(total, rank, 1))

    @pl.when(step == 0)
    def _():
        out_ref[...] = jnp.zeros_like(out_ref)

    half = parts // 2
    for s in range(half):
        rows = pl.ds(s * requests, requests)
        out_ref[rows, :] += jnp.where(low, folded[s], folded[s + half])


def expand_kernel(parts, *refs):
    owner_refs, low_refs, weight_ref = refs[:parts], refs[parts : 2 * parts], refs[2 * parts]
    out_refs, total_ref = refs[2 * parts + 1 : 3 * parts + 1], refs[3 * parts + 1]
    count, rank, outputs = weight_ref.shape
    requests = owner_refs[0].shape[0]
    step, last = pl.program_id(0), pl.num_programs(0) - 1
    weight = weight_ref[...].reshape(count * rank, outputs)
    half = parts // 2
    low = lax.broadcasted_iota(jnp.int32, (requests, LANES), 1) < rank
    held = [[0.0] * half for _ in range(2)]
    for t in range(parts):
        sums = low_refs[t][...].astype(jnp.float32)
        for s in range(half):
            at = (s ^ t) % half
            piece = sums[at * requests : (at + 1) * requests]
            held[t // half][s] = held[t // half][s] + piece
    for s in range(half):
        straight = held[0][s] + pltpu.roll(held[1][s], rank, 1)
        turned = pltpu.roll(straight, rank, 1)
        for part in (s, s + half):
            first, other = (straight, turned) if part < half else (turned, straight)
            wide = jnp.concatenate([jnp.where(low, first, other)] * (count * rank // LANES), axis=1)
            mask = owner_mask(owner_refs[part][...], step * count, count, rank)
            wide = jnp.where(mask, wide, 0.0)
            product = jnp.dot(
                wide.astype(jnp.bfloat16), weight, preferred_element_type=jnp.float32
            )

            @pl.when(step == 0)
            def _():
                total_ref[part] = product

            @pl.when(step > 0)
            def _():
                total_ref[part] += product

            @pl.when(step == last)
            def _():
                out_refs[part][...] = total_ref[part].astype(jnp.bfloat16)


def attend_kernel(parts, me_ref, len_ref, *refs):
    base_ref, nk_ref, nv_ref, ck_ref, cv_ref, *delta_refs, out_ref = refs
    me = me_ref[0]
    columns = base_ref.shape[1]
    width = columns // parts
    groups = nk_ref.shape[1] // HEAD
    slots = ck_ref.shape[1]
    heads = columns // HEAD
    per_part = width // HEAD
    span = heads * HALF
    part_span = per_part * HALF
    keys_in = HALF * slots + STEP
    row = lax.broadcasted_iota(jnp.int32, (keys_in, span), 0)
    lane_req = lax.broadcasted_iota(jnp.int32, (keys_in, span), 1) % HALF
    own = row - HALF * slots
    slot_of = []
    for h in range(STEP // HALF):
        cached = jnp.where(row // slots == lane_req, row % slots, slots)
        fresh = jnp.where(own == lane_req + h * HALF, -1, slots)
        slot_of.append(jnp.where(own >= 0, fresh, cached))
    part_at = [me ^ s for s in range(parts)]
    group_at = [p // (parts // groups) for p in part_at]
    lane_part = lax.broadcasted_iota(jnp.int32, (1, span), 1) // part_span
    lane_group = jnp.zeros_like(lane_part)
    for s in range(parts):
        lane_group = jnp.where(lane_part == s, group_at[s], lane_group)
    scale = 1.0 / math.sqrt(HEAD)
    ones = jnp.ones((keys_in, HEAD), jnp.bfloat16)

    if True:
        step = pl.program_id(0)
        units = []
        for j in range(BATCH):
            start = j * STEP
            at = pl.ds(start, STEP)
            pieces = []
            for s in range(parts):
                lanes = pl.ds(pl.multiple_of(part_at[s] * width, width), width)
                q = base_ref[at, lanes].astype(jnp.float32)
                q = q + delta_refs[s][at, :].astype(jnp.float32)
                pieces += [q[:, k * HEAD : (k + 1) * HEAD] for k in range(per_part)]
            for h in range(STEP // HALF):
                slab = pl.ds(start + h * HALF, HALF)
                q = jnp.concatenate([p[h * HALF : (h + 1) * HALF] for p in pieces], axis=0)
                units.append((step * BATCH + j, at, h, slab, q.astype(jnp.bfloat16)))
        scores = []
        for _, at, h, slab, q in units:
            both = []
            for g in range(groups):
                lanes = slice(g * HEAD, (g + 1) * HEAD)
                keys = ck_ref[slab, :, lanes].reshape(HALF * slots, HEAD)
                keys = jnp.concatenate([keys, nk_ref[at, lanes]], axis=0)
                both.append(lax.dot_general(keys, q, NT, preferred_element_type=jnp.float32))
            score = both[0]
            for g in range(1, groups):
                score = jnp.where(lane_group == g, both[g], score)
            scores.append(score)
        probs = []
        for (i, at, h, slab, q), score in zip(units, scores):
            lens = len_ref[pl.ds(i * (STEP // HALF) + h, 1), :]
            score = jnp.where(slot_of[h] < lens, score, DEAD)
            top = jnp.max(score, axis=0, keepdims=True)
            exps = jnp.exp((score - top) * scale)
            total = jnp.sum(exps, axis=0, keepdims=True)
            probs.append((exps * (1.0 / total)).astype(jnp.bfloat16))
        mixed = []
        for (i, at, h, slab, q), prob in zip(units, probs):
            whole = []
            for g in range(groups):
                lanes = slice(g * HEAD, (g + 1) * HEAD)
                values = cv_ref[slab, :, lanes].reshape(HALF * slots, HEAD)
                values = jnp.concatenate([values, nv_ref[at, lanes]], axis=0)
                whole.append(
                    lax.dot_general(prob, values, TN, preferred_element_type=jnp.float32)
                )
            mixed.append(whole)
        for j in range(BATCH):
            at = units[2 * j][1]
            for s in range(parts):
                rows = slice(s * part_span, (s + 1) * part_span)
                halves = []
                for h in range(STEP // HALF):
                    whole = mixed[2 * j + h]
                    part = whole[0][rows]
                    for g in range(1, groups):
                        part = jnp.where(group_at[s] == g, whole[g][rows], part)
                    halves.append(part)
                out = [
                    jnp.concatenate([p[k * HALF : (k + 1) * HALF] for p in halves], axis=0)
                    for k in range(per_part)
                ]
                lanes = pl.ds(pl.multiple_of(part_at[s] * width, width), width)
                out_ref[at, lanes] = jnp.concatenate(out, axis=1).astype(jnp.bfloat16)


def attend(me, base, new_key, new_value, cache_keys, cache_values, lengths, deltas):
    requests, columns = base.shape
    kv = new_key.shape[1]
    slots = cache_keys.shape[1]
    lengths = jnp.tile(lengths.reshape(requests // HALF, HALF), (1, columns // HEAD))
    block = STEP * BATCH
    rows2 = lambda a: pl.BlockSpec((block,) + a.shape[1:], lambda i: (i,) + (0,) * (a.ndim - 1))
    arrays = [base, new_key, new_value, cache_keys, cache_values, *deltas]
    return pl.pallas_call(
        functools.partial(attend_kernel, len(deltas)),
        out_shape=jax.ShapeDtypeStruct((requests, columns), jnp.bfloat16),
        grid=(requests // block,),
        in_specs=[SMEM, whole(lengths), *map(rows2, arrays)],
        out_specs=rows2(base),
        cost_estimate=pl.CostEstimate(
            flops=4 * requests * HALF * slots * columns,
            bytes_accessed=4 * requests * (columns + slots * kv),
            transcendentals=requests * slots * columns // 16,
        ),
    )(me, lengths, *arrays)


def whole(array):
    return pl.BlockSpec(array.shape, lambda *_: (0,) * len(array.shape))


def in_chunks(weight):
    chunk = math.gcd(weight.shape[0], 8)
    return weight.shape[0] // chunk, pl.BlockSpec((chunk,) + weight.shape[1:], lambda i: (i, 0, 0))


def shrink_rows(rows, weight):
    parts, requests = len(rows), rows[0].shape[0]
    steps, spec = in_chunks(weight)
    out = jax.ShapeDtypeStruct((parts // 2 * requests, LANES), jnp.float32)
    return pl.pallas_call(
        functools.partial(shrink_kernel, parts),
        out_shape=out,
        grid=(steps,),
        in_specs=[*map(whole, rows), spec],
        out_specs=whole(out),
        compiler_params=PARAMS,
    )(*rows, weight)


def expand_rows(rows, lows, weight):
    parts, requests, outputs = len(rows), rows[0].shape[0], weight.shape[2]
    steps, spec = in_chunks(weight)
    last_lanes = rows[0].shape[1] // LANES - 1
    owners = pl.BlockSpec((requests, LANES), lambda i: (0, last_lanes))
    out = jax.ShapeDtypeStruct((requests, outputs), jnp.bfloat16)
    return pl.pallas_call(
        functools.partial(expand_kernel, parts),
        out_shape=[out] * parts,
        grid=(steps,),
        in_specs=[owners] * parts + [*map(whole, lows), spec],
        out_specs=[whole(out)] * parts,
        scratch_shapes=[pltpu.VMEM((parts, requests, outputs), jnp.float32)],
    )(*rows, *lows, weight)


def per_device(
    hidden,
    adapter_ids,
    owner_map,
    shrink_factors,
    expand_factors,
    query_base,
    new_key,
    new_value,
    cache_keys,
    cache_values,
    lengths,
):
    reps, levels, sides, tp = (lax.axis_size(a) for a in ("rep", "level", "side", "tp"))
    pool = levels * sides
    requests, wide = hidden.shape
    rank = shrink_factors.shape[2]
    square = reps * sides
    rep = lax.axis_index("rep")
    me = rep * sides + lax.axis_index("side")

    def swap(a, s):
        pairs = [(c, c ^ s) for c in range(square)]
        return lax.ppermute(a, ("rep", "side"), pairs)

    def to_pool(factor, after=None):
        width = factor.shape[2] // square
        send = pl.pallas_call(
            functools.partial(factor_kernel, sides, levels),
            out_shape=jax.ShapeDtypeStruct((pool, rank, width), jnp.bfloat16),
            in_specs=[SMEM, HBM],
            out_specs=VMEM,
            scratch_shapes=[pltpu.SemaphoreType.DMA((pool,))],
        )(rep[None], factor)
        if after is not None:
            send, after = lax.optimization_barrier((send, after))
        got = lax.all_to_all(send, ("level", "side"), split_axis=0, concat_axis=0, tiled=True)
        return got, after

    shrink, _ = to_pool(shrink_factors.swapaxes(1, 2))
    rows = pl.pallas_call(
        functools.partial(row_kernel, square),
        out_shape=[jax.ShapeDtypeStruct((requests, wide // square + LANES), jnp.bfloat16)] * square,
        in_specs=[SMEM, SMEM, VMEM, HBM],
        out_specs=[VMEM] * square,
        scratch_shapes=[pltpu.SemaphoreType.DMA((square,))],
    )(me[None], owner_map, adapter_ids.T, hidden)
    rows = [rows[0]] + [swap(rows[s], s) for s in range(1, square)]
    expand, rows = to_pool(expand_factors, rows)
    partial = shrink_rows(rows, shrink)
    for c in range(1, tp):
        partial = partial + lax.ppermute(partial, "tp", [(t, t ^ c) for t in range(tp)])
    partial = partial.astype(jnp.bfloat16)
    lows = [partial] + [swap(partial, s) for s in range(1, square)]
    deltas = expand_rows(rows, lows, expand)
    deltas = [deltas[0]] + [swap(deltas[s], s) for s in range(1, square)]
    return attend(
        me[None], query_base, new_key, new_value, cache_keys, cache_values, lengths, deltas
    )


def solution(mesh):
    reps, pool, tp = (mesh.shape[a] for a in ("rep", "pool", "tp"))
    finer = Mesh(mesh.devices.reshape(reps, pool // 2, 2, tp), ("rep", "level", "side", "tp"))
    pooled = ("level", "side")
    requests = ("rep", "level", "side")
    in_specs = (
        P(requests, "tp"),
        P(requests, None),
        P(),
        P(pooled, "tp", None),
        P(pooled, None, "tp"),
        P(requests, "tp"),
        P(requests, "tp"),
        P(requests, "tp"),
        P(requests, None, "tp"),
        P(requests, None, "tp"),
        P(requests),
    )
    return jax.shard_map(
        per_device, mesh=finer, in_specs=in_specs, out_specs=P(requests, "tp"), check_vma=False
    )
```

```python
import functools
import math

import jax
import jax.numpy as jnp
from jax import lax
from jax.experimental import pallas as pl
from jax.experimental.pallas import tpu as pltpu
from jax.sharding import Mesh
from jax.sharding import PartitionSpec as P

HEAD = 128
LANES = 128
STEP = 16
HALF = 8
BATCH = 2
DEAD = -1e30
VMEM = pl.BlockSpec(memory_space=pltpu.VMEM)
SMEM = pl.BlockSpec(memory_space=pltpu.SMEM)
HBM = pl.BlockSpec(memory_space=pltpu.HBM)
PARAMS = pltpu.CompilerParams(vmem_limit_bytes=12 * 1024 * 1024)
NT = (((1,), (1,)), ((), ()))
TN = (((0,), (0,)), ((), ()))


def columns(at, width):
    return pl.ds(pl.multiple_of(at * width, width), width)


def run_copies(moves, sems, meanwhile=None):
    copies = [pltpu.make_async_copy(src, dst, sems.at[k]) for k, (src, dst) in enumerate(moves)]
    for copy in copies:
        copy.start()
    if meanwhile is not None:
        meanwhile()
    for copy in copies:
        copy.wait()


def factor_kernel(parts, me_ref, shrink_ref, expand_ref, own_ref, other_ref, sems):
    features, outputs = shrink_ref.shape[2] // parts, expand_ref.shape[2] // parts
    me = me_ref[0]
    moves = []
    for at, ref in ((me, own_ref), (me ^ 1, other_ref)):
        shrink = shrink_ref.at[0, :, columns(at, features)]
        expand = expand_ref.at[0, :, columns(at, outputs)]
        for k in range(ref.shape[0]):
            moves.append((shrink, ref.at[k, :, :features]))
            moves.append((expand, ref.at[k, :, features:]))
    run_copies(moves, sems)


def row_kernel(parts, me_ref, map_ref, ids_ref, hidden_ref, *refs):
    out_refs, sems = refs[:parts], refs[parts]
    requests, wide = hidden_ref.shape
    features = wide // parts
    moves = [
        (hidden_ref.at[:, columns(me_ref[0] ^ s, features)], out_refs[s].at[:, :features])
        for s in range(parts)
    ]

    def owners():
        ids = ids_ref[...]

        def look(k, found):
            return jnp.where(ids == k, map_ref[k], found)

        found = lax.fori_loop(0, map_ref.shape[0], look, jnp.zeros_like(ids))
        found = jnp.broadcast_to(found.astype(jnp.float32), (LANES, requests)).T
        for s in range(parts):
            out_refs[s][:, features:] = found.astype(jnp.bfloat16)

    run_copies(moves, sems, owners)


def owner_mask(owners, ids, rank):
    lane = lax.broadcasted_iota(jnp.int32, (1, len(ids) * rank), 1) // rank
    named = jnp.full_like(lane, -1)
    for k, owner in enumerate(ids):
        named = jnp.where(lane == k, owner, named)
    owners = owners.astype(jnp.float32).astype(jnp.int32)
    return jnp.concatenate([owners] * (len(ids) * rank // LANES), axis=1) == named


def stacked(refs, lanes):
    return jnp.concatenate([r[k, :, lanes] for r in refs for k in range(r.shape[0])], axis=0)


def step_ids(ids_ref, refs):
    count = sum(r.shape[0] for r in refs)
    return [ids_ref[pl.program_id(0) * count + k] for k in range(count)]


def shrink_kernel(parts, ids_ref, *refs):
    row_refs, factor_refs, out_ref = refs[:parts], refs[parts:-1], refs[-1]
    rank = factor_refs[0].shape[1]
    requests, features = row_refs[0].shape[0], row_refs[0].shape[1] - LANES
    ids = step_ids(ids_ref, factor_refs)
    weight = stacked(factor_refs, slice(0, features))
    low = lax.broadcasted_iota(jnp.int32, (requests, LANES), 1) < rank
    folded = []
    for ref in row_refs:
        sums = lax.dot_general(
            ref[:, :features], weight, NT, preferred_element_type=jnp.float32
        )
        sums = jnp.where(owner_mask(ref[:, features:], ids, rank), sums, 0.0)
        total = sums[:, :LANES]
        for k in range(1, len(ids) * rank // LANES):
            total = total + sums[:, k * LANES : (k + 1) * LANES]
        folded.append(total + pltpu.roll(total, rank, 1))

    @pl.when(pl.program_id(0) == 0)
    def _():
        out_ref[...] = jnp.zeros_like(out_ref)

    half = parts // 2
    for s in range(half):
        rows = pl.ds(s * requests, requests)
        out_ref[rows, :] += jnp.where(low, folded[s], folded[s + half])


def expand_kernel(parts, ids_ref, *refs):
    owner_refs, low_refs, factor_refs = refs[:parts], refs[parts : 2 * parts], refs[2 * parts : -parts - 1]
    out_refs, total_ref = refs[-parts - 1 : -1], refs[-1]
    rank, width = factor_refs[0].shape[1:]
    requests, outputs = out_refs[0].shape
    step, last = pl.program_id(0), pl.num_programs(0) - 1
    ids = step_ids(ids_ref, factor_refs)
    weight = stacked(factor_refs, slice(width - outputs, width))
    half = parts // 2
    low = lax.broadcasted_iota(jnp.int32, (requests, LANES), 1) < rank
    held = [[0.0] * half for _ in range(2)]
    for t in range(parts):
        sums = low_refs[t][...].astype(jnp.float32)
        for s in range(half):
            at = (s ^ t) % half
            piece = sums[at * requests : (at + 1) * requests]
            held[t // half][s] = held[t // half][s] + piece
    for s in range(half):
        straight = held[0][s] + pltpu.roll(held[1][s], rank, 1)
        turned = pltpu.roll(straight, rank, 1)
        for part in (s, s + half):
            first, other = (straight, turned) if part < half else (turned, straight)
            both = jnp.where(low, first, other)
            wide = jnp.concatenate([both] * (len(ids) * rank // LANES), axis=1)
            wide = jnp.where(owner_mask(owner_refs[part][...], ids, rank), wide, 0.0)
            product = jnp.dot(
                wide.astype(jnp.bfloat16), weight, preferred_element_type=jnp.float32
            )

            @pl.when(step == 0)
            def _():
                total_ref[part] = product

            @pl.when(step > 0)
            def _():
                total_ref[part] += product

            @pl.when(step == last)
            def _():
                out_refs[part][...] = total_ref[part].astype(jnp.bfloat16)


def attend_kernel(parts, me_ref, len_ref, *refs):
    base_ref, nk_ref, nv_ref, ck_ref, cv_ref, *delta_refs, out_ref = refs
    me = me_ref[0]
    columns = base_ref.shape[1]
    width = columns // parts
    groups = nk_ref.shape[1] // HEAD
    slots = ck_ref.shape[1]
    heads = columns // HEAD
    per_part = width // HEAD
    span = heads * HALF
    part_span = per_part * HALF
    keys_in = HALF * slots + STEP
    row = lax.broadcasted_iota(jnp.int32, (keys_in, span), 0)
    lane_req = lax.broadcasted_iota(jnp.int32, (keys_in, span), 1) % HALF
    own = row - HALF * slots
    slot_of = []
    for h in range(STEP // HALF):
        cached = jnp.where(row // slots == lane_req, row % slots, slots)
        fresh = jnp.where(own == lane_req + h * HALF, -1, slots)
        slot_of.append(jnp.where(own >= 0, fresh, cached))
    part_at = [me ^ s for s in range(parts)]
    group_at = [p // (parts // groups) for p in part_at]
    lane_part = lax.broadcasted_iota(jnp.int32, (1, span), 1) // part_span
    lane_group = jnp.zeros_like(lane_part)
    for s in range(parts):
        lane_group = jnp.where(lane_part == s, group_at[s], lane_group)
    scale = 1.0 / math.sqrt(HEAD)
    ones = jnp.ones((keys_in, HEAD), jnp.bfloat16)

    if True:
        step = pl.program_id(0)
        units = []
        for j in range(BATCH):
            start = j * STEP
            at = pl.ds(start, STEP)
            pieces = []
            for s in range(parts):
                lanes = pl.ds(pl.multiple_of(part_at[s] * width, width), width)
                q = base_ref[at, lanes].astype(jnp.float32)
                q = q + delta_refs[s][at, :].astype(jnp.float32)
                pieces += [q[:, k * HEAD : (k + 1) * HEAD] for k in range(per_part)]
            for h in range(STEP // HALF):
                slab = pl.ds(start + h * HALF, HALF)
                q = jnp.concatenate([p[h * HALF : (h + 1) * HALF] for p in pieces], axis=0)
                units.append((step * BATCH + j, at, h, slab, q.astype(jnp.bfloat16)))
        scores = []
        for _, at, h, slab, q in units:
            both = []
            for g in range(groups):
                lanes = slice(g * HEAD, (g + 1) * HEAD)
                keys = ck_ref[slab, :, lanes].reshape(HALF * slots, HEAD)
                keys = jnp.concatenate([keys, nk_ref[at, lanes]], axis=0)
                both.append(lax.dot_general(keys, q, NT, preferred_element_type=jnp.float32))
            score = both[0]
            for g in range(1, groups):
                score = jnp.where(lane_group == g, both[g], score)
            scores.append(score)
        probs = []
        for (i, at, h, slab, q), score in zip(units, scores):
            lens = len_ref[pl.ds(i * (STEP // HALF) + h, 1), :]
            score = jnp.where(slot_of[h] < lens, score, DEAD)
            top = jnp.max(score, axis=0, keepdims=True)
            exps = jnp.exp((score - top) * scale)
            total = jnp.sum(exps, axis=0, keepdims=True)
            probs.append((exps * (1.0 / total)).astype(jnp.bfloat16))
        mixed = []
        for (i, at, h, slab, q), prob in zip(units, probs):
            whole = []
            for g in range(groups):
                lanes = slice(g * HEAD, (g + 1) * HEAD)
                values = cv_ref[slab, :, lanes].reshape(HALF * slots, HEAD)
                values = jnp.concatenate([values, nv_ref[at, lanes]], axis=0)
                whole.append(
                    lax.dot_general(prob, values, TN, preferred_element_type=jnp.float32)
                )
            mixed.append(whole)
        for j in range(BATCH):
            at = units[2 * j][1]
            for s in range(parts):
                rows = slice(s * part_span, (s + 1) * part_span)
                halves = []
                for h in range(STEP // HALF):
                    whole = mixed[2 * j + h]
                    part = whole[0][rows]
                    for g in range(1, groups):
                        part = jnp.where(group_at[s] == g, whole[g][rows], part)
                    halves.append(part)
                out = [
                    jnp.concatenate([p[k * HALF : (k + 1) * HALF] for p in halves], axis=0)
                    for k in range(per_part)
                ]
                lanes = pl.ds(pl.multiple_of(part_at[s] * width, width), width)
                out_ref[at, lanes] = jnp.concatenate(out, axis=1).astype(jnp.bfloat16)


def attend(me, base, new_key, new_value, cache_keys, cache_values, lengths, deltas):
    requests, columns = base.shape
    kv = new_key.shape[1]
    slots = cache_keys.shape[1]
    lengths = jnp.tile(lengths.reshape(requests // HALF, HALF), (1, columns // HEAD))
    block = STEP * BATCH
    rows2 = lambda a: pl.BlockSpec((block,) + a.shape[1:], lambda i: (i,) + (0,) * (a.ndim - 1))
    arrays = [base, new_key, new_value, cache_keys, cache_values, *deltas]
    return pl.pallas_call(
        functools.partial(attend_kernel, len(deltas)),
        out_shape=jax.ShapeDtypeStruct((requests, columns), jnp.bfloat16),
        grid=(requests // block,),
        in_specs=[SMEM, whole(lengths), *map(rows2, arrays)],
        out_specs=rows2(base),
        cost_estimate=pl.CostEstimate(
            flops=4 * requests * HALF * slots * columns,
            bytes_accessed=4 * requests * (columns + slots * kv),
            transcendentals=requests * slots * columns // 16,
        ),
    )(me, lengths, *arrays)


def whole(array):
    return pl.BlockSpec(array.shape, lambda *_: (0,) * len(array.shape))


def in_chunks(factors):
    chunk = [math.gcd(f.shape[0], 4) for f in factors]
    return factors[0].shape[0] // chunk[0], [
        pl.BlockSpec((c,) + f.shape[1:], lambda i: (i, 0, 0)) for c, f in zip(chunk, factors)
    ]


def shrink_rows(ids, rows, factors):
    parts, requests = len(rows), rows[0].shape[0]
    steps, specs = in_chunks(factors)
    out = jax.ShapeDtypeStruct((parts // 2 * requests, LANES), jnp.float32)
    return pl.pallas_call(
        functools.partial(shrink_kernel, parts),
        out_shape=out,
        grid=(steps,),
        in_specs=[SMEM, *map(whole, rows), *specs],
        out_specs=whole(out),
        compiler_params=PARAMS,
    )(ids, *rows, *factors)


def expand_rows(ids, rows, lows, factors, outputs):
    parts, requests = len(rows), rows[0].shape[0]
    steps, specs = in_chunks(factors)
    last_lanes = rows[0].shape[1] // LANES - 1
    owners = pl.BlockSpec((requests, LANES), lambda i: (0, last_lanes))
    out = jax.ShapeDtypeStruct((requests, outputs), jnp.bfloat16)
    return pl.pallas_call(
        functools.partial(expand_kernel, parts),
        out_shape=[out] * parts,
        grid=(steps,),
        in_specs=[SMEM] + [owners] * parts + [*map(whole, lows), *specs],
        out_specs=[whole(out)] * parts,
        scratch_shapes=[pltpu.VMEM((parts, requests, outputs), jnp.float32)],
        compiler_params=PARAMS,
    )(ids, *rows, *lows, *factors)


def per_device(
    hidden,
    adapter_ids,
    owner_map,
    shrink_factors,
    expand_factors,
    query_base,
    new_key,
    new_value,
    cache_keys,
    cache_values,
    lengths,
):
    reps, levels, sides, tp = (lax.axis_size(a) for a in ("rep", "level", "side", "tp"))
    requests, wide = hidden.shape
    rank = shrink_factors.shape[2]
    square = reps * sides
    features, outputs = wide // square, query_base.shape[1] // square
    level, side = lax.axis_index("level"), lax.axis_index("side")
    me = lax.axis_index("rep") * sides + side

    def swap(a, s):
        pairs = [(c, c ^ s) for c in range(square)]
        return lax.ppermute(a, ("rep", "side"), pairs)

    block = (rank, features + outputs)
    own, other = pl.pallas_call(
        functools.partial(factor_kernel, square),
        out_shape=[jax.ShapeDtypeStruct((k,) + block, jnp.bfloat16) for k in (levels, 1)],
        in_specs=[SMEM, HBM, HBM],
        out_specs=[VMEM] * 2,
        scratch_shapes=[pltpu.SemaphoreType.DMA((2 * levels + 2,))],
    )(me[None], shrink_factors.swapaxes(1, 2), expand_factors)
    own = lax.all_to_all(own, "level", split_axis=0, concat_axis=0, tiled=True)
    other = swap(other, 1)
    rows = pl.pallas_call(
        functools.partial(row_kernel, square),
        out_shape=[jax.ShapeDtypeStruct((requests, features + LANES), jnp.bfloat16)] * square,
        in_specs=[SMEM, SMEM, VMEM, HBM],
        out_specs=[VMEM] * square,
        scratch_shapes=[pltpu.SemaphoreType.DMA((square,))],
    )(me[None], owner_map, adapter_ids.T, hidden)
    rows = [rows[0]] + [swap(rows[s], s) for s in range(1, square)]
    order = jnp.arange(levels, dtype=jnp.int32)
    if levels == 4:
        pairs = [[(i, i ^ k) for i in range(levels)] for k in range(levels)]
        other = [other] + [lax.ppermute(other, "level", pairs[k]) for k in range(1, levels)]
        other_at = level ^ order
    else:
        other = jnp.broadcast_to(other, (levels,) + block)
        other = [lax.all_to_all(other, "level", split_axis=0, concat_axis=0, tiled=True)]
        other_at = order
    factors = [own, *other]
    ids = [a.reshape(-1, 4) for a in (order * sides + side, other_at * sides + (side ^ 1))]
    ids = jnp.concatenate(ids, axis=1).reshape(-1)

    partial = shrink_rows(ids, rows, factors)
    for c in range(1, tp):
        partial = partial + lax.ppermute(partial, "tp", [(t, t ^ c) for t in range(tp)])
    partial = partial.astype(jnp.bfloat16)
    lows = [partial] + [swap(partial, s) for s in range(1, square)]
    deltas = expand_rows(ids, rows, lows, factors, outputs)
    deltas = [deltas[0]] + [swap(deltas[s], s) for s in range(1, square)]
    return attend(
        me[None], query_base, new_key, new_value, cache_keys, cache_values, lengths, deltas
    )


def solution(mesh):
    reps, pool, tp = (mesh.shape[a] for a in ("rep", "pool", "tp"))
    finer = Mesh(mesh.devices.reshape(reps, pool // 2, 2, tp), ("rep", "level", "side", "tp"))
    pooled = ("level", "side")
    requests = ("rep", "level", "side")
    in_specs = (
        P(requests, "tp"),
        P(requests, None),
        P(),
        P(pooled, "tp", None),
        P(pooled, None, "tp"),
        P(requests, "tp"),
        P(requests, "tp"),
        P(requests, "tp"),
        P(requests, None, "tp"),
        P(requests, None, "tp"),
        P(requests),
    )
    return jax.shard_map(
        per_device, mesh=finer, in_specs=in_specs, out_specs=P(requests, "tp"), check_vma=False
    )
```

```python
import functools
import math

import jax
import jax.numpy as jnp
from jax import lax
from jax.experimental import pallas as pl
from jax.experimental.pallas import tpu as pltpu
from jax.sharding import Mesh
from jax.sharding import PartitionSpec as P

HEAD = 128
LANES = 128
STEP = 16
HALF = 8
BATCH = 2
DEAD = -1e30
VMEM = pl.BlockSpec(memory_space=pltpu.VMEM)
SMEM = pl.BlockSpec(memory_space=pltpu.SMEM)
HBM = pl.BlockSpec(memory_space=pltpu.HBM)
PARAMS = pltpu.CompilerParams(vmem_limit_bytes=12 * 1024 * 1024)
NT = (((1,), (1,)), ((), ()))
TN = (((0,), (0,)), ((), ()))


def columns(at, width):
    return pl.ds(pl.multiple_of(at * width, width), width)


def run_copies(moves, sems, meanwhile=None):
    copies = [pltpu.make_async_copy(src, dst, sems.at[k]) for k, (src, dst) in enumerate(moves)]
    for copy in copies:
        copy.start()
    if meanwhile is not None:
        meanwhile()
    for copy in copies:
        copy.wait()


def factor_kernel(parts, me_ref, shrink_ref, expand_ref, own_ref, expand_own_ref, other_ref, sems):
    features, outputs = shrink_ref.shape[2] // parts, expand_ref.shape[2] // parts
    me = me_ref[0]
    moves = [
        (shrink_ref.at[:, :, columns(me ^ 1, features)], other_ref.at[:, :, :features]),
        (expand_ref.at[:, :, columns(me ^ 1, outputs)], other_ref.at[:, :, features:]),
        (expand_ref.at[:, :, columns(me, outputs)], expand_own_ref),
    ]
    share = shrink_ref.at[0, :, columns(me, features)]
    moves += [(share, own_ref.at[k]) for k in range(own_ref.shape[0])]
    run_copies(moves, sems)


def row_kernel(parts, me_ref, map_ref, ids_ref, hidden_ref, *refs):
    out_refs, sems = refs[:parts], refs[parts]
    requests, wide = hidden_ref.shape
    features = wide // parts
    moves = [
        (hidden_ref.at[:, columns(me_ref[0] ^ s, features)], out_refs[s].at[:, :features])
        for s in range(parts)
    ]

    def owners():
        ids = ids_ref[...]

        def look(k, found):
            return jnp.where(ids == k, map_ref[k], found)

        found = lax.fori_loop(0, map_ref.shape[0], look, jnp.zeros_like(ids))
        found = jnp.broadcast_to(found.astype(jnp.float32), (LANES, requests)).T
        for s in range(parts):
            out_refs[s][:, features:] = found.astype(jnp.bfloat16)

    run_copies(moves, sems, owners)


def owner_mask(owners, ids, rank):
    lane = lax.broadcasted_iota(jnp.int32, (1, len(ids) * rank), 1) // rank
    named = jnp.full_like(lane, -1)
    for k, owner in enumerate(ids):
        named = jnp.where(lane == k, owner, named)
    owners = owners.astype(jnp.float32).astype(jnp.int32)
    return jnp.concatenate([owners] * (len(ids) * rank // LANES), axis=1) == named


def stacked(refs):
    return jnp.concatenate([r[k] for r in refs for k in range(r.shape[0])], axis=0)


def step_ids(ids_ref, refs):
    count = sum(r.shape[0] for r in refs)
    return [ids_ref[pl.program_id(0) * count + k] for k in range(count)]


def shrink_kernel(parts, ids_ref, *refs):
    row_refs, factor_refs, out_ref = refs[:parts], refs[parts:-1], refs[-1]
    rank = factor_refs[0].shape[1]
    requests, features = row_refs[0].shape[0], row_refs[0].shape[1] - LANES
    ids = step_ids(ids_ref, factor_refs)
    weight = stacked(factor_refs)
    low = lax.broadcasted_iota(jnp.int32, (requests, LANES), 1) < rank
    folded = []
    for ref in row_refs:
        sums = lax.dot_general(
            ref[:, :features], weight, NT, preferred_element_type=jnp.float32
        )
        sums = jnp.where(owner_mask(ref[:, features:], ids, rank), sums, 0.0)
        total = sums[:, :LANES]
        for k in range(1, len(ids) * rank // LANES):
            total = total + sums[:, k * LANES : (k + 1) * LANES]
        folded.append(total + pltpu.roll(total, rank, 1))

    @pl.when(pl.program_id(0) == 0)
    def _():
        out_ref[...] = jnp.zeros_like(out_ref)

    half = parts // 2
    for s in range(half):
        rows = pl.ds(s * requests, requests)
        out_ref[rows, :] += jnp.where(low, folded[s], folded[s + half])


def expand_kernel(parts, ids_ref, *refs):
    owner_refs, low_refs, factor_refs = refs[:parts], refs[parts : 2 * parts], refs[2 * parts : -parts - 1]
    out_refs, total_ref = refs[-parts - 1 : -1], refs[-1]
    rank, outputs = factor_refs[0].shape[1:]
    requests = out_refs[0].shape[0]
    step, last = pl.program_id(0), pl.num_programs(0) - 1
    ids = step_ids(ids_ref, factor_refs)
    weight = stacked(factor_refs)
    half = parts // 2
    low = lax.broadcasted_iota(jnp.int32, (requests, LANES), 1) < rank
    held = [[0.0] * half for _ in range(2)]
    for t in range(parts):
        sums = low_refs[t][...].astype(jnp.float32)
        for s in range(half):
            at = (s ^ t) % half
            piece = sums[at * requests : (at + 1) * requests]
            held[t // half][s] = held[t // half][s] + piece
    for s in range(half):
        straight = held[0][s] + pltpu.roll(held[1][s], rank, 1)
        turned = pltpu.roll(straight, rank, 1)
        for part in (s, s + half):
            first, other = (straight, turned) if part < half else (turned, straight)
            both = jnp.where(low, first, other)
            wide = jnp.concatenate([both] * (len(ids) * rank // LANES), axis=1)
            wide = jnp.where(owner_mask(owner_refs[part][...], ids, rank), wide, 0.0)
            product = jnp.dot(
                wide.astype(jnp.bfloat16), weight, preferred_element_type=jnp.float32
            )

            @pl.when(step == 0)
            def _():
                total_ref[part] = product

            @pl.when(step > 0)
            def _():
                total_ref[part] += product

            @pl.when(step == last)
            def _():
                out_refs[part][...] = total_ref[part].astype(jnp.bfloat16)


def attend_kernel(first, parts, me_ref, len_ref, base_ref, nk_ref, nv_ref, ck_ref, cv_ref, *refs):
    delta_refs, out_ref = refs[:parts], refs[-1]
    block = base_ref.shape[0]
    width = base_ref.shape[1] // parts
    slots = ck_ref.shape[1]
    per_part = width // HEAD
    sets = STEP // HALF
    span = parts * per_part * STEP
    set_span = span // sets
    keys_in = HALF * slots + STEP
    row = lax.broadcasted_iota(jnp.int32, (keys_in, span), 0)
    lane = lax.broadcasted_iota(jnp.int32, (keys_in, span), 1)
    lane_req = lane % HALF
    lane_set = lane // set_span
    own = row - HALF * slots
    cached = jnp.where(row // slots == lane_req, row % slots, slots)
    fresh = jnp.where(own == lane_req + lane_set * HALF, -1, slots)
    slot_of = jnp.where(own >= 0, fresh, cached)
    lane_set = lax.broadcasted_iota(jnp.int32, (1, span), 1) // set_span
    part_at = [(me_ref[0] ^ (first + s)) % parts for s in range(parts)]
    scale = 1.0 / math.sqrt(HEAD)
    step = pl.program_id(0)
    units = range(block // STEP)

    def rows_of(j):
        return pl.ds(j * STEP, STEP)

    def keys_of(cache_ref, fresh_ref, j, h):
        cache = cache_ref[pl.ds(j * STEP + h * HALF, HALF)].reshape(HALF * slots, HEAD)
        return jnp.concatenate([cache, fresh_ref[rows_of(j), :]], axis=0)

    scores = []
    for j in units:
        pieces = []
        for s in range(parts):
            q = base_ref[rows_of(j), columns(part_at[s], width)].astype(jnp.float32)
            q = q + delta_refs[s][rows_of(j), :].astype(jnp.float32)
            pieces += [q[:, k * HEAD : (k + 1) * HEAD] for k in range(per_part)]
        q = jnp.concatenate(
            [p[h * HALF : (h + 1) * HALF] for h in range(sets) for p in pieces], axis=0
        ).astype(jnp.bfloat16)
        score = None
        for h in range(sets):
            keys = keys_of(ck_ref, nk_ref, j, h)
            whole_score = lax.dot_general(keys, q, NT, preferred_element_type=jnp.float32)
            score = whole_score if h == 0 else jnp.where(lane_set == h, whole_score, score)
        scores.append(score)
    probs = []
    for j, score in zip(units, scores):
        lens = len_ref[pl.ds(step * (block // STEP) + j, 1), :]
        score = jnp.where(slot_of < lens, score, DEAD)
        top = jnp.max(score, axis=0, keepdims=True)
        exps = jnp.exp((score - top) * scale)
        total = jnp.sum(exps, axis=0, keepdims=True)
        probs.append((exps * (1.0 / total)).astype(jnp.bfloat16))
    for j, prob in zip(units, probs):
        mixed = []
        for h in range(sets):
            values = keys_of(cv_ref, nv_ref, j, h)
            got = lax.dot_general(prob, values, TN, preferred_element_type=jnp.float32)
            mixed.append(got[h * set_span : (h + 1) * set_span])
        for s in range(parts):
            out = []
            for k in range(per_part):
                at = (s * per_part + k) * HALF
                out.append(jnp.concatenate([m[at : at + HALF] for m in mixed], axis=0))
            out = jnp.concatenate(out, axis=1).astype(jnp.bfloat16)
            out_ref[rows_of(j), columns(part_at[s], width)] = out


def attend_half(first, me, base, new_key, new_value, cache_keys, cache_values, lengths, deltas, out):
    requests, columns = base.shape
    slots, kv = cache_keys.shape[1:]
    groups = kv // HEAD
    parts = len(deltas)
    block = STEP * BATCH
    group = lambda me: (me[0] ^ first) // parts
    wide = pl.BlockSpec((block, columns // groups), lambda i, me: (i, group(me)))
    fresh = pl.BlockSpec((block, HEAD), lambda i, me: (i, group(me)))
    cache = pl.BlockSpec((block, slots, HEAD), lambda i, me: (i, 0, group(me)))
    part = pl.BlockSpec((block, columns // groups // parts), lambda i, me: (i, 0))
    table = pl.BlockSpec(lengths.shape, lambda i, me: (0, 0))
    earlier = [] if out is None else [out]
    return pl.pallas_call(
        functools.partial(attend_kernel, first, parts),
        out_shape=jax.ShapeDtypeStruct((requests, columns), jnp.bfloat16),
        grid_spec=pltpu.PrefetchScalarGridSpec(
            num_scalar_prefetch=1,
            grid=(requests // block,),
            in_specs=[table, wide, fresh, fresh, cache, cache]
            + [part] * parts
            + [pl.BlockSpec(memory_space=pl.ANY)] * len(earlier),
            out_specs=wide,
        ),
        input_output_aliases={7 + parts: 0} if earlier else {},
        cost_estimate=pl.CostEstimate(
            flops=4 * requests * HALF * slots * columns // groups,
            bytes_accessed=4 * requests * (columns + slots * kv) // groups,
            transcendentals=requests * slots * columns // 16 // groups,
        ),
    )(me, lengths, base, new_key, new_value, cache_keys, cache_values, *deltas, *earlier)


def attend(me, base, new_key, new_value, cache_keys, cache_values, lengths, deltas):
    groups = new_key.shape[1] // HEAD
    heads = base.shape[1] // groups // HEAD
    lengths = lengths.reshape(-1, STEP // HALF, 1, HALF)
    lengths = jnp.broadcast_to(lengths, lengths.shape[:2] + (heads, HALF)).reshape(-1, heads * STEP)
    parts = len(deltas) // groups
    out = None
    for first in range(0, len(deltas), parts):
        mine = deltas[first : first + parts]
        arrays = (base, new_key, new_value, cache_keys, cache_values)
        out = attend_half(first, me, *arrays, lengths, mine, out)
    return out


def whole(array):
    return pl.BlockSpec(array.shape, lambda *_: (0,) * len(array.shape))


def in_chunks(factors, most):
    chunk = [math.gcd(f.shape[0], most) for f in factors]
    return factors[0].shape[0] // chunk[0], [
        pl.BlockSpec((c,) + f.shape[1:], lambda i: (i, 0, 0)) for c, f in zip(chunk, factors)
    ]


def shrink_rows(ids, rows, factors):
    parts, requests = len(rows), rows[0].shape[0]
    steps, specs = in_chunks(factors, 4)
    out = jax.ShapeDtypeStruct((parts // 2 * requests, LANES), jnp.float32)
    return pl.pallas_call(
        functools.partial(shrink_kernel, parts),
        out_shape=out,
        grid=(steps,),
        in_specs=[SMEM, *map(whole, rows), *specs],
        out_specs=whole(out),
        compiler_params=PARAMS,
    )(ids, *rows, *factors)


def expand_rows(ids, rows, lows, factors):
    parts, requests, outputs = len(rows), rows[0].shape[0], factors[0].shape[2]
    steps, specs = in_chunks(factors, 8)
    last_lanes = rows[0].shape[1] // LANES - 1
    owners = pl.BlockSpec((requests, LANES), lambda i: (0, last_lanes))
    out = jax.ShapeDtypeStruct((requests, outputs), jnp.bfloat16)
    return pl.pallas_call(
        functools.partial(expand_kernel, parts),
        out_shape=[out] * parts,
        grid=(steps,),
        in_specs=[SMEM] + [owners] * parts + [*map(whole, lows), *specs],
        out_specs=[whole(out)] * parts,
        scratch_shapes=[pltpu.VMEM((parts, requests, outputs), jnp.float32)],
        compiler_params=PARAMS,
    )(ids, *rows, *lows, *factors)


def per_device(
    hidden,
    adapter_ids,
    owner_map,
    shrink_factors,
    expand_factors,
    query_base,
    new_key,
    new_value,
    cache_keys,
    cache_values,
    lengths,
):
    reps, levels, sides, tp = (lax.axis_size(a) for a in ("rep", "level", "side", "tp"))
    requests, wide = hidden.shape
    rank = shrink_factors.shape[2]
    square = reps * sides
    features, outputs = wide // square, query_base.shape[1] // square
    level, side = lax.axis_index("level"), lax.axis_index("side")
    me = lax.axis_index("rep") * sides + side

    def swap(a, s):
        pairs = [(c, c ^ s) for c in range(square)]
        return lax.ppermute(a, ("rep", "side"), pairs)

    shapes = [(levels, rank, features), (1, rank, outputs), (1, rank, features + outputs)]
    own, expand_own, other = pl.pallas_call(
        functools.partial(factor_kernel, square),
        out_shape=[jax.ShapeDtypeStruct(shape, jnp.bfloat16) for shape in shapes],
        in_specs=[SMEM, HBM, HBM],
        out_specs=[VMEM] * 3,
        scratch_shapes=[pltpu.SemaphoreType.DMA((levels + 3,))],
    )(me[None], shrink_factors.swapaxes(1, 2), expand_factors)

    def to_levels(a):
        return lax.all_to_all(a, "level", split_axis=0, concat_axis=0, tiled=True)

    own = to_levels(own)
    other = swap(other, 1)
    rows = pl.pallas_call(
        functools.partial(row_kernel, square),
        out_shape=[jax.ShapeDtypeStruct((requests, features + LANES), jnp.bfloat16)] * square,
        in_specs=[SMEM, SMEM, VMEM, HBM],
        out_specs=[VMEM] * square,
        scratch_shapes=[pltpu.SemaphoreType.DMA((square,))],
    )(me[None], owner_map, adapter_ids.T, hidden)
    *rows, other = lax.optimization_barrier((*rows, other))
    rows = [rows[0]] + [swap(rows[s], s) for s in range(1, square)]
    other, expand_next = other[:, :, :features], other[:, :, features:]
    order = jnp.arange(levels, dtype=jnp.int32)
    if levels == 4:
        pairs = [[(i, i ^ k) for i in range(levels)] for k in range(levels)]
        other = [other] + [lax.ppermute(other, "level", pairs[k]) for k in range(1, levels)]
        other_at = level ^ order
    else:
        other = [to_levels(jnp.broadcast_to(other, own.shape))]
        other_at = order
    ids = [a.reshape(-1, 4) for a in (order * sides + side, other_at * sides + (side ^ 1))]
    ids = jnp.concatenate(ids, axis=1).reshape(-1)
    expand = jnp.concatenate([expand_own, expand_next], axis=1)
    expand = jnp.broadcast_to(expand, (levels,) + expand.shape[1:])
    expand, *rows = lax.optimization_barrier((expand, *rows))
    expand = to_levels(expand).reshape(levels * sides, rank, outputs)
    expand_ids = (order[:, None] * sides + jnp.stack([side, side ^ 1])[None, :]).reshape(-1)

    partial = shrink_rows(ids, rows, [own, *other])
    for c in range(1, tp):
        partial = partial + lax.ppermute(partial, "tp", [(t, t ^ c) for t in range(tp)])
    partial = partial.astype(jnp.bfloat16)
    lows = [partial] + [swap(partial, s) for s in range(1, square)]
    deltas = expand_rows(expand_ids, rows, lows, [expand])
    deltas = [deltas[0]] + [swap(deltas[s], s) for s in range(1, square)]
    return attend(
        me[None], query_base, new_key, new_value, cache_keys, cache_values, lengths, deltas
    )


def solution(mesh):
    reps, pool, tp = (mesh.shape[a] for a in ("rep", "pool", "tp"))
    finer = Mesh(mesh.devices.reshape(reps, pool // 2, 2, tp), ("rep", "level", "side", "tp"))
    pooled = ("level", "side")
    requests = ("rep", "level", "side")
    in_specs = (
        P(requests, "tp"),
        P(requests, None),
        P(),
        P(pooled, "tp", None),
        P(pooled, None, "tp"),
        P(requests, "tp"),
        P(requests, "tp"),
        P(requests, "tp"),
        P(requests, None, "tp"),
        P(requests, None, "tp"),
        P(requests),
    )
    return jax.shard_map(
        per_device, mesh=finer, in_specs=in_specs, out_specs=P(requests, "tp"), check_vma=False
    )
```

```python
import functools
import math

import jax
import jax.numpy as jnp
from jax import lax
from jax.experimental import pallas as pl
from jax.experimental.pallas import tpu as pltpu
from jax.sharding import Mesh
from jax.sharding import PartitionSpec as P

HEAD = 128
LANES = 128
STEP = 16
HALF = 8
BATCH = 4
DEAD = -1e30
VMEM = pl.BlockSpec(memory_space=pltpu.VMEM)
SMEM = pl.BlockSpec(memory_space=pltpu.SMEM)
HBM = pl.BlockSpec(memory_space=pltpu.HBM)
PARAMS = pltpu.CompilerParams(vmem_limit_bytes=12 * 1024 * 1024)
NT = (((1,), (1,)), ((), ()))
TN = (((0,), (0,)), ((), ()))


def columns(at, width):
    return pl.ds(pl.multiple_of(at * width, width), width)


def run_copies(moves, sems, meanwhile=None):
    copies = [pltpu.make_async_copy(src, dst, sems.at[k]) for k, (src, dst) in enumerate(moves)]
    for copy in copies:
        copy.start()
    if meanwhile is not None:
        meanwhile()
    for copy in copies:
        copy.wait()


def factor_kernel(sides, me_ref, shrink_ref, expand_ref, own_ref, other_ref, expand_send_ref, sems):
    features, outputs = own_ref.shape[2], expand_send_ref.shape[2]
    levels = own_ref.shape[0]
    me = me_ref[0]
    moves = [(shrink_ref.at[:, :, columns(me ^ 1, features)], other_ref)]
    share = shrink_ref.at[0, :, columns(me, features)]
    moves += [(share, own_ref.at[k]) for k in range(levels)]
    for side in range(sides):
        share = expand_ref.at[0, :, columns(me // sides * sides + side, outputs)]
        moves += [(share, expand_send_ref.at[k * sides + side]) for k in range(levels)]
    run_copies(moves, sems)


def row_kernel(parts, me_ref, map_ref, ids_ref, hidden_ref, *refs):
    out_refs, sems = refs[:parts], refs[parts]
    requests, wide = hidden_ref.shape
    features = wide // parts
    moves = [
        (hidden_ref.at[:, columns(me_ref[0] ^ s, features)], out_refs[s].at[:, :features])
        for s in range(parts)
    ]

    def owners():
        ids = ids_ref[...]

        def look(k, found):
            return jnp.where(ids == k, map_ref[k], found)

        found = lax.fori_loop(0, map_ref.shape[0], look, jnp.zeros_like(ids))
        found = jnp.broadcast_to(found.astype(jnp.float32), (LANES, requests)).T
        for s in range(parts):
            out_refs[s][:, features:] = found.astype(jnp.bfloat16)

    run_copies(moves, sems, owners)


def owner_mask(owners, ids, rank):
    lane = lax.broadcasted_iota(jnp.int32, (1, len(ids) * rank), 1) // rank
    named = jnp.full_like(lane, -1)
    for k, owner in enumerate(ids):
        named = jnp.where(lane == k, owner, named)
    owners = owners.astype(jnp.float32).astype(jnp.int32)
    return jnp.concatenate([owners] * (len(ids) * rank // LANES), axis=1) == named


def stacked(refs):
    return jnp.concatenate([r[k] for r in refs for k in range(r.shape[0])], axis=0)


def step_ids(ids_ref, refs):
    count = sum(r.shape[0] for r in refs)
    return [ids_ref[pl.program_id(0) * count + k] for k in range(count)]


def shrink_kernel(parts, ids_ref, *refs):
    row_refs, factor_refs, out_ref = refs[:parts], refs[parts:-1], refs[-1]
    rank = factor_refs[0].shape[1]
    requests, features = row_refs[0].shape[0], row_refs[0].shape[1] - LANES
    ids = step_ids(ids_ref, factor_refs)
    weight = stacked(factor_refs)
    low = lax.broadcasted_iota(jnp.int32, (requests, LANES), 1) < rank
    folded = []
    for ref in row_refs:
        sums = lax.dot_general(
            ref[:, :features], weight, NT, preferred_element_type=jnp.float32
        )
        sums = jnp.where(owner_mask(ref[:, features:], ids, rank), sums, 0.0)
        total = sums[:, :LANES]
        for k in range(1, len(ids) * rank // LANES):
            total = total + sums[:, k * LANES : (k + 1) * LANES]
        folded.append(total + pltpu.roll(total, rank, 1))

    @pl.when(pl.program_id(0) == 0)
    def _():
        out_ref[...] = jnp.zeros_like(out_ref)

    half = parts // 2
    for s in range(half):
        rows = pl.ds(s * requests, requests)
        out_ref[rows, :] += jnp.where(low, folded[s], folded[s + half])


def expand_kernel(parts, ids_ref, *refs):
    owner_refs, low_refs, factor_refs = refs[:parts], refs[parts : 2 * parts], refs[2 * parts : -parts - 1]
    out_refs, total_ref = refs[-parts - 1 : -1], refs[-1]
    rank, outputs = factor_refs[0].shape[1:]
    requests = out_refs[0].shape[0]
    step, last = pl.program_id(0), pl.num_programs(0) - 1
    ids = step_ids(ids_ref, factor_refs)
    weight = stacked(factor_refs)
    half = parts // 2
    low = lax.broadcasted_iota(jnp.int32, (requests, LANES), 1) < rank
    held = [[0.0] * half for _ in range(2)]
    for t in range(parts):
        sums = low_refs[t][...].astype(jnp.float32)
        for s in range(half):
            at = (s ^ t) % half
            piece = sums[at * requests : (at + 1) * requests]
            held[t // half][s] = held[t // half][s] + piece
    for s in range(half):
        straight = held[0][s] + pltpu.roll(held[1][s], rank, 1)
        turned = pltpu.roll(straight, rank, 1)
        for part in (s, s + half):
            first, other = (straight, turned) if part < half else (turned, straight)
            both = jnp.where(low, first, other)
            wide = jnp.concatenate([both] * (len(ids) * rank // LANES), axis=1)
            wide = jnp.where(owner_mask(owner_refs[part][...], ids, rank), wide, 0.0)
            product = jnp.dot(
                wide.astype(jnp.bfloat16), weight, preferred_element_type=jnp.float32
            )

            @pl.when(step == 0)
            def _():
                total_ref[part] = product

            @pl.when(step > 0)
            def _():
                total_ref[part] += product

            @pl.when(step == last)
            def _():
                out_refs[part][...] = total_ref[part].astype(jnp.bfloat16)


def attend_kernel(first, parts, me_ref, len_ref, base_ref, nk_ref, nv_ref, ck_ref, cv_ref, *refs):
    delta_refs, out_ref = refs[:parts], refs[-1]
    block = base_ref.shape[0]
    width = base_ref.shape[1] // parts
    slots = ck_ref.shape[1]
    per_part = width // HEAD
    sets = STEP // HALF
    span = parts * per_part * STEP
    set_span = span // sets
    keys_in = HALF * slots + STEP
    row = lax.broadcasted_iota(jnp.int32, (keys_in, span), 0)
    lane = lax.broadcasted_iota(jnp.int32, (keys_in, span), 1)
    lane_req = lane % HALF
    lane_set = lane // set_span
    own = row - HALF * slots
    cached = jnp.where(row // slots == lane_req, row % slots, slots)
    fresh = jnp.where(own == lane_req + lane_set * HALF, -1, slots)
    slot_of = jnp.where(own >= 0, fresh, cached)
    lane_set = lax.broadcasted_iota(jnp.int32, (1, span), 1) // set_span
    part_at = [(me_ref[0] ^ (first + s)) % parts for s in range(parts)]
    scale = 1.0 / math.sqrt(HEAD)
    step = pl.program_id(0)
    units = range(block // STEP)

    def rows_of(j):
        return pl.ds(j * STEP, STEP)

    def keys_of(cache_ref, fresh_ref, j, h):
        cache = cache_ref[pl.ds(j * STEP + h * HALF, HALF)].reshape(HALF * slots, HEAD)
        return jnp.concatenate([cache, fresh_ref[rows_of(j), :]], axis=0)

    scores = []
    for j in units:
        pieces = []
        for s in range(parts):
            q = base_ref[rows_of(j), columns(part_at[s], width)].astype(jnp.float32)
            q = q + delta_refs[s][rows_of(j), :].astype(jnp.float32)
            pieces += [q[:, k * HEAD : (k + 1) * HEAD] for k in range(per_part)]
        q = jnp.concatenate(
            [p[h * HALF : (h + 1) * HALF] for h in range(sets) for p in pieces], axis=0
        ).astype(jnp.bfloat16)
        score = None
        for h in range(sets):
            keys = keys_of(ck_ref, nk_ref, j, h)
            whole_score = lax.dot_general(keys, q, NT, preferred_element_type=jnp.float32)
            score = whole_score if h == 0 else jnp.where(lane_set == h, whole_score, score)
        scores.append(score)
    probs = []
    for j, score in zip(units, scores):
        lens = len_ref[pl.ds(step * (block // STEP) + j, 1), :]
        score = jnp.where(slot_of < lens, score, DEAD)
        top = jnp.max(score, axis=0, keepdims=True)
        exps = jnp.exp((score - top) * scale)
        total = jnp.sum(exps, axis=0, keepdims=True)
        probs.append((exps * (1.0 / total)).astype(jnp.bfloat16))
    for j, prob in zip(units, probs):
        mixed = []
        for h in range(sets):
            values = keys_of(cv_ref, nv_ref, j, h)
            got = lax.dot_general(prob, values, TN, preferred_element_type=jnp.float32)
            mixed.append(got[h * set_span : (h + 1) * set_span])
        for s in range(parts):
            out = []
            for k in range(per_part):
                at = (s * per_part + k) * HALF
                out.append(jnp.concatenate([m[at : at + HALF] for m in mixed], axis=0))
            out = jnp.concatenate(out, axis=1).astype(jnp.bfloat16)
            out_ref[rows_of(j), columns(part_at[s], width)] = out


def attend_half(first, me, base, new_key, new_value, cache_keys, cache_values, lengths, deltas, out):
    requests, columns = base.shape
    slots, kv = cache_keys.shape[1:]
    groups = kv // HEAD
    parts = len(deltas)
    block = STEP * BATCH
    group = lambda me: (me[0] ^ first) // parts
    wide = pl.BlockSpec((block, columns // groups), lambda i, me: (i, group(me)))
    fresh = pl.BlockSpec((block, HEAD), lambda i, me: (i, group(me)))
    cache = pl.BlockSpec((block, slots, HEAD), lambda i, me: (i, 0, group(me)))
    part = pl.BlockSpec((block, columns // groups // parts), lambda i, me: (i, 0))
    table = pl.BlockSpec(lengths.shape, lambda i, me: (0, 0))
    earlier = [] if out is None else [out]
    return pl.pallas_call(
        functools.partial(attend_kernel, first, parts),
        out_shape=jax.ShapeDtypeStruct((requests, columns), jnp.bfloat16),
        grid_spec=pltpu.PrefetchScalarGridSpec(
            num_scalar_prefetch=1,
            grid=(requests // block,),
            in_specs=[table, wide, fresh, fresh, cache, cache]
            + [part] * parts
            + [pl.BlockSpec(memory_space=pl.ANY)] * len(earlier),
            out_specs=wide,
        ),
        input_output_aliases={7 + parts: 0} if earlier else {},
        cost_estimate=pl.CostEstimate(
            flops=4 * requests * HALF * slots * columns // groups,
            bytes_accessed=4 * requests * (columns + slots * kv) // groups,
            transcendentals=requests * slots * columns // 16 // groups,
        ),
    )(me, lengths, base, new_key, new_value, cache_keys, cache_values, *deltas, *earlier)


def length_table(lengths, heads):
    lengths = lengths.reshape(-1, STEP // HALF, 1, HALF)
    lengths = jnp.broadcast_to(lengths, lengths.shape[:2] + (heads, HALF))
    return lengths.reshape(-1, heads * STEP)


def attend(me, base, new_key, new_value, cache_keys, cache_values, lengths, deltas):
    groups = new_key.shape[1] // HEAD
    parts = len(deltas) // groups
    out = None
    for first in range(0, len(deltas), parts):
        mine = deltas[first : first + parts]
        arrays = (base, new_key, new_value, cache_keys, cache_values)
        out = attend_half(first, me, *arrays, lengths, mine, out)
    return out


def whole(array):
    return pl.BlockSpec(array.shape, lambda *_: (0,) * len(array.shape))


def in_chunks(factors, most):
    chunk = [math.gcd(f.shape[0], most) for f in factors]
    return factors[0].shape[0] // chunk[0], [
        pl.BlockSpec((c,) + f.shape[1:], lambda i: (i, 0, 0)) for c, f in zip(chunk, factors)
    ]


def shrink_rows(ids, rows, factors):
    parts, requests = len(rows), rows[0].shape[0]
    steps, specs = in_chunks(factors, 4)
    out = jax.ShapeDtypeStruct((parts // 2 * requests, LANES), jnp.float32)
    return pl.pallas_call(
        functools.partial(shrink_kernel, parts),
        out_shape=out,
        grid=(steps,),
        in_specs=[SMEM, *map(whole, rows), *specs],
        out_specs=whole(out),
        compiler_params=PARAMS,
    )(ids, *rows, *factors)


def expand_rows(ids, rows, lows, factors):
    parts, requests, outputs = len(rows), rows[0].shape[0], factors[0].shape[2]
    steps, specs = in_chunks(factors, 8)
    last_lanes = rows[0].shape[1] // LANES - 1
    owners = pl.BlockSpec((requests, LANES), lambda i: (0, last_lanes))
    out = jax.ShapeDtypeStruct((requests, outputs), jnp.bfloat16)
    return pl.pallas_call(
        functools.partial(expand_kernel, parts),
        out_shape=[out] * parts,
        grid=(steps,),
        in_specs=[SMEM] + [owners] * parts + [*map(whole, lows), *specs],
        out_specs=[whole(out)] * parts,
        scratch_shapes=[pltpu.VMEM((parts, requests, outputs), jnp.float32)],
        compiler_params=PARAMS,
    )(ids, *rows, *lows, *factors)


def per_device(
    hidden,
    adapter_ids,
    owner_map,
    shrink_factors,
    expand_factors,
    query_base,
    new_key,
    new_value,
    cache_keys,
    cache_values,
    lengths,
):
    reps, levels, sides, tp = (lax.axis_size(a) for a in ("rep", "level", "side", "tp"))
    requests, wide = hidden.shape
    rank = shrink_factors.shape[2]
    square = reps * sides
    features, outputs = wide // square, query_base.shape[1] // square
    level, side = lax.axis_index("level"), lax.axis_index("side")
    me = lax.axis_index("rep") * sides + side

    def swap(a, s):
        pairs = [(c, c ^ s) for c in range(square)]
        return lax.ppermute(a, ("rep", "side"), pairs)

    shapes = [(levels, rank, features), (1, rank, features), (levels * sides, rank, outputs)]
    own, other, expand = pl.pallas_call(
        functools.partial(factor_kernel, sides),
        out_shape=[jax.ShapeDtypeStruct(shape, jnp.bfloat16) for shape in shapes],
        in_specs=[SMEM, HBM, HBM],
        out_specs=[VMEM] * 3,
        scratch_shapes=[pltpu.SemaphoreType.DMA((levels * (sides + 1) + 1,))],
    )(me[None], shrink_factors.swapaxes(1, 2), expand_factors)

    def to_levels(a):
        return lax.all_to_all(a, "level", split_axis=0, concat_axis=0, tiled=True)

    own = to_levels(own)
    other = swap(other, 1)
    rows = pl.pallas_call(
        functools.partial(row_kernel, square),
        out_shape=[jax.ShapeDtypeStruct((requests, features + LANES), jnp.bfloat16)] * square,
        in_specs=[SMEM, SMEM, VMEM, HBM],
        out_specs=[VMEM] * square,
        scratch_shapes=[pltpu.SemaphoreType.DMA((square,))],
    )(me[None], owner_map, adapter_ids.T, hidden)
    table = length_table(lengths, outputs * square // new_key.shape[1])
    *rows, other, table = lax.optimization_barrier((*rows, other, table))
    rows = [rows[0]] + [swap(rows[s], s) for s in range(1, square)]

    order = jnp.arange(levels, dtype=jnp.int32)
    if levels == 4:
        pairs = [[(i, i ^ k) for i in range(levels)] for k in range(levels)]
        other = [other] + [lax.ppermute(other, "level", pairs[k]) for k in range(1, levels)]
        other_at = level ^ order
    else:
        other = [to_levels(jnp.broadcast_to(other, own.shape))]
        other_at = order
    ids = [a.reshape(-1, 4) for a in (order * sides + side, other_at * sides + (side ^ 1))]
    ids = jnp.concatenate(ids, axis=1).reshape(-1)
    expand, *rows = lax.optimization_barrier((expand, *rows))
    pooled = ("level", "side")
    expand = lax.all_to_all(expand, pooled, split_axis=0, concat_axis=0, tiled=True)
    expand_ids = jnp.arange(levels * sides, dtype=jnp.int32)

    partial = shrink_rows(ids, rows, [own, *other])
    for c in range(1, tp):
        partial = partial + lax.ppermute(partial, "tp", [(t, t ^ c) for t in range(tp)])
    partial = partial.astype(jnp.bfloat16)
    lows = [partial] + [swap(partial, s) for s in range(1, square)]
    deltas = expand_rows(expand_ids, rows, lows, [expand])
    deltas = [deltas[0]] + [swap(deltas[s], s) for s in range(1, square)]
    return attend(
        me[None], query_base, new_key, new_value, cache_keys, cache_values, table, deltas
    )


def solution(mesh):
    reps, pool, tp = (mesh.shape[a] for a in ("rep", "pool", "tp"))
    finer = Mesh(mesh.devices.reshape(reps, pool // 2, 2, tp), ("rep", "level", "side", "tp"))
    pooled = ("level", "side")
    requests = ("rep", "level", "side")
    in_specs = (
        P(requests, "tp"),
        P(requests, None),
        P(),
        P(pooled, "tp", None),
        P(pooled, None, "tp"),
        P(requests, "tp"),
        P(requests, "tp"),
        P(requests, "tp"),
        P(requests, None, "tp"),
        P(requests, None, "tp"),
        P(requests),
    )
    return jax.shard_map(
        per_device, mesh=finer, in_specs=in_specs, out_specs=P(requests, "tp"), check_vma=False
    )
```

```python
import functools
import math

import jax
import jax.numpy as jnp
from jax import lax
from jax.experimental import pallas as pl
from jax.experimental.pallas import tpu as pltpu
from jax.sharding import Mesh
from jax.sharding import PartitionSpec as P

HEAD = 128
LANES = 128
STEP = 16
HALF = 8
BATCH = 4
DEAD = -1e30
VMEM = pl.BlockSpec(memory_space=pltpu.VMEM)
SMEM = pl.BlockSpec(memory_space=pltpu.SMEM)
HBM = pl.BlockSpec(memory_space=pltpu.HBM)
PARAMS = pltpu.CompilerParams(vmem_limit_bytes=12 * 1024 * 1024)
NT = (((1,), (1,)), ((), ()))
TN = (((0,), (0,)), ((), ()))


def columns(at, width):
    return pl.ds(pl.multiple_of(at * width, width), width)


def run_copies(moves, sems, meanwhile=None):
    copies = [pltpu.make_async_copy(src, dst, sems.at[k]) for k, (src, dst) in enumerate(moves)]
    for copy in copies:
        copy.start()
    if meanwhile is not None:
        meanwhile()
    for copy in copies:
        copy.wait()


def factor_kernel(sides, me_ref, shrink_ref, expand_ref, own_ref, other_ref, expand_send_ref, sems):
    features, outputs = own_ref.shape[2], expand_send_ref.shape[2]
    levels = own_ref.shape[0]
    me = me_ref[0]
    moves = [(shrink_ref.at[:, :, columns(me ^ 1, features)], other_ref)]
    share = shrink_ref.at[0, :, columns(me, features)]
    moves += [(share, own_ref.at[k]) for k in range(levels)]
    for side in range(sides):
        share = expand_ref.at[0, :, columns(me // sides * sides + side, outputs)]
        moves += [(share, expand_send_ref.at[k * sides + side]) for k in range(levels)]
    run_copies(moves, sems)


def row_kernel(parts, me_ref, map_ref, ids_ref, hidden_ref, *refs):
    out_refs, sems = refs[:parts], refs[parts]
    requests, wide = hidden_ref.shape
    features = wide // parts
    moves = [
        (hidden_ref.at[:, columns(me_ref[0] ^ s, features)], out_refs[s].at[:, :features])
        for s in range(parts)
    ]

    def owners():
        ids = ids_ref[...]

        def look(k, found):
            return jnp.where(ids == k, map_ref[k], found)

        found = lax.fori_loop(0, map_ref.shape[0], look, jnp.zeros_like(ids))
        found = jnp.broadcast_to(found.astype(jnp.float32), (LANES, requests)).T
        for s in range(parts):
            out_refs[s][:, features:] = found.astype(jnp.bfloat16)

    run_copies(moves, sems, owners)


def owner_mask(owners, ids, rank):
    lane = lax.broadcasted_iota(jnp.int32, (1, len(ids) * rank), 1) // rank
    named = jnp.full_like(lane, -1)
    for k, owner in enumerate(ids):
        named = jnp.where(lane == k, owner, named)
    owners = owners.astype(jnp.float32).astype(jnp.int32)
    return jnp.concatenate([owners] * (len(ids) * rank // LANES), axis=1) == named


def stacked(refs):
    return jnp.concatenate([r[k] for r in refs for k in range(r.shape[0])], axis=0)


def step_ids(ids_ref, refs):
    count = sum(r.shape[0] for r in refs)
    return [ids_ref[pl.program_id(0) * count + k] for k in range(count)]


def shrink_kernel(parts, ids_ref, *refs):
    row_refs, factor_refs, out_ref = refs[:parts], refs[parts:-1], refs[-1]
    rank = factor_refs[0].shape[1]
    requests, features = row_refs[0].shape[0], row_refs[0].shape[1] - LANES
    ids = step_ids(ids_ref, factor_refs)
    weight = stacked(factor_refs)
    low = lax.broadcasted_iota(jnp.int32, (requests, LANES), 1) < rank
    folded = []
    for ref in row_refs:
        sums = lax.dot_general(
            ref[:, :features], weight, NT, preferred_element_type=jnp.float32
        )
        sums = jnp.where(owner_mask(ref[:, features:], ids, rank), sums, 0.0)
        total = sums[:, :LANES]
        for k in range(1, len(ids) * rank // LANES):
            total = total + sums[:, k * LANES : (k + 1) * LANES]
        folded.append(total + pltpu.roll(total, rank, 1))

    @pl.when(pl.program_id(0) == 0)
    def _():
        out_ref[...] = jnp.zeros_like(out_ref)

    half = parts // 2
    for s in range(half):
        rows = pl.ds(s * requests, requests)
        out_ref[rows, :] += jnp.where(low, folded[s], folded[s + half])


def expand_kernel(parts, ids_ref, *refs):
    owner_refs, low_refs, factor_refs = refs[:parts], refs[parts : 2 * parts], refs[2 * parts : -parts - 1]
    out_refs, total_ref = refs[-parts - 1 : -1], refs[-1]
    rank, outputs = factor_refs[0].shape[1:]
    requests = out_refs[0].shape[0]
    step, last = pl.program_id(0), pl.num_programs(0) - 1
    ids = step_ids(ids_ref, factor_refs)
    weight = stacked(factor_refs)
    half = parts // 2
    low = lax.broadcasted_iota(jnp.int32, (requests, LANES), 1) < rank
    held = [[0.0] * half for _ in range(2)]
    for t in range(parts):
        sums = low_refs[t][...].astype(jnp.float32)
        for s in range(half):
            at = (s ^ t) % half
            piece = sums[at * requests : (at + 1) * requests]
            held[t // half][s] = held[t // half][s] + piece
    for s in range(half):
        straight = held[0][s] + pltpu.roll(held[1][s], rank, 1)
        turned = pltpu.roll(straight, rank, 1)
        for part in (s, s + half):
            first, other = (straight, turned) if part < half else (turned, straight)
            both = jnp.where(low, first, other)
            wide = jnp.concatenate([both] * (len(ids) * rank // LANES), axis=1)
            wide = jnp.where(owner_mask(owner_refs[part][...], ids, rank), wide, 0.0)
            product = jnp.dot(
                wide.astype(jnp.bfloat16), weight, preferred_element_type=jnp.float32
            )

            @pl.when(step == 0)
            def _():
                total_ref[part] = product

            @pl.when(step > 0)
            def _():
                total_ref[part] += product

            @pl.when(step == last)
            def _():
                out_refs[part][...] = total_ref[part].astype(jnp.bfloat16)


def attend_kernel(first, parts, me_ref, len_ref, base_ref, nk_ref, nv_ref, ck_ref, cv_ref, *refs):
    delta_refs, out_ref = refs[:parts], refs[-1]
    block = base_ref.shape[0]
    width = base_ref.shape[1] // parts
    slots = ck_ref.shape[1]
    per_part = width // HEAD
    sets = STEP // HALF
    span = parts * per_part * STEP
    set_span = span // sets
    keys_in = HALF * slots + STEP
    row = lax.broadcasted_iota(jnp.int32, (keys_in, span), 0)
    lane = lax.broadcasted_iota(jnp.int32, (keys_in, span), 1)
    lane_req = lane % HALF
    lane_set = lane // set_span
    own = row - HALF * slots
    cached = jnp.where(row // slots == lane_req, row % slots, slots)
    fresh = jnp.where(own == lane_req + lane_set * HALF, -1, slots)
    slot_of = jnp.where(own >= 0, fresh, cached)
    lane_set = lax.broadcasted_iota(jnp.int32, (1, span), 1) // set_span
    part_at = [(me_ref[0] ^ (first + s)) % parts for s in range(parts)]
    scale = 1.0 / math.sqrt(HEAD)
    step = pl.program_id(0)
    units = range(block // STEP)

    def rows_of(j):
        return pl.ds(j * STEP, STEP)

    def keys_of(cache_ref, fresh_ref, j, h):
        cache = cache_ref[pl.ds(j * STEP + h * HALF, HALF)].reshape(HALF * slots, HEAD)
        return jnp.concatenate([cache, fresh_ref[rows_of(j), :]], axis=0)

    scores = []
    for j in units:
        pieces = []
        for s in range(parts):
            q = base_ref[rows_of(j), columns(part_at[s], width)].astype(jnp.float32)
            q = q + delta_refs[s][rows_of(j), :].astype(jnp.float32)
            pieces += [q[:, k * HEAD : (k + 1) * HEAD] for k in range(per_part)]
        q = jnp.concatenate(
            [p[h * HALF : (h + 1) * HALF] for h in range(sets) for p in pieces], axis=0
        ).astype(jnp.bfloat16)
        score = None
        for h in range(sets):
            keys = keys_of(ck_ref, nk_ref, j, h)
            whole_score = lax.dot_general(keys, q, NT, preferred_element_type=jnp.float32)
            score = whole_score if h == 0 else jnp.where(lane_set == h, whole_score, score)
        scores.append(score)
    probs = []
    for j, score in zip(units, scores):
        lens = len_ref[pl.ds(step * (block // STEP) + j, 1), :]
        score = jnp.where(slot_of < lens, score, DEAD)
        top = jnp.max(score, axis=0, keepdims=True)
        exps = jnp.exp((score - top) * scale)
        total = jnp.sum(exps, axis=0, keepdims=True)
        probs.append((exps * (1.0 / total)).astype(jnp.bfloat16))
    for j, prob in zip(units, probs):
        mixed = []
        for h in range(sets):
            values = keys_of(cv_ref, nv_ref, j, h)
            got = lax.dot_general(prob, values, TN, preferred_element_type=jnp.float32)
            mixed.append(got[h * set_span : (h + 1) * set_span])
        for s in range(parts):
            out = []
            for k in range(per_part):
                at = (s * per_part + k) * HALF
                out.append(jnp.concatenate([m[at : at + HALF] for m in mixed], axis=0))
            out = jnp.concatenate(out, axis=1).astype(jnp.bfloat16)
            out_ref[rows_of(j), columns(part_at[s], width)] = out


def attend_half(first, me, base, new_key, new_value, cache_keys, cache_values, lengths, deltas, out):
    requests, columns = base.shape
    slots, kv = cache_keys.shape[1:]
    groups = kv // HEAD
    parts = len(deltas)
    block = STEP * BATCH
    group = lambda me: (me[0] ^ first) // parts
    wide = pl.BlockSpec((block, columns // groups), lambda i, me: (i, group(me)))
    fresh = pl.BlockSpec((block, HEAD), lambda i, me: (i, group(me)))
    cache = pl.BlockSpec((block, slots, HEAD), lambda i, me: (i, 0, group(me)))
    part = pl.BlockSpec((block, columns // groups // parts), lambda i, me: (i, 0))
    table = pl.BlockSpec(lengths.shape, lambda i, me: (0, 0))
    earlier = [] if out is None else [out]
    return pl.pallas_call(
        functools.partial(attend_kernel, first, parts),
        out_shape=jax.ShapeDtypeStruct((requests, columns), jnp.bfloat16),
        grid_spec=pltpu.PrefetchScalarGridSpec(
            num_scalar_prefetch=1,
            grid=(requests // block,),
            in_specs=[table, wide, fresh, fresh, cache, cache]
            + [part] * parts
            + [pl.BlockSpec(memory_space=pl.ANY)] * len(earlier),
            out_specs=wide,
        ),
        input_output_aliases={7 + parts: 0} if earlier else {},
        cost_estimate=pl.CostEstimate(
            flops=4 * requests * HALF * slots * columns // groups,
            bytes_accessed=4 * requests * (columns + slots * kv) // groups,
            transcendentals=requests * slots * columns // 16 // groups,
        ),
    )(me, lengths, base, new_key, new_value, cache_keys, cache_values, *deltas, *earlier)


def length_table(lengths, heads):
    lengths = lengths.reshape(-1, STEP // HALF, 1, HALF)
    lengths = jnp.broadcast_to(lengths, lengths.shape[:2] + (heads, HALF))
    return lengths.reshape(-1, heads * STEP)


def attend(me, base, new_key, new_value, cache_keys, cache_values, lengths, deltas):
    groups = new_key.shape[1] // HEAD
    parts = len(deltas) // groups
    out = None
    for first in range(0, len(deltas), parts):
        mine = deltas[first : first + parts]
        arrays = (base, new_key, new_value, cache_keys, cache_values)
        out = attend_half(first, me, *arrays, lengths, mine, out)
    return out


def whole(array):
    return pl.BlockSpec(array.shape, lambda *_: (0,) * len(array.shape))


def in_chunks(factors, most):
    chunk = [math.gcd(f.shape[0], most) for f in factors]
    return factors[0].shape[0] // chunk[0], [
        pl.BlockSpec((c,) + f.shape[1:], lambda i: (i, 0, 0)) for c, f in zip(chunk, factors)
    ]


def shrink_rows(ids, rows, factors):
    parts, requests = len(rows), rows[0].shape[0]
    steps, specs = in_chunks(factors, 4)
    out = jax.ShapeDtypeStruct((parts // 2 * requests, LANES), jnp.float32)
    return pl.pallas_call(
        functools.partial(shrink_kernel, parts),
        out_shape=out,
        grid=(steps,),
        in_specs=[SMEM, *map(whole, rows), *specs],
        out_specs=whole(out),
        compiler_params=PARAMS,
    )(ids, *rows, *factors)


def expand_rows(ids, rows, lows, factors):
    parts, requests, outputs = len(rows), rows[0].shape[0], factors[0].shape[2]
    steps, specs = in_chunks(factors, 8)
    last_lanes = rows[0].shape[1] // LANES - 1
    owners = pl.BlockSpec((requests, LANES), lambda i: (0, last_lanes))
    out = jax.ShapeDtypeStruct((requests, outputs), jnp.bfloat16)
    return pl.pallas_call(
        functools.partial(expand_kernel, parts),
        out_shape=[out] * parts,
        grid=(steps,),
        in_specs=[SMEM] + [owners] * parts + [*map(whole, lows), *specs],
        out_specs=[whole(out)] * parts,
        scratch_shapes=[pltpu.VMEM((parts, requests, outputs), jnp.float32)],
        compiler_params=PARAMS,
    )(ids, *rows, *lows, *factors)


def per_device(
    hidden,
    adapter_ids,
    owner_map,
    shrink_factors,
    expand_factors,
    query_base,
    new_key,
    new_value,
    cache_keys,
    cache_values,
    lengths,
):
    reps, levels, sides, tp = (lax.axis_size(a) for a in ("rep", "level", "side", "tp"))
    requests, wide = hidden.shape
    rank = shrink_factors.shape[2]
    square = reps * sides
    features, outputs = wide // square, query_base.shape[1] // square
    level, side = lax.axis_index("level"), lax.axis_index("side")
    me = lax.axis_index("rep") * sides + side

    def swap(a, s):
        pairs = [(c, c ^ s) for c in range(square)]
        return lax.ppermute(a, ("rep", "side"), pairs)

    shapes = [(levels, rank, features), (1, rank, features), (levels * sides, rank, outputs)]
    own, other, expand = pl.pallas_call(
        functools.partial(factor_kernel, sides),
        out_shape=[jax.ShapeDtypeStruct(shape, jnp.bfloat16) for shape in shapes],
        in_specs=[SMEM, HBM, HBM],
        out_specs=[VMEM] * 3,
        scratch_shapes=[pltpu.SemaphoreType.DMA((levels * (sides + 1) + 1,))],
    )(me[None], shrink_factors.swapaxes(1, 2), expand_factors)

    def to_levels(a):
        return lax.all_to_all(a, "level", split_axis=0, concat_axis=0, tiled=True)

    own = to_levels(own)
    other = swap(other, 1)
    rows = pl.pallas_call(
        functools.partial(row_kernel, square),
        out_shape=[jax.ShapeDtypeStruct((requests, features + LANES), jnp.bfloat16)] * square,
        in_specs=[SMEM, SMEM, VMEM, HBM],
        out_specs=[VMEM] * square,
        scratch_shapes=[pltpu.SemaphoreType.DMA((square,))],
    )(me[None], owner_map, adapter_ids.T, hidden)
    table = length_table(lengths, outputs * square // new_key.shape[1])
    *rows, other, table = lax.optimization_barrier((*rows, other, table))
    rows = [rows[0]] + [swap(rows[s], s) for s in range(1, square)]

    order = jnp.arange(levels, dtype=jnp.int32)
    if levels == 4:
        pairs = [[(i, i ^ k) for i in range(levels)] for k in range(levels)]
        other = [other] + [lax.ppermute(other, "level", pairs[k]) for k in range(1, levels)]
        other_at = level ^ order
    else:
        other = [to_levels(jnp.broadcast_to(other, own.shape))]
        other_at = order
    ids = [a.reshape(-1, 4) for a in (order * sides + side, other_at * sides + (side ^ 1))]
    ids = jnp.concatenate(ids, axis=1).reshape(-1)
    expand, other, rows = lax.optimization_barrier((expand, other, rows))
    pooled = ("level", "side")
    expand = lax.all_to_all(expand, pooled, split_axis=0, concat_axis=0, tiled=True)
    expand_ids = jnp.arange(levels * sides, dtype=jnp.int32)

    partial = shrink_rows(ids, rows, [own, *other])
    for c in range(1, tp):
        partial = partial + lax.ppermute(partial, "tp", [(t, t ^ c) for t in range(tp)])
    partial = partial.astype(jnp.bfloat16)
    lows = [partial] + [swap(partial, s) for s in range(1, square)]
    deltas = expand_rows(expand_ids, rows, lows, [expand])
    deltas = [deltas[0]] + [swap(deltas[s], s) for s in range(1, square)]
    return attend(
        me[None], query_base, new_key, new_value, cache_keys, cache_values, table, deltas
    )


def solution(mesh):
    reps, pool, tp = (mesh.shape[a] for a in ("rep", "pool", "tp"))
    finer = Mesh(mesh.devices.reshape(reps, pool // 2, 2, tp), ("rep", "level", "side", "tp"))
    pooled = ("level", "side")
    requests = ("rep", "level", "side")
    in_specs = (
        P(requests, "tp"),
        P(requests, None),
        P(),
        P(pooled, "tp", None),
        P(pooled, None, "tp"),
        P(requests, "tp"),
        P(requests, "tp"),
        P(requests, "tp"),
        P(requests, None, "tp"),
        P(requests, None, "tp"),
        P(requests),
    )
    return jax.shard_map(
        per_device, mesh=finer, in_specs=in_specs, out_specs=P(requests, "tp"), check_vma=False
    )
```

```python
import functools
import math

import jax
import jax.numpy as jnp
from jax import lax
from jax.experimental import pallas as pl
from jax.experimental.pallas import tpu as pltpu
from jax.sharding import Mesh
from jax.sharding import PartitionSpec as P

HEAD = 128
LANES = 128
STEP = 16
HALF = 8
BATCH = 4
DEAD = -1e30
VMEM = pl.BlockSpec(memory_space=pltpu.VMEM)
SMEM = pl.BlockSpec(memory_space=pltpu.SMEM)
HBM = pl.BlockSpec(memory_space=pltpu.HBM)
PARAMS = pltpu.CompilerParams(vmem_limit_bytes=12 * 1024 * 1024)
NT = (((1,), (1,)), ((), ()))
TN = (((0,), (0,)), ((), ()))


def columns(at, width):
    return pl.ds(pl.multiple_of(at * width, width), width)


def run_copies(moves, sems, meanwhile=None):
    copies = [pltpu.make_async_copy(src, dst, sems.at[k]) for k, (src, dst) in enumerate(moves)]
    for copy in copies:
        copy.start()
    if meanwhile is not None:
        meanwhile()
    for copy in copies:
        copy.wait()


def factor_kernel(parts, me_ref, shrink_ref, expand_ref, own_ref, expand_own_ref, other_ref, sems):
    features, outputs = shrink_ref.shape[2] // parts, expand_ref.shape[2] // parts
    me = me_ref[0]
    moves = [
        (shrink_ref.at[:, :, columns(me ^ 1, features)], other_ref.at[:, :, :features]),
        (expand_ref.at[:, :, columns(me ^ 1, outputs)], other_ref.at[:, :, features:]),
        (expand_ref.at[:, :, columns(me, outputs)], expand_own_ref),
    ]
    share = shrink_ref.at[0, :, columns(me, features)]
    moves += [(share, own_ref.at[k]) for k in range(own_ref.shape[0])]
    run_copies(moves, sems)


def row_kernel(parts, me_ref, map_ref, ids_ref, hidden_ref, *refs):
    out_refs, sems = refs[:parts], refs[parts]
    requests, wide = hidden_ref.shape
    features = wide // parts
    moves = [
        (hidden_ref.at[:, columns(me_ref[0] ^ s, features)], out_refs[s].at[:, :features])
        for s in range(parts)
    ]

    def owners():
        ids = ids_ref[...]

        def look(k, found):
            return jnp.where(ids == k, map_ref[k], found)

        found = lax.fori_loop(0, map_ref.shape[0], look, jnp.zeros_like(ids))
        found = jnp.broadcast_to(found.astype(jnp.float32), (LANES, requests)).T
        for s in range(parts):
            out_refs[s][:, features:] = found.astype(jnp.bfloat16)

    run_copies(moves, sems, owners)


def owner_mask(owners, ids, rank):
    lane = lax.broadcasted_iota(jnp.int32, (1, len(ids) * rank), 1) // rank
    named = jnp.full_like(lane, -1)
    for k, owner in enumerate(ids):
        named = jnp.where(lane == k, owner, named)
    owners = owners.astype(jnp.float32).astype(jnp.int32)
    return jnp.concatenate([owners] * (len(ids) * rank // LANES), axis=1) == named


def stacked(refs):
    return jnp.concatenate([r[k] for r in refs for k in range(r.shape[0])], axis=0)


def step_ids(ids_ref, refs):
    count = sum(r.shape[0] for r in refs)
    return [ids_ref[pl.program_id(0) * count + k] for k in range(count)]


def shrink_kernel(parts, ids_ref, *refs):
    row_refs, factor_refs, out_ref = refs[:parts], refs[parts:-1], refs[-1]
    rank = factor_refs[0].shape[1]
    requests, features = row_refs[0].shape[0], row_refs[0].shape[1] - LANES
    ids = step_ids(ids_ref, factor_refs)
    weight = stacked(factor_refs)
    low = lax.broadcasted_iota(jnp.int32, (requests, LANES), 1) < rank
    folded = []
    for ref in row_refs:
        sums = lax.dot_general(
            ref[:, :features], weight, NT, preferred_element_type=jnp.float32
        )
        sums = jnp.where(owner_mask(ref[:, features:], ids, rank), sums, 0.0)
        total = sums[:, :LANES]
        for k in range(1, len(ids) * rank // LANES):
            total = total + sums[:, k * LANES : (k + 1) * LANES]
        folded.append(total + pltpu.roll(total, rank, 1))

    @pl.when(pl.program_id(0) == 0)
    def _():
        out_ref[...] = jnp.zeros_like(out_ref)

    half = parts // 2
    for s in range(half):
        rows = pl.ds(s * requests, requests)
        out_ref[rows, :] += jnp.where(low, folded[s], folded[s + half])


def expand_kernel(parts, ids_ref, *refs):
    owner_refs, low_refs, factor_refs = refs[:parts], refs[parts : 2 * parts], refs[2 * parts : -parts - 1]
    out_refs, total_ref = refs[-parts - 1 : -1], refs[-1]
    rank, outputs = factor_refs[0].shape[1:]
    requests = out_refs[0].shape[0]
    step, last = pl.program_id(0), pl.num_programs(0) - 1
    ids = step_ids(ids_ref, factor_refs)
    weight = stacked(factor_refs)
    half = parts // 2
    low = lax.broadcasted_iota(jnp.int32, (requests, LANES), 1) < rank
    held = [[0.0] * half for _ in range(2)]
    for t in range(parts):
        sums = low_refs[t][...].astype(jnp.float32)
        for s in range(half):
            at = (s ^ t) % half
            piece = sums[at * requests : (at + 1) * requests]
            held[t // half][s] = held[t // half][s] + piece
    for s in range(half):
        straight = held[0][s] + pltpu.roll(held[1][s], rank, 1)
        turned = pltpu.roll(straight, rank, 1)
        for part in (s, s + half):
            first, other = (straight, turned) if part < half else (turned, straight)
            both = jnp.where(low, first, other)
            wide = jnp.concatenate([both] * (len(ids) * rank // LANES), axis=1)
            wide = jnp.where(owner_mask(owner_refs[part][...], ids, rank), wide, 0.0)
            product = jnp.dot(
                wide.astype(jnp.bfloat16), weight, preferred_element_type=jnp.float32
            )

            @pl.when(step == 0)
            def _():
                total_ref[part] = product

            @pl.when(step > 0)
            def _():
                total_ref[part] += product

            @pl.when(step == last)
            def _():
                out_refs[part][...] = total_ref[part].astype(jnp.bfloat16)


def attend_kernel(first, parts, me_ref, len_ref, base_ref, nk_ref, nv_ref, ck_ref, cv_ref, *refs):
    delta_refs, out_ref = refs[:parts], refs[-1]
    block = base_ref.shape[0]
    width = base_ref.shape[1] // parts
    slots = ck_ref.shape[1]
    per_part = width // HEAD
    sets = STEP // HALF
    span = parts * per_part * STEP
    set_span = span // sets
    keys_in = HALF * slots + STEP
    row = lax.broadcasted_iota(jnp.int32, (keys_in, span), 0)
    lane = lax.broadcasted_iota(jnp.int32, (keys_in, span), 1)
    lane_req = lane % HALF
    lane_set = lane // set_span
    own = row - HALF * slots
    cached = jnp.where(row // slots == lane_req, row % slots, slots)
    fresh = jnp.where(own == lane_req + lane_set * HALF, -1, slots)
    slot_of = jnp.where(own >= 0, fresh, cached)
    lane_set = lax.broadcasted_iota(jnp.int32, (1, span), 1) // set_span
    part_at = [(me_ref[0] ^ (first + s)) % parts for s in range(parts)]
    scale = 1.0 / math.sqrt(HEAD)
    step = pl.program_id(0)
    units = range(block // STEP)

    def rows_of(j):
        return pl.ds(j * STEP, STEP)

    def keys_of(cache_ref, fresh_ref, j, h):
        cache = cache_ref[pl.ds(j * STEP + h * HALF, HALF)].reshape(HALF * slots, HEAD)
        return jnp.concatenate([cache, fresh_ref[rows_of(j), :]], axis=0)

    scores = []
    for j in units:
        pieces = []
        for s in range(parts):
            q = base_ref[rows_of(j), columns(part_at[s], width)].astype(jnp.float32)
            q = q + delta_refs[s][rows_of(j), :].astype(jnp.float32)
            pieces += [q[:, k * HEAD : (k + 1) * HEAD] for k in range(per_part)]
        q = jnp.concatenate(
            [p[h * HALF : (h + 1) * HALF] for h in range(sets) for p in pieces], axis=0
        ).astype(jnp.bfloat16)
        score = None
        for h in range(sets):
            keys = keys_of(ck_ref, nk_ref, j, h)
            whole_score = lax.dot_general(keys, q, NT, preferred_element_type=jnp.float32)
            score = whole_score if h == 0 else jnp.where(lane_set == h, whole_score, score)
        scores.append(score)
    probs = []
    for j, score in zip(units, scores):
        lens = len_ref[pl.ds(step * (block // STEP) + j, 1), :]
        score = jnp.where(slot_of < lens, score, DEAD)
        top = jnp.max(score, axis=0, keepdims=True)
        exps = jnp.exp((score - top) * scale)
        total = jnp.sum(exps, axis=0, keepdims=True)
        probs.append((exps * (1.0 / total)).astype(jnp.bfloat16))
    for j, prob in zip(units, probs):
        mixed = []
        for h in range(sets):
            values = keys_of(cv_ref, nv_ref, j, h)
            got = lax.dot_general(prob, values, TN, preferred_element_type=jnp.float32)
            mixed.append(got[h * set_span : (h + 1) * set_span])
        for s in range(parts):
            out = []
            for k in range(per_part):
                at = (s * per_part + k) * HALF
                out.append(jnp.concatenate([m[at : at + HALF] for m in mixed], axis=0))
            out = jnp.concatenate(out, axis=1).astype(jnp.bfloat16)
            out_ref[rows_of(j), columns(part_at[s], width)] = out


def attend_half(first, me, base, new_key, new_value, cache_keys, cache_values, lengths, deltas, out):
    requests, columns = base.shape
    slots, kv = cache_keys.shape[1:]
    groups = kv // HEAD
    parts = len(deltas)
    block = STEP * BATCH
    group = lambda me: (me[0] ^ first) // parts
    wide = pl.BlockSpec((block, columns // groups), lambda i, me: (i, group(me)))
    fresh = pl.BlockSpec((block, HEAD), lambda i, me: (i, group(me)))
    cache = pl.BlockSpec((block, slots, HEAD), lambda i, me: (i, 0, group(me)))
    part = pl.BlockSpec((block, columns // groups // parts), lambda i, me: (i, 0))
    table = pl.BlockSpec(lengths.shape, lambda i, me: (0, 0))
    earlier = [] if out is None else [out]
    return pl.pallas_call(
        functools.partial(attend_kernel, first, parts),
        out_shape=jax.ShapeDtypeStruct((requests, columns), jnp.bfloat16),
        grid_spec=pltpu.PrefetchScalarGridSpec(
            num_scalar_prefetch=1,
            grid=(requests // block,),
            in_specs=[table, wide, fresh, fresh, cache, cache]
            + [part] * parts
            + [pl.BlockSpec(memory_space=pl.ANY)] * len(earlier),
            out_specs=wide,
        ),
        input_output_aliases={7 + parts: 0} if earlier else {},
        cost_estimate=pl.CostEstimate(
            flops=4 * requests * HALF * slots * columns // groups,
            bytes_accessed=4 * requests * (columns + slots * kv) // groups,
            transcendentals=requests * slots * columns // 16 // groups,
        ),
    )(me, lengths, base, new_key, new_value, cache_keys, cache_values, *deltas, *earlier)


def length_table(lengths, heads):
    lengths = lengths.reshape(-1, STEP // HALF, 1, HALF)
    lengths = jnp.broadcast_to(lengths, lengths.shape[:2] + (heads, HALF))
    return lengths.reshape(-1, heads * STEP)


def attend(me, base, new_key, new_value, cache_keys, cache_values, lengths, deltas):
    groups = new_key.shape[1] // HEAD
    parts = len(deltas) // groups
    out = None
    for first in range(0, len(deltas), parts):
        mine = deltas[first : first + parts]
        arrays = (base, new_key, new_value, cache_keys, cache_values)
        out = attend_half(first, me, *arrays, lengths, mine, out)
    return out


def whole(array):
    return pl.BlockSpec(array.shape, lambda *_: (0,) * len(array.shape))


def in_chunks(factors, most):
    chunk = [math.gcd(f.shape[0], most) for f in factors]
    return factors[0].shape[0] // chunk[0], [
        pl.BlockSpec((c,) + f.shape[1:], lambda i: (i, 0, 0)) for c, f in zip(chunk, factors)
    ]


def shrink_rows(ids, rows, factors):
    parts, requests = len(rows), rows[0].shape[0]
    steps, specs = in_chunks(factors, 4)
    out = jax.ShapeDtypeStruct((parts // 2 * requests, LANES), jnp.float32)
    return pl.pallas_call(
        functools.partial(shrink_kernel, parts),
        out_shape=out,
        grid=(steps,),
        in_specs=[SMEM, *map(whole, rows), *specs],
        out_specs=whole(out),
        compiler_params=PARAMS,
    )(ids, *rows, *factors)


def expand_rows(ids, rows, lows, factors):
    parts, requests, outputs = len(rows), rows[0].shape[0], factors[0].shape[2]
    steps, specs = in_chunks(factors, 8)
    last_lanes = rows[0].shape[1] // LANES - 1
    owners = pl.BlockSpec((requests, LANES), lambda i: (0, last_lanes))
    out = jax.ShapeDtypeStruct((requests, outputs), jnp.bfloat16)
    return pl.pallas_call(
        functools.partial(expand_kernel, parts),
        out_shape=[out] * parts,
        grid=(steps,),
        in_specs=[SMEM] + [owners] * parts + [*map(whole, lows), *specs],
        out_specs=[whole(out)] * parts,
        scratch_shapes=[pltpu.VMEM((parts, requests, outputs), jnp.float32)],
        compiler_params=PARAMS,
    )(ids, *rows, *lows, *factors)


def per_device(
    hidden,
    adapter_ids,
    owner_map,
    shrink_factors,
    expand_factors,
    query_base,
    new_key,
    new_value,
    cache_keys,
    cache_values,
    lengths,
):
    reps, levels, sides, tp = (lax.axis_size(a) for a in ("rep", "level", "side", "tp"))
    requests, wide = hidden.shape
    rank = shrink_factors.shape[2]
    square = reps * sides
    features, outputs = wide // square, query_base.shape[1] // square
    level, side = lax.axis_index("level"), lax.axis_index("side")
    me = lax.axis_index("rep") * sides + side

    def swap(a, s):
        pairs = [(c, c ^ s) for c in range(square)]
        return lax.ppermute(a, ("rep", "side"), pairs)

    shapes = [(levels, rank, features), (1, rank, outputs), (1, rank, features + outputs)]
    own, expand_own, other = pl.pallas_call(
        functools.partial(factor_kernel, square),
        out_shape=[jax.ShapeDtypeStruct(shape, jnp.bfloat16) for shape in shapes],
        in_specs=[SMEM, HBM, HBM],
        out_specs=[VMEM] * 3,
        scratch_shapes=[pltpu.SemaphoreType.DMA((levels + 3,))],
    )(me[None], shrink_factors.swapaxes(1, 2), expand_factors)

    def to_levels(a):
        return lax.all_to_all(a, "level", split_axis=0, concat_axis=0, tiled=True)

    own = to_levels(own)
    other = swap(other, 1)
    rows = pl.pallas_call(
        functools.partial(row_kernel, square),
        out_shape=[jax.ShapeDtypeStruct((requests, features + LANES), jnp.bfloat16)] * square,
        in_specs=[SMEM, SMEM, VMEM, HBM],
        out_specs=[VMEM] * square,
        scratch_shapes=[pltpu.SemaphoreType.DMA((square,))],
    )(me[None], owner_map, adapter_ids.T, hidden)
    table = length_table(lengths, outputs * square // new_key.shape[1])
    *rows, other, table = lax.optimization_barrier((*rows, other, table))
    rows = [rows[0]] + [swap(rows[s], s) for s in range(1, square)]
    other, expand_next = other[:, :, :features], other[:, :, features:]
    order = jnp.arange(levels, dtype=jnp.int32)
    if levels == 4:
        pairs = [[(i, i ^ k) for i in range(levels)] for k in range(levels)]
        other = [other] + [lax.ppermute(other, "level", pairs[k]) for k in range(1, levels)]
        other_at = level ^ order
    else:
        other = [to_levels(jnp.broadcast_to(other, own.shape))]
        other_at = order
    ids = [a.reshape(-1, 4) for a in (order * sides + side, other_at * sides + (side ^ 1))]
    ids = jnp.concatenate(ids, axis=1).reshape(-1)
    expand = jnp.concatenate([expand_own, expand_next], axis=1)
    expand = jnp.broadcast_to(expand, (levels,) + expand.shape[1:])
    expand, *rows = lax.optimization_barrier((expand, *rows))
    expand = to_levels(expand).reshape(levels * sides, rank, outputs)
    expand_ids = (order[:, None] * sides + jnp.stack([side, side ^ 1])[None, :]).reshape(-1)

    partial = shrink_rows(ids, rows, [own, *other])
    for c in range(1, tp):
        partial = partial + lax.ppermute(partial, "tp", [(t, t ^ c) for t in range(tp)])
    partial = partial.astype(jnp.bfloat16)
    lows = [partial] + [swap(partial, s) for s in range(1, square)]
    deltas = expand_rows(expand_ids, rows, lows, [expand])
    deltas = [deltas[0]] + [swap(deltas[s], s) for s in range(1, square)]
    return attend(
        me[None], query_base, new_key, new_value, cache_keys, cache_values, table, deltas
    )


def solution(mesh):
    reps, pool, tp = (mesh.shape[a] for a in ("rep", "pool", "tp"))
    finer = Mesh(mesh.devices.reshape(reps, pool // 2, 2, tp), ("rep", "level", "side", "tp"))
    pooled = ("level", "side")
    requests = ("rep", "level", "side")
    in_specs = (
        P(requests, "tp"),
        P(requests, None),
        P(),
        P(pooled, "tp", None),
        P(pooled, None, "tp"),
        P(requests, "tp"),
        P(requests, "tp"),
        P(requests, "tp"),
        P(requests, None, "tp"),
        P(requests, None, "tp"),
        P(requests),
    )
    return jax.shard_map(
        per_device, mesh=finer, in_specs=in_specs, out_specs=P(requests, "tp"), check_vma=False
    )
```

```python
import functools
import math

import jax
import jax.numpy as jnp
from jax import lax
from jax.experimental import pallas as pl
from jax.experimental.pallas import tpu as pltpu
from jax.sharding import Mesh
from jax.sharding import PartitionSpec as P

HEAD = 128
LANES = 128
STEP = 16
HALF = 8
BATCH = 4
DEAD = -1e30
VMEM = pl.BlockSpec(memory_space=pltpu.VMEM)
SMEM = pl.BlockSpec(memory_space=pltpu.SMEM)
HBM = pl.BlockSpec(memory_space=pltpu.HBM)
PARAMS = pltpu.CompilerParams(vmem_limit_bytes=12 * 1024 * 1024)
NT = (((1,), (1,)), ((), ()))
TN = (((0,), (0,)), ((), ()))


def columns(at, width):
    return pl.ds(pl.multiple_of(at * width, width), width)


def run_copies(moves, sems, meanwhile=None):
    copies = [pltpu.make_async_copy(src, dst, sems.at[k]) for k, (src, dst) in enumerate(moves)]
    for copy in copies:
        copy.start()
    if meanwhile is not None:
        meanwhile()
    for copy in copies:
        copy.wait()


def factor_kernel(parts, me_ref, shrink_ref, expand_ref, own_ref, expand_own_ref, other_ref, sems):
    features, outputs = shrink_ref.shape[2] // parts, expand_ref.shape[2] // parts
    me = me_ref[0]
    moves = [
        (shrink_ref.at[:, :, columns(me ^ 1, features)], other_ref.at[:, :, :features]),
        (expand_ref.at[:, :, columns(me ^ 1, outputs)], other_ref.at[:, :, features:]),
        (expand_ref.at[:, :, columns(me, outputs)], expand_own_ref),
    ]
    share = shrink_ref.at[0, :, columns(me, features)]
    moves += [(share, own_ref.at[k]) for k in range(own_ref.shape[0])]
    run_copies(moves, sems)


def row_kernel(parts, me_ref, map_ref, ids_ref, hidden_ref, *refs):
    out_refs, sems = refs[:parts], refs[parts]
    requests, wide = hidden_ref.shape
    features = wide // parts
    moves = [
        (hidden_ref.at[:, columns(me_ref[0] ^ s, features)], out_refs[s].at[:, :features])
        for s in range(parts)
    ]

    def owners():
        ids = ids_ref[...]

        def look(k, found):
            return jnp.where(ids == k, map_ref[k], found)

        found = lax.fori_loop(0, map_ref.shape[0], look, jnp.zeros_like(ids))
        found = jnp.broadcast_to(found.astype(jnp.float32), (LANES, requests)).T
        for s in range(parts):
            out_refs[s][:, features:] = found.astype(jnp.bfloat16)

    run_copies(moves, sems, owners)


def owner_mask(owners, ids, rank):
    lane = lax.broadcasted_iota(jnp.int32, (1, len(ids) * rank), 1) // rank
    named = jnp.full_like(lane, -1)
    for k, owner in enumerate(ids):
        named = jnp.where(lane == k, owner, named)
    owners = owners.astype(jnp.float32).astype(jnp.int32)
    return jnp.concatenate([owners] * (len(ids) * rank // LANES), axis=1) == named


def stacked(refs):
    return jnp.concatenate([r[k] for r in refs for k in range(r.shape[0])], axis=0)


def step_ids(ids_ref, refs):
    count = sum(r.shape[0] for r in refs)
    return [ids_ref[pl.program_id(0) * count + k] for k in range(count)]


def shrink_kernel(parts, ids_ref, *refs):
    row_refs, factor_refs, out_ref = refs[:parts], refs[parts:-1], refs[-1]
    rank = factor_refs[0].shape[1]
    requests, features = row_refs[0].shape[0], row_refs[0].shape[1] - LANES
    ids = step_ids(ids_ref, factor_refs)
    weight = stacked(factor_refs)
    low = lax.broadcasted_iota(jnp.int32, (requests, LANES), 1) < rank
    folded = []
    for ref in row_refs:
        sums = lax.dot_general(
            ref[:, :features], weight, NT, preferred_element_type=jnp.float32
        )
        sums = jnp.where(owner_mask(ref[:, features:], ids, rank), sums, 0.0)
        total = sums[:, :LANES]
        for k in range(1, len(ids) * rank // LANES):
            total = total + sums[:, k * LANES : (k + 1) * LANES]
        folded.append(total + pltpu.roll(total, rank, 1))

    @pl.when(pl.program_id(0) == 0)
    def _():
        out_ref[...] = jnp.zeros_like(out_ref)

    half = parts // 2
    for s in range(half):
        rows = pl.ds(s * requests, requests)
        out_ref[rows, :] += jnp.where(low, folded[s], folded[s + half])


def expand_kernel(parts, ids_ref, *refs):
    owner_refs, low_refs, factor_refs = refs[:parts], refs[parts : 2 * parts], refs[2 * parts : -parts - 1]
    out_refs, total_ref = refs[-parts - 1 : -1], refs[-1]
    rank, outputs = factor_refs[0].shape[1:]
    requests = out_refs[0].shape[0]
    step, last = pl.program_id(0), pl.num_programs(0) - 1
    ids = step_ids(ids_ref, factor_refs)
    weight = stacked(factor_refs)
    half = parts // 2
    low = lax.broadcasted_iota(jnp.int32, (requests, LANES), 1) < rank
    held = [[0.0] * half for _ in range(2)]
    for t in range(parts):
        sums = low_refs[t][...].astype(jnp.float32)
        for s in range(half):
            at = (s ^ t) % half
            piece = sums[at * requests : (at + 1) * requests]
            held[t // half][s] = held[t // half][s] + piece
    for s in range(half):
        straight = held[0][s] + pltpu.roll(held[1][s], rank, 1)
        turned = pltpu.roll(straight, rank, 1)
        for part in (s, s + half):
            first, other = (straight, turned) if part < half else (turned, straight)
            both = jnp.where(low, first, other)
            wide = jnp.concatenate([both] * (len(ids) * rank // LANES), axis=1)
            wide = jnp.where(owner_mask(owner_refs[part][...], ids, rank), wide, 0.0)
            product = jnp.dot(
                wide.astype(jnp.bfloat16), weight, preferred_element_type=jnp.float32
            )

            @pl.when(step == 0)
            def _():
                total_ref[part] = product

            @pl.when(step > 0)
            def _():
                total_ref[part] += product

            @pl.when(step == last)
            def _():
                out_refs[part][...] = total_ref[part].astype(jnp.bfloat16)


def attend_kernel(first, parts, me_ref, len_ref, base_ref, nk_ref, nv_ref, ck_ref, cv_ref, *refs):
    delta_refs, out_ref = refs[:parts], refs[-1]
    block = base_ref.shape[0]
    width = base_ref.shape[1] // parts
    slots = ck_ref.shape[1]
    per_part = width // HEAD
    sets = STEP // HALF
    span = parts * per_part * STEP
    set_span = span // sets
    keys_in = HALF * slots + STEP
    row = lax.broadcasted_iota(jnp.int32, (keys_in, span), 0)
    lane = lax.broadcasted_iota(jnp.int32, (keys_in, span), 1)
    lane_req = lane % HALF
    lane_set = lane // set_span
    own = row - HALF * slots
    cached = jnp.where(row // slots == lane_req, row % slots, slots)
    fresh = jnp.where(own == lane_req + lane_set * HALF, -1, slots)
    slot_of = jnp.where(own >= 0, fresh, cached)
    lane_set = lax.broadcasted_iota(jnp.int32, (1, span), 1) // set_span
    part_at = [(me_ref[0] ^ (first + s)) % parts for s in range(parts)]
    scale = 1.0 / math.sqrt(HEAD)
    step = pl.program_id(0)
    units = range(block // STEP)

    def rows_of(j):
        return pl.ds(j * STEP, STEP)

    def keys_of(cache_ref, fresh_ref, j, h):
        cache = cache_ref[pl.ds(j * STEP + h * HALF, HALF)].reshape(HALF * slots, HEAD)
        return jnp.concatenate([cache, fresh_ref[rows_of(j), :]], axis=0)

    scores = []
    for j in units:
        pieces = []
        for s in range(parts):
            q = base_ref[rows_of(j), columns(part_at[s], width)].astype(jnp.float32)
            q = q + delta_refs[s][rows_of(j), :].astype(jnp.float32)
            pieces += [q[:, k * HEAD : (k + 1) * HEAD] for k in range(per_part)]
        q = jnp.concatenate(
            [p[h * HALF : (h + 1) * HALF] for h in range(sets) for p in pieces], axis=0
        ).astype(jnp.bfloat16)
        score = None
        for h in range(sets):
            keys = keys_of(ck_ref, nk_ref, j, h)
            whole_score = lax.dot_general(keys, q, NT, preferred_element_type=jnp.float32)
            score = whole_score if h == 0 else jnp.where(lane_set == h, whole_score, score)
        scores.append(score)
    probs = []
    for j, score in zip(units, scores):
        lens = len_ref[pl.ds(step * (block // STEP) + j, 1), :]
        score = jnp.where(slot_of < lens, score, DEAD)
        top = jnp.max(score, axis=0, keepdims=True)
        exps = jnp.exp((score - top) * scale)
        total = jnp.sum(exps, axis=0, keepdims=True)
        probs.append((exps * (1.0 / total)).astype(jnp.bfloat16))
    for j, prob in zip(units, probs):
        mixed = []
        for h in range(sets):
            values = keys_of(cv_ref, nv_ref, j, h)
            got = lax.dot_general(prob, values, TN, preferred_element_type=jnp.float32)
            mixed.append(got[h * set_span : (h + 1) * set_span])
        for s in range(parts):
            out = []
            for k in range(per_part):
                at = (s * per_part + k) * HALF
                out.append(jnp.concatenate([m[at : at + HALF] for m in mixed], axis=0))
            out = jnp.concatenate(out, axis=1).astype(jnp.bfloat16)
            out_ref[rows_of(j), columns(part_at[s], width)] = out


def attend_half(first, me, base, new_key, new_value, cache_keys, cache_values, lengths, deltas, out):
    requests, columns = base.shape
    slots, kv = cache_keys.shape[1:]
    groups = kv // HEAD
    parts = len(deltas)
    block = STEP * BATCH
    group = lambda me: (me[0] ^ first) // parts
    wide = pl.BlockSpec((block, columns // groups), lambda i, me: (i, group(me)))
    fresh = pl.BlockSpec((block, HEAD), lambda i, me: (i, group(me)))
    cache = pl.BlockSpec((block, slots, HEAD), lambda i, me: (i, 0, group(me)))
    part = pl.BlockSpec((block, columns // groups // parts), lambda i, me: (i, 0))
    table = pl.BlockSpec(lengths.shape, lambda i, me: (0, 0))
    earlier = [] if out is None else [out]
    return pl.pallas_call(
        functools.partial(attend_kernel, first, parts),
        out_shape=jax.ShapeDtypeStruct((requests, columns), jnp.bfloat16),
        grid_spec=pltpu.PrefetchScalarGridSpec(
            num_scalar_prefetch=1,
            grid=(requests // block,),
            in_specs=[table, wide, fresh, fresh, cache, cache]
            + [part] * parts
            + [pl.BlockSpec(memory_space=pl.ANY)] * len(earlier),
            out_specs=wide,
        ),
        input_output_aliases={7 + parts: 0} if earlier else {},
        cost_estimate=pl.CostEstimate(
            flops=4 * requests * HALF * slots * columns // groups,
            bytes_accessed=4 * requests * (columns + slots * kv) // groups,
            transcendentals=requests * slots * columns // 16 // groups,
        ),
    )(me, lengths, base, new_key, new_value, cache_keys, cache_values, *deltas, *earlier)


def length_table(lengths, heads):
    lengths = lengths.reshape(-1, STEP // HALF, 1, HALF)
    lengths = jnp.broadcast_to(lengths, lengths.shape[:2] + (heads, HALF))
    return lengths.reshape(-1, heads * STEP)


def attend(me, base, new_key, new_value, cache_keys, cache_values, lengths, deltas):
    groups = new_key.shape[1] // HEAD
    parts = len(deltas) // groups
    out = None
    for first in range(0, len(deltas), parts):
        mine = deltas[first : first + parts]
        arrays = (base, new_key, new_value, cache_keys, cache_values)
        out = attend_half(first, me, *arrays, lengths, mine, out)
    return out


def whole(array):
    return pl.BlockSpec(array.shape, lambda *_: (0,) * len(array.shape))


def in_chunks(factors, most):
    chunk = [math.gcd(f.shape[0], most) for f in factors]
    return factors[0].shape[0] // chunk[0], [
        pl.BlockSpec((c,) + f.shape[1:], lambda i: (i, 0, 0)) for c, f in zip(chunk, factors)
    ]


def shrink_rows(ids, rows, factors):
    parts, requests = len(rows), rows[0].shape[0]
    steps, specs = in_chunks(factors, 4)
    out = jax.ShapeDtypeStruct((parts // 2 * requests, LANES), jnp.float32)
    return pl.pallas_call(
        functools.partial(shrink_kernel, parts),
        out_shape=out,
        grid=(steps,),
        in_specs=[SMEM, *map(whole, rows), *specs],
        out_specs=whole(out),
        compiler_params=PARAMS,
    )(ids, *rows, *factors)


def expand_rows(ids, rows, lows, factors):
    parts, requests, outputs = len(rows), rows[0].shape[0], factors[0].shape[2]
    steps, specs = in_chunks(factors, 8)
    last_lanes = rows[0].shape[1] // LANES - 1
    owners = pl.BlockSpec((requests, LANES), lambda i: (0, last_lanes))
    out = jax.ShapeDtypeStruct((requests, outputs), jnp.bfloat16)
    return pl.pallas_call(
        functools.partial(expand_kernel, parts),
        out_shape=[out] * parts,
        grid=(steps,),
        in_specs=[SMEM] + [owners] * parts + [*map(whole, lows), *specs],
        out_specs=[whole(out)] * parts,
        scratch_shapes=[pltpu.VMEM((parts, requests, outputs), jnp.float32)],
        compiler_params=PARAMS,
    )(ids, *rows, *lows, *factors)


def per_device(
    hidden,
    adapter_ids,
    owner_map,
    shrink_factors,
    expand_factors,
    query_base,
    new_key,
    new_value,
    cache_keys,
    cache_values,
    lengths,
):
    reps, levels, sides, tp = (lax.axis_size(a) for a in ("rep", "level", "side", "tp"))
    requests, wide = hidden.shape
    rank = shrink_factors.shape[2]
    square = reps * sides
    features, outputs = wide // square, query_base.shape[1] // square
    level, side = lax.axis_index("level"), lax.axis_index("side")
    me = lax.axis_index("rep") * sides + side

    def swap(a, s):
        pairs = [(c, c ^ s) for c in range(square)]
        return lax.ppermute(a, ("rep", "side"), pairs)

    shapes = [(levels, rank, features), (1, rank, outputs), (1, rank, features + outputs)]
    own, expand_own, other = pl.pallas_call(
        functools.partial(factor_kernel, square),
        out_shape=[jax.ShapeDtypeStruct(shape, jnp.bfloat16) for shape in shapes],
        in_specs=[SMEM, HBM, HBM],
        out_specs=[VMEM] * 3,
        scratch_shapes=[pltpu.SemaphoreType.DMA((levels + 3,))],
    )(me[None], shrink_factors.swapaxes(1, 2), expand_factors)

    def to_levels(a):
        return lax.all_to_all(a, "level", split_axis=0, concat_axis=0, tiled=True)

    own = to_levels(own)
    other = swap(other, 1)
    rows = pl.pallas_call(
        functools.partial(row_kernel, square),
        out_shape=[jax.ShapeDtypeStruct((requests, features + LANES), jnp.bfloat16)] * square,
        in_specs=[SMEM, SMEM, VMEM, HBM],
        out_specs=[VMEM] * square,
        scratch_shapes=[pltpu.SemaphoreType.DMA((square,))],
    )(me[None], owner_map, adapter_ids.T, hidden)
    table = length_table(lengths, outputs * square // new_key.shape[1])
    *rows, other, table = lax.optimization_barrier((*rows, other, table))
    rows = [rows[0]] + [swap(rows[s], s) for s in range(1, square)]
    other, expand_next = other[:, :, :features], other[:, :, features:]
    expand = jnp.concatenate([expand_own, expand_next], axis=1)
    expand = jnp.broadcast_to(expand, (levels,) + expand.shape[1:])
    other, expand = lax.optimization_barrier((other, expand))
    order = jnp.arange(levels, dtype=jnp.int32)
    if levels == 4:
        pairs = [[(i, i ^ k) for i in range(levels)] for k in range(levels)]
        other = [other] + [lax.ppermute(other, "level", pairs[k]) for k in range(1, levels)]
        other_at = level ^ order
    else:
        other = [to_levels(jnp.broadcast_to(other, own.shape))]
        other_at = order
    ids = [a.reshape(-1, 4) for a in (order * sides + side, other_at * sides + (side ^ 1))]
    ids = jnp.concatenate(ids, axis=1).reshape(-1)
    expand, *rows = lax.optimization_barrier((expand, *rows))
    expand = to_levels(expand).reshape(levels * sides, rank, outputs)
    expand_ids = (order[:, None] * sides + jnp.stack([side, side ^ 1])[None, :]).reshape(-1)

    partial = shrink_rows(ids, rows, [own, *other])
    for c in range(1, tp):
        partial = partial + lax.ppermute(partial, "tp", [(t, t ^ c) for t in range(tp)])
    partial = partial.astype(jnp.bfloat16)
    lows = [partial] + [swap(partial, s) for s in range(1, square)]
    deltas = expand_rows(expand_ids, rows, lows, [expand])
    deltas = [deltas[0]] + [swap(deltas[s], s) for s in range(1, square)]
    return attend(
        me[None], query_base, new_key, new_value, cache_keys, cache_values, table, deltas
    )


def solution(mesh):
    reps, pool, tp = (mesh.shape[a] for a in ("rep", "pool", "tp"))
    finer = Mesh(mesh.devices.reshape(reps, pool // 2, 2, tp), ("rep", "level", "side", "tp"))
    pooled = ("level", "side")
    requests = ("rep", "level", "side")
    in_specs = (
        P(requests, "tp"),
        P(requests, None),
        P(),
        P(pooled, "tp", None),
        P(pooled, None, "tp"),
        P(requests, "tp"),
        P(requests, "tp"),
        P(requests, "tp"),
        P(requests, None, "tp"),
        P(requests, None, "tp"),
        P(requests),
    )
    return jax.shard_map(
        per_device, mesh=finer, in_specs=in_specs, out_specs=P(requests, "tp"), check_vma=False
    )
```

```python
import functools
import math

import jax
import jax.numpy as jnp
from jax import lax
from jax.experimental import pallas as pl
from jax.experimental.pallas import tpu as pltpu
from jax.sharding import Mesh
from jax.sharding import PartitionSpec as P

HEAD = 128
LANES = 128
STEP = 16
HALF = 8
BATCH = 8
DEAD = -1e30
VMEM = pl.BlockSpec(memory_space=pltpu.VMEM)
SMEM = pl.BlockSpec(memory_space=pltpu.SMEM)
HBM = pl.BlockSpec(memory_space=pltpu.HBM)
PARAMS = pltpu.CompilerParams(vmem_limit_bytes=12 * 1024 * 1024)
NT = (((1,), (1,)), ((), ()))
TN = (((0,), (0,)), ((), ()))


def columns(at, width):
    return pl.ds(pl.multiple_of(at * width, width), width)


def run_copies(moves, sems, meanwhile=None):
    copies = [pltpu.make_async_copy(src, dst, sems.at[k]) for k, (src, dst) in enumerate(moves)]
    for copy in copies:
        copy.start()
    if meanwhile is not None:
        meanwhile()
    for copy in copies:
        copy.wait()


def factor_kernel(parts, me_ref, shrink_ref, expand_ref, own_ref, expand_own_ref, other_ref, sems):
    features, outputs = shrink_ref.shape[2] // parts, expand_ref.shape[2] // parts
    me = me_ref[0]
    moves = [
        (shrink_ref.at[:, :, columns(me ^ 1, features)], other_ref.at[:, :, :features]),
        (expand_ref.at[:, :, columns(me ^ 1, outputs)], other_ref.at[:, :, features:]),
        (expand_ref.at[:, :, columns(me, outputs)], expand_own_ref),
    ]
    share = shrink_ref.at[0, :, columns(me, features)]
    moves += [(share, own_ref.at[k]) for k in range(own_ref.shape[0])]
    run_copies(moves, sems)


def row_kernel(parts, me_ref, map_ref, ids_ref, hidden_ref, *refs):
    out_refs, sems = refs[:parts], refs[parts]
    requests, wide = hidden_ref.shape
    features = wide // parts
    moves = [
        (hidden_ref.at[:, columns(me_ref[0] ^ s, features)], out_refs[s].at[:, :features])
        for s in range(parts)
    ]

    def owners():
        ids = ids_ref[...]

        def look(k, found):
            return jnp.where(ids == k, map_ref[k], found)

        found = lax.fori_loop(0, map_ref.shape[0], look, jnp.zeros_like(ids))
        found = jnp.broadcast_to(found.astype(jnp.float32), (LANES, requests)).T
        for s in range(parts):
            out_refs[s][:, features:] = found.astype(jnp.bfloat16)

    run_copies(moves, sems, owners)


def owner_mask(owners, ids, rank):
    lane = lax.broadcasted_iota(jnp.int32, (1, len(ids) * rank), 1) // rank
    named = jnp.full_like(lane, -1)
    for k, owner in enumerate(ids):
        named = jnp.where(lane == k, owner, named)
    owners = owners.astype(jnp.float32).astype(jnp.int32)
    return jnp.concatenate([owners] * (len(ids) * rank // LANES), axis=1) == named


def stacked(refs):
    return jnp.concatenate([r[k] for r in refs for k in range(r.shape[0])], axis=0)


def step_ids(ids_ref, refs):
    count = sum(r.shape[0] for r in refs)
    return [ids_ref[pl.program_id(0) * count + k] for k in range(count)]


def shrink_kernel(parts, ids_ref, *refs):
    row_refs, factor_refs, out_ref = refs[:parts], refs[parts:-1], refs[-1]
    rank = factor_refs[0].shape[1]
    requests, features = row_refs[0].shape[0], row_refs[0].shape[1] - LANES
    ids = step_ids(ids_ref, factor_refs)
    weight = stacked(factor_refs)
    low = lax.broadcasted_iota(jnp.int32, (requests, LANES), 1) < rank
    folded = []
    for ref in row_refs:
        sums = lax.dot_general(
            ref[:, :features], weight, NT, preferred_element_type=jnp.float32
        )
        sums = jnp.where(owner_mask(ref[:, features:], ids, rank), sums, 0.0)
        total = sums[:, :LANES]
        for k in range(1, len(ids) * rank // LANES):
            total = total + sums[:, k * LANES : (k + 1) * LANES]
        folded.append(total + pltpu.roll(total, rank, 1))

    @pl.when(pl.program_id(0) == 0)
    def _():
        out_ref[...] = jnp.zeros_like(out_ref)

    half = parts // 2
    for s in range(half):
        rows = pl.ds(s * requests, requests)
        out_ref[rows, :] += jnp.where(low, folded[s], folded[s + half])


def expand_kernel(parts, ids_ref, *refs):
    owner_refs, low_refs, factor_refs = refs[:parts], refs[parts : 2 * parts], refs[2 * parts : -parts - 1]
    out_refs, total_ref = refs[-parts - 1 : -1], refs[-1]
    rank, outputs = factor_refs[0].shape[1:]
    requests = out_refs[0].shape[0]
    step, last = pl.program_id(0), pl.num_programs(0) - 1
    ids = step_ids(ids_ref, factor_refs)
    weight = stacked(factor_refs)
    half = parts // 2
    low = lax.broadcasted_iota(jnp.int32, (requests, LANES), 1) < rank
    held = [[0.0] * half for _ in range(2)]
    for t in range(parts):
        sums = low_refs[t][...].astype(jnp.float32)
        for s in range(half):
            at = (s ^ t) % half
            piece = sums[at * requests : (at + 1) * requests]
            held[t // half][s] = held[t // half][s] + piece
    for s in range(half):
        straight = held[0][s] + pltpu.roll(held[1][s], rank, 1)
        turned = pltpu.roll(straight, rank, 1)
        for part in (s, s + half):
            first, other = (straight, turned) if part < half else (turned, straight)
            both = jnp.where(low, first, other)
            wide = jnp.concatenate([both] * (len(ids) * rank // LANES), axis=1)
            wide = jnp.where(owner_mask(owner_refs[part][...], ids, rank), wide, 0.0)
            product = jnp.dot(
                wide.astype(jnp.bfloat16), weight, preferred_element_type=jnp.float32
            )

            @pl.when(step == 0)
            def _():
                total_ref[part] = product

            @pl.when(step > 0)
            def _():
                total_ref[part] += product

            @pl.when(step == last)
            def _():
                out_refs[part][...] = total_ref[part].astype(jnp.bfloat16)


def attend_kernel(first, parts, me_ref, len_ref, base_ref, nk_ref, nv_ref, ck_ref, cv_ref, *refs):
    delta_refs, out_ref = refs[:parts], refs[-1]
    block = base_ref.shape[0]
    width = base_ref.shape[1] // parts
    slots = ck_ref.shape[1]
    per_part = width // HEAD
    sets = STEP // HALF
    span = parts * per_part * STEP
    set_span = span // sets
    keys_in = HALF * slots + STEP
    row = lax.broadcasted_iota(jnp.int32, (keys_in, span), 0)
    lane = lax.broadcasted_iota(jnp.int32, (keys_in, span), 1)
    lane_req = lane % HALF
    lane_set = lane // set_span
    own = row - HALF * slots
    cached = jnp.where(row // slots == lane_req, row % slots, slots)
    fresh = jnp.where(own == lane_req + lane_set * HALF, -1, slots)
    slot_of = jnp.where(own >= 0, fresh, cached)
    lane_set = lax.broadcasted_iota(jnp.int32, (1, span), 1) // set_span
    part_at = [(me_ref[0] ^ (first + s)) % parts for s in range(parts)]
    scale = 1.0 / math.sqrt(HEAD)
    step = pl.program_id(0)
    units = range(block // STEP)

    def rows_of(j):
        return pl.ds(j * STEP, STEP)

    def keys_of(cache_ref, fresh_ref, j, h):
        cache = cache_ref[pl.ds(j * STEP + h * HALF, HALF)].reshape(HALF * slots, HEAD)
        return jnp.concatenate([cache, fresh_ref[rows_of(j), :]], axis=0)

    scores = []
    for j in units:
        pieces = []
        for s in range(parts):
            q = base_ref[rows_of(j), columns(part_at[s], width)].astype(jnp.float32)
            q = q + delta_refs[s][rows_of(j), :].astype(jnp.float32)
            pieces += [q[:, k * HEAD : (k + 1) * HEAD] for k in range(per_part)]
        q = jnp.concatenate(
            [p[h * HALF : (h + 1) * HALF] for h in range(sets) for p in pieces], axis=0
        ).astype(jnp.bfloat16)
        score = None
        for h in range(sets):
            keys = keys_of(ck_ref, nk_ref, j, h)
            whole_score = lax.dot_general(keys, q, NT, preferred_element_type=jnp.float32)
            score = whole_score if h == 0 else jnp.where(lane_set == h, whole_score, score)
        scores.append(score)
    probs = []
    for j, score in zip(units, scores):
        lens = len_ref[pl.ds(step * (block // STEP) + j, 1), :]
        score = jnp.where(slot_of < lens, score, DEAD)
        top = jnp.max(score, axis=0, keepdims=True)
        exps = jnp.exp((score - top) * scale)
        total = jnp.sum(exps, axis=0, keepdims=True)
        probs.append((exps * (1.0 / total)).astype(jnp.bfloat16))
    for j, prob in zip(units, probs):
        mixed = []
        for h in range(sets):
            values = keys_of(cv_ref, nv_ref, j, h)
            got = lax.dot_general(prob, values, TN, preferred_element_type=jnp.float32)
            mixed.append(got[h * set_span : (h + 1) * set_span])
        for s in range(parts):
            out = []
            for k in range(per_part):
                at = (s * per_part + k) * HALF
                out.append(jnp.concatenate([m[at : at + HALF] for m in mixed], axis=0))
            out = jnp.concatenate(out, axis=1).astype(jnp.bfloat16)
            out_ref[rows_of(j), columns(part_at[s], width)] = out


def attend_half(first, me, base, new_key, new_value, cache_keys, cache_values, lengths, deltas, out):
    requests, columns = base.shape
    slots, kv = cache_keys.shape[1:]
    groups = kv // HEAD
    parts = len(deltas)
    block = STEP * BATCH
    group = lambda me: (me[0] ^ first) // parts
    wide = pl.BlockSpec((block, columns // groups), lambda i, me: (i, group(me)))
    fresh = pl.BlockSpec((block, HEAD), lambda i, me: (i, group(me)))
    cache = pl.BlockSpec((block, slots, HEAD), lambda i, me: (i, 0, group(me)))
    part = pl.BlockSpec((block, columns // groups // parts), lambda i, me: (i, 0))
    table = pl.BlockSpec(lengths.shape, lambda i, me: (0, 0))
    earlier = [] if out is None else [out]
    return pl.pallas_call(
        functools.partial(attend_kernel, first, parts),
        out_shape=jax.ShapeDtypeStruct((requests, columns), jnp.bfloat16),
        grid_spec=pltpu.PrefetchScalarGridSpec(
            num_scalar_prefetch=1,
            grid=(requests // block,),
            in_specs=[table, wide, fresh, fresh, cache, cache]
            + [part] * parts
            + [pl.BlockSpec(memory_space=pl.ANY)] * len(earlier),
            out_specs=wide,
        ),
        input_output_aliases={7 + parts: 0} if earlier else {},
        cost_estimate=pl.CostEstimate(
            flops=4 * requests * HALF * slots * columns // groups,
            bytes_accessed=4 * requests * (columns + slots * kv) // groups,
            transcendentals=requests * slots * columns // 16 // groups,
        ),
    )(me, lengths, base, new_key, new_value, cache_keys, cache_values, *deltas, *earlier)


def length_table(lengths, heads):
    lengths = lengths.reshape(-1, STEP // HALF, 1, HALF)
    lengths = jnp.broadcast_to(lengths, lengths.shape[:2] + (heads, HALF))
    return lengths.reshape(-1, heads * STEP)


def attend(me, base, new_key, new_value, cache_keys, cache_values, lengths, deltas):
    groups = new_key.shape[1] // HEAD
    parts = len(deltas) // groups
    out = None
    for first in range(0, len(deltas), parts):
        mine = deltas[first : first + parts]
        arrays = (base, new_key, new_value, cache_keys, cache_values)
        out = attend_half(first, me, *arrays, lengths, mine, out)
    return out


def whole(array):
    return pl.BlockSpec(array.shape, lambda *_: (0,) * len(array.shape))


def in_chunks(factors, most):
    chunk = [math.gcd(f.shape[0], most) for f in factors]
    return factors[0].shape[0] // chunk[0], [
        pl.BlockSpec((c,) + f.shape[1:], lambda i: (i, 0, 0)) for c, f in zip(chunk, factors)
    ]


def shrink_rows(ids, rows, factors):
    parts, requests = len(rows), rows[0].shape[0]
    steps, specs = in_chunks(factors, 4)
    out = jax.ShapeDtypeStruct((parts // 2 * requests, LANES), jnp.float32)
    return pl.pallas_call(
        functools.partial(shrink_kernel, parts),
        out_shape=out,
        grid=(steps,),
        in_specs=[SMEM, *map(whole, rows), *specs],
        out_specs=whole(out),
        compiler_params=PARAMS,
    )(ids, *rows, *factors)


def expand_rows(ids, rows, lows, factors):
    parts, requests, outputs = len(rows), rows[0].shape[0], factors[0].shape[2]
    steps, specs = in_chunks(factors, 8)
    last_lanes = rows[0].shape[1] // LANES - 1
    owners = pl.BlockSpec((requests, LANES), lambda i: (0, last_lanes))
    out = jax.ShapeDtypeStruct((requests, outputs), jnp.bfloat16)
    return pl.pallas_call(
        functools.partial(expand_kernel, parts),
        out_shape=[out] * parts,
        grid=(steps,),
        in_specs=[SMEM] + [owners] * parts + [*map(whole, lows), *specs],
        out_specs=[whole(out)] * parts,
        scratch_shapes=[pltpu.VMEM((parts, requests, outputs), jnp.float32)],
        compiler_params=PARAMS,
    )(ids, *rows, *lows, *factors)


def per_device(
    hidden,
    adapter_ids,
    owner_map,
    shrink_factors,
    expand_factors,
    query_base,
    new_key,
    new_value,
    cache_keys,
    cache_values,
    lengths,
):
    reps, levels, sides, tp = (lax.axis_size(a) for a in ("rep", "level", "side", "tp"))
    requests, wide = hidden.shape
    rank = shrink_factors.shape[2]
    square = reps * sides
    features, outputs = wide // square, query_base.shape[1] // square
    level, side = lax.axis_index("level"), lax.axis_index("side")
    me = lax.axis_index("rep") * sides + side

    def swap(a, s):
        pairs = [(c, c ^ s) for c in range(square)]
        return lax.ppermute(a, ("rep", "side"), pairs)

    shapes = [(levels, rank, features), (1, rank, outputs), (1, rank, features + outputs)]
    own, expand_own, other = pl.pallas_call(
        functools.partial(factor_kernel, square),
        out_shape=[jax.ShapeDtypeStruct(shape, jnp.bfloat16) for shape in shapes],
        in_specs=[SMEM, HBM, HBM],
        out_specs=[VMEM] * 3,
        scratch_shapes=[pltpu.SemaphoreType.DMA((levels + 3,))],
    )(me[None], shrink_factors.swapaxes(1, 2), expand_factors)

    def to_levels(a):
        return lax.all_to_all(a, "level", split_axis=0, concat_axis=0, tiled=True)

    own = to_levels(own)
    other = swap(other, 1)
    rows = pl.pallas_call(
        functools.partial(row_kernel, square),
        out_shape=[jax.ShapeDtypeStruct((requests, features + LANES), jnp.bfloat16)] * square,
        in_specs=[SMEM, SMEM, VMEM, HBM],
        out_specs=[VMEM] * square,
        scratch_shapes=[pltpu.SemaphoreType.DMA((square,))],
    )(me[None], owner_map, adapter_ids.T, hidden)
    table = length_table(lengths, outputs * square // new_key.shape[1])
    *rows, other, table = lax.optimization_barrier((*rows, other, table))
    rows = [rows[0]] + [swap(rows[s], s) for s in range(1, square)]
    other, expand_next = other[:, :, :features], other[:, :, features:]
    expand = jnp.concatenate([expand_own, expand_next], axis=1)
    expand = jnp.broadcast_to(expand, (levels,) + expand.shape[1:])
    other, expand = lax.optimization_barrier((other, expand))
    order = jnp.arange(levels, dtype=jnp.int32)
    if levels == 4:
        pairs = [[(i, i ^ k) for i in range(levels)] for k in range(levels)]
        other = [other] + [lax.ppermute(other, "level", pairs[k]) for k in range(1, levels)]
        other_at = level ^ order
    else:
        other = [to_levels(jnp.broadcast_to(other, own.shape))]
        other_at = order
    ids = [a.reshape(-1, 4) for a in (order * sides + side, other_at * sides + (side ^ 1))]
    ids = jnp.concatenate(ids, axis=1).reshape(-1)
    expand, *rows = lax.optimization_barrier((expand, *rows))
    expand = to_levels(expand).reshape(levels * sides, rank, outputs)
    expand_ids = (order[:, None] * sides + jnp.stack([side, side ^ 1])[None, :]).reshape(-1)

    partial = shrink_rows(ids, rows, [own, *other])
    for c in range(1, tp):
        partial = partial + lax.ppermute(partial, "tp", [(t, t ^ c) for t in range(tp)])
    partial = partial.astype(jnp.bfloat16)
    lows = [partial] + [swap(partial, s) for s in range(1, square)]
    deltas = expand_rows(expand_ids, rows, lows, [expand])
    deltas = [deltas[0]] + [swap(deltas[s], s) for s in range(1, square)]
    return attend(
        me[None], query_base, new_key, new_value, cache_keys, cache_values, table, deltas
    )


def solution(mesh):
    reps, pool, tp = (mesh.shape[a] for a in ("rep", "pool", "tp"))
    finer = Mesh(mesh.devices.reshape(reps, pool // 2, 2, tp), ("rep", "level", "side", "tp"))
    pooled = ("level", "side")
    requests = ("rep", "level", "side")
    in_specs = (
        P(requests, "tp"),
        P(requests, None),
        P(),
        P(pooled, "tp", None),
        P(pooled, None, "tp"),
        P(requests, "tp"),
        P(requests, "tp"),
        P(requests, "tp"),
        P(requests, None, "tp"),
        P(requests, None, "tp"),
        P(requests),
    )
    return jax.shard_map(
        per_device, mesh=finer, in_specs=in_specs, out_specs=P(requests, "tp"), check_vma=False
    )
```
